32 devices in a mesh: cfg: 2 (over core), vox: 8 (over z, x), head: 2 (over y).
Axes of the slice: x: 2, y: 2, z: 4, core: 2. Of those that a mesh axis runs over, the one named last changes fastest.
Arguments:
- x_latent: bfloat16 [6144, 1024], P(('cfg', 'vox')), may hold values from -6 to 6
- windows: int32 [6144], P(('cfg', 'vox')), may hold values from 0 to 15, as said below
- coords: int32 [3, 6144], P(None, ('cfg', 'vox')), may hold values from 0 to 63
- modulation: float32 [3, 3, 1024], replicated, may hold values from -3 to 3
- w_qkv: bfloat16 [1024, 3, 1024], P(None, None, 'head'), may hold values from -0.1875 to 0.1875
- w_out: bfloat16 [1024, 1024], P('head'), may hold values from -0.1875 to 0.1875
- qk_gain: float32 [2, 1024], P(None, 'head'), may hold values from 0.5 to 8
- guidance: float32 [2], replicated, may hold values from 1.5 to 7.5
Outputs:
- guided: bfloat16 [6144, 1024], P(('cfg', 'vox'), 'head')
The draws below stay inside these ranges and needn't reach their ends.
Inputs may be any that keep to these rules, and one draw needn't show every extreme that they name: `windows`: the voxels of one device (aligned blocks of 384) name each window at most 32 times; in every draw one window is named exactly 32 times by every block, so it fills all 512 slots.
All inputs are finite; a program needn't handle non-finite values.
Results may differ from the reference program's by a relative error of at most 0.0045.
The reference program's roundings to bfloat16 on the way (of `normed`, `query_rows`, `key_rows`, `value_rows`, `attend` and `attended`) count: a program that leaves them out, or rounds other values in their place, can miss the bound.
Values may be sent and summed in bfloat16 or wider, within the bound.
No kernel may reach another device: no remote copies, remote signals or barrier semaphores. Data moves between devices by JAX's collectives and lax.ppermute only.
A program may use at most 384 MiB of HBM per device.

```python
import math
import jax
import jax.numpy as jnp
from jax import lax

D = 1024
HEADS = 16
BRANCHES = 3
SLOTS = 512
VOX_DEV = 384
VOXELS = 6144
WINDOWS = 16
CAP = 32


def draw_windows(key, part):
    key = jax.random.fold_in(key, 11)
    key_full, key_noise, key_order = jax.random.split(key, 3)
    full_window = jax.random.randint(key_full, (), 0, WINDOWS)
    slot_count = WINDOWS * CAP
    slot_window = jnp.arange(slot_count, dtype=jnp.int32) // CAP
    source = jnp.arange(WINDOWS, dtype=jnp.int32)[:, None]
    distance = jnp.abs(slot_window[None, :] - source)
    distance = jnp.minimum(distance, WINDOWS - distance)
    noise = jax.random.randint(key_noise, (WINDOWS, slot_count), 0, 4096)
    score = jnp.where(slot_window[None, :] == full_window, -1, noise + 256 * distance)
    score = score * slot_count + jnp.arange(slot_count, dtype=jnp.int32)[None, :]
    chosen = jnp.argsort(score, axis=1)[:, :VOX_DEV] // CAP
    shuffle = jax.random.randint(key_order, (WINDOWS, VOX_DEV), 0, 4096) * VOX_DEV + jnp.arange(VOX_DEV, dtype=jnp.int32)[None, :]
    order = jnp.argsort(shuffle, axis=1)
    return jnp.take_along_axis(chosen, order, axis=1).reshape(WINDOWS * VOX_DEV).astype(jnp.int32)


def draw_qk_gain(key, part):
    key = jax.random.fold_in(key, 23)
    return jax.random.uniform(key, (2, D), jnp.float32, 0.5, 1.5)


def touch_ends(entries, key, low, top_value):
    dims = entries.shape
    spot = [jax.random.randint(jax.random.fold_in(key, axis), (), 0, dims[axis]) for axis in range(len(dims))]
    entries = entries.at[tuple(spot)].set(low)
    longest = dims.index(max(dims))
    spot[longest] = (spot[longest] + 1) % dims[longest]
    return entries.at[tuple(spot)].set(top_value)


def level_of(stream_key, extent, pieces, smallest, top_value):
    level, own = 1.0, jax.random.fold_in(stream_key, 6)
    for position, parts in pieces:
        heights = jnp.exp(jax.random.uniform(jax.random.fold_in(own, position), (parts,), jnp.float32, smallest / len(pieces), top_value / len(pieces)))
        level = level * jnp.repeat(heights, extent[position] // parts).reshape([-1 if axis == position else 1 for axis in range(len(extent))])
    return level


def normal_values(own_key, shape, width, most, cuts=(), held_as=jnp.bfloat16):
    entries = jax.random.normal(own_key, shape, jnp.float32) * width
    if len(cuts) > 0:
        entries = level_of(own_key, shape, cuts, -0.22, 0.18) * entries
    return jnp.clip(entries, min=-most, max=most).astype(held_as)


def setup_inputs(seed: int = 0) -> dict:
    streams_of = jax.random.split(jax.random.key(seed), 9)
    x_latent = normal_values(streams_of[0], (VOXELS, D), 1.0, 6.0, ((0, 16),))
    windows = draw_windows(jax.random.fold_in(streams_of[8], 71), 0)
    coords = touch_ends(jax.random.randint(streams_of[2], (3, VOXELS), 0, 64), jax.random.fold_in(streams_of[2], 1), 0, 63).astype(jnp.int32)
    modulation = normal_values(streams_of[3], (BRANCHES, 3, D), 0.5, 3.0, (), jnp.float32)
    w_qkv = normal_values(streams_of[4], (D, 3, D), D ** -0.5, 0.1875, ((2, 2),))
    w_out = normal_values(streams_of[5], (D, D), D ** -0.5, 0.1875, ((0, 2),))
    qk_gain = draw_qk_gain(jax.random.fold_in(streams_of[8], 71), 0)
    guidance = jnp.clip(jax.random.uniform(streams_of[7], (2,), jnp.float32, 1.5, 7.5), 1.5, 7.5)
    return dict(x_latent=x_latent, windows=windows, coords=coords, modulation=modulation, w_qkv=w_qkv, w_out=w_out, qk_gain=qk_gain, guidance=guidance)


def position_table(coords, model_width):
    freq_count = model_width // 3 // 2
    frequency = 1.0 / 10000.0 ** (jnp.arange(freq_count, dtype=jnp.float32) / freq_count)
    angles = coords.astype(jnp.float32)[:, :, None] * frequency[None, None, :]
    embedding = jnp.concatenate([jnp.sin(angles), jnp.cos(angles)], axis=2)
    embedding = jnp.transpose(embedding, (1, 0, 2)).reshape(coords.shape[1], 6 * freq_count)
    padding = jnp.zeros((coords.shape[1], model_width - 6 * freq_count), jnp.float32)
    return jnp.concatenate([embedding, padding], axis=1)

def modulate(hidden, modulation):
    centred = hidden - lax.optimization_barrier(jnp.mean(hidden, axis=1, keepdims=True))
    spread = lax.optimization_barrier(jnp.mean(centred * centred, axis=1, keepdims=True))
    normal = centred * lax.rsqrt(spread + 1e-06)
    return (normal[None] * (1.0 + modulation[:, 1, None, :]) + modulation[:, 0, None, :]).astype(jnp.bfloat16)

def head_norm(projected, gain_row, head_size):
    shaped = projected.reshape(projected.shape[:-1] + (projected.shape[-1] // head_size, head_size))
    scale_rms = lax.rsqrt(lax.optimization_barrier(jnp.mean(shaped * shaped, axis=-1, keepdims=True)) + 1e-06)
    return (shaped * scale_rms).reshape(projected.shape) * gain_row

def reference(x_latent, windows, coords, modulation, w_qkv, w_out, qk_gain, guidance):
    hidden = x_latent.astype(jnp.float32) + position_table(coords, D)
    normed = modulate(hidden, modulation)
    head_size = D // HEADS
    voxels = hidden.shape[0]
    onehot = (windows[:, None] == jnp.arange(WINDOWS, dtype=jnp.int32)[None, :]).astype(jnp.int32)
    blocks = onehot.reshape(WINDOWS, VOX_DEV, WINDOWS)
    before = jnp.cumsum(blocks, axis=1) - blocks
    rank_in = lax.optimization_barrier(jnp.sum(before * blocks, axis=2)).reshape(voxels)
    source = jnp.arange(voxels, dtype=jnp.int32) // VOX_DEV
    slot_index = (windows * SLOTS + source * CAP + rank_in).astype(jnp.int32)
    live_slot = jnp.zeros((WINDOWS * SLOTS,), jnp.float32).at[slot_index].set(1.0)
    flat_qkv = w_qkv.reshape(D, 3 * D)
    scale_factor = 1.0 / math.sqrt(head_size)
    coefficients = [1.0 - guidance[0], guidance[0] - guidance[1], guidance[1]]

    def place(rows):
        buffer = jnp.zeros((WINDOWS * SLOTS, D), jnp.bfloat16).at[slot_index].set(rows)
        return buffer.reshape(WINDOWS, SLOTS, HEADS, head_size)

    def window_attention(operands):
        query_win, key_win, value_win, live_win = operands
        scores = jnp.einsum('qhd,khd->hqk', query_win.astype(jnp.float32), key_win.astype(jnp.float32)) * scale_factor
        scores = jnp.where(live_win[None, None, :] > 0.5, scores, -1e+30)
        highest = lax.optimization_barrier(jnp.max(scores, axis=2, keepdims=True))
        weights = jnp.exp(scores - highest)
        attend = (weights / lax.optimization_barrier(jnp.sum(weights, axis=2, keepdims=True))).astype(jnp.bfloat16)
        mixed = jnp.einsum('hqk,khd->qhd', attend.astype(jnp.float32), value_win.astype(jnp.float32))
        return mixed.astype(jnp.bfloat16).reshape(SLOTS, D)
    guided = jnp.zeros((voxels, D), jnp.float32)
    for branch in range(BRANCHES):
        projected = jnp.dot(normed[branch], flat_qkv, preferred_element_type=jnp.float32)
        query_rows = head_norm(projected[:, :D], qk_gain[0], head_size).astype(jnp.bfloat16)
        key_rows = head_norm(projected[:, D:2 * D], qk_gain[1], head_size).astype(jnp.bfloat16)
        value_rows = projected[:, 2 * D:].astype(jnp.bfloat16)
        attended = lax.map(window_attention, (place(query_rows), place(key_rows), place(value_rows), live_slot.reshape(WINDOWS, SLOTS)))
        returned = attended.reshape(WINDOWS * SLOTS, D)[slot_index]
        branch_out = jnp.dot(returned, w_out, preferred_element_type=jnp.float32)
        guided = guided + coefficients[branch] * (hidden + modulation[branch, 2][None, :] * branch_out)
    return guided.astype(jnp.bfloat16)
```

```python
import functools

import jax
import jax.numpy as jnp
from jax import lax
from jax.experimental import pallas as pl
from jax.experimental.pallas import tpu as pltpu
from jax.sharding import PartitionSpec as P

HEADS = 16
SLOTS = 512
GRID = 64
EXTRA = 128
BF16 = jnp.bfloat16
F32 = jnp.float32
VMEM = pl.BlockSpec(memory_space=pltpu.VMEM)
SMEM = pl.BlockSpec(memory_space=pltpu.SMEM)
NT = (((1,), (1,)), ((), ()))
TN = (((0,), (0,)), ((), ()))


def params(megabytes):
    return pltpu.CompilerParams(vmem_limit_bytes=megabytes * 1024 * 1024)


def iota(shape, dim):
    return lax.broadcasted_iota(jnp.int32, shape, dim)


def dot(a, b):
    return jnp.dot(a, b, preferred_element_type=F32)


def position_parts(model_width):
    freq_count = model_width // 3 // 2
    frequency = 1.0 / 10000.0 ** (jnp.arange(freq_count, dtype=F32) / freq_count)
    angles = jnp.arange(GRID, dtype=F32)[:, None] * frequency[None, :]
    block = jnp.concatenate([jnp.sin(angles), jnp.cos(angles)], axis=1)
    width = 2 * freq_count
    rows = [
        jnp.pad(block, ((0, 0), (c * width, model_width - (c + 1) * width))) for c in range(3)
    ]
    table = jnp.concatenate(rows, axis=0)
    top = lax.reduce_precision(table, 8, 7)
    rest = table - top
    middle = lax.reduce_precision(rest, 8, 7)
    low = rest - middle
    return jnp.concatenate([top, middle, low], axis=0).astype(BF16)


def place_kernel(senders, capacity, windows_ref, coords_ref, x_ref, out_ref, placing_ref):
    windows = windows_ref[...]
    voxels = windows.shape[1]
    width = x_ref.shape[1]
    member = windows == iota((senders, voxels), 0)
    earlier = (iota((voxels, voxels), 0) < iota((voxels, voxels), 1)).astype(F32).astype(BF16)
    member_f = member.astype(F32)
    before = dot(member_f.astype(BF16), earlier)
    rank = jnp.sum(before * member_f, axis=0, keepdims=True).astype(jnp.int32)
    placed = windows * capacity + rank
    placing = (placed == iota((SLOTS, voxels), 0)).astype(F32).astype(BF16)
    placing_ref[...] = placing
    row = iota((EXTRA, voxels), 0)
    extra = jnp.where(row == 3, 1.0, 0.0).astype(F32)
    for c in range(3):
        extra = jnp.where(row == c, coords_ref[c : c + 1, :].astype(F32), extra)
    out_ref[:, :width] = dot(placing, x_ref[...]).astype(BF16)
    out_ref[:, width:] = lax.dot_general(
        placing, extra.astype(BF16), NT, preferred_element_type=F32
    ).astype(BF16)


def attend_branch(normed, normed_q, weight, gain_ref, bias, head_size, att_ref):
    slots, queries = bias.shape[1], att_ref.shape[0]
    group = att_ref.shape[1]
    tile = min(256, group)
    square = (iota((tile, tile), 0) // head_size) == (iota((tile, tile), 1) // head_size)
    same_head = square.astype(F32).astype(BF16)

    def head_norm(rows, gain):
        squares = rows * rows
        top = squares.astype(BF16)
        low = (squares - top.astype(F32)).astype(BF16)
        mean = (dot(top, same_head) + dot(low, same_head)) * (1.0 / head_size)
        return rows * lax.rsqrt(mean + 1e-06) * gain

    lane_head = iota((queries, tile), 1) // head_size
    for start in range(0, group, tile):
        columns = slice(start, start + tile)
        query = head_norm(weight(0, columns, True), gain_ref[0:1, columns])
        key = head_norm(weight(1, columns, False), gain_ref[1:2, columns]).astype(BF16)
        value = weight(2, columns, False).astype(BF16)
        query = query.astype(BF16).astype(F32) * (1.0 / head_size**0.5)
        count = tile // head_size

        def score(head):
            one = jnp.where(lane_head == head, query, 0.0).astype(BF16)
            return lax.dot_general(one, key, NT, preferred_element_type=F32)

        scores = score(0)
        mixed = jnp.zeros((queries, tile), F32)
        for head in range(count):
            following = score(head + 1) if head + 1 < count else None
            step = min(32, queries)
            pieces = []
            for r in range(0, queries, step):
                piece = scores[r : r + step] + bias
                weights = jnp.exp(piece - jnp.max(piece, axis=1, keepdims=True))
                total = jnp.sum(weights, axis=1, keepdims=True)
                pieces.append((weights * (1.0 / total)).astype(BF16))
            attend = jnp.concatenate(pieces, axis=0)
            mixed = jnp.where(lane_head == head, dot(attend, value), mixed)
            scores = following
        att_ref[:, columns] = mixed.astype(BF16)


def own_kernel(
    senders,
    head_size,
    guidance_ref,
    rows_ref,
    table_ref,
    modulation_ref,
    w_ref,
    gain_ref,
    w_out_ref,
    normed_ref,
    normed_q_ref,
    acc_ref,
    bias_ref,
    hidden_ref,
    att_ref,
):
    branches, slots, width = normed_ref.shape
    queries = normed_q_ref.shape[1]
    group = att_ref.shape[1]
    capacity = slots // senders
    share = queries // senders
    first = lax.axis_index("head") * share
    g0, g1 = guidance_ref[0], guidance_ref[1]
    coefficients = (1.0 - g0, g0 - g1, g1)
    total = (coefficients[0] + coefficients[1]) + coefficients[2]

    extra = rows_ref[:, width:]
    pick = ((iota((8, EXTRA), 1) == 3)).astype(F32).astype(BF16)
    live = lax.dot_general(pick, extra, NT, preferred_element_type=F32)
    bias_ref[...] = jnp.where(live > 0.5, 0.0, -1e30)

    spots = extra.astype(F32)
    lane = iota((slots, 3 * GRID), 1)
    wanted = jnp.where(
        lane < GRID,
        spots[:, 0:1],
        jnp.where(lane < 2 * GRID, spots[:, 1:2], spots[:, 2:3]),
    )
    chosen = (wanted == (lane % GRID).astype(F32)).astype(F32).astype(BF16)
    chosen = jnp.concatenate([chosen, chosen, chosen], axis=1)
    hidden_ref[...] = dot(chosen, table_ref[...]) + rows_ref[:, :width].astype(F32)

    chunk = 32

    def normalise(i, carry):
        rows = pl.ds(pl.multiple_of(i * chunk, chunk), chunk)
        hidden = hidden_ref[rows, :]
        centred = hidden - jnp.mean(hidden, axis=1, keepdims=True)
        spread = jnp.mean(centred * centred, axis=1, keepdims=True)
        normal = centred * lax.rsqrt(spread + 1e-06)
        for b in range(branches):
            normed_ref[b, rows, :] = (
                normal * (1.0 + modulation_ref[b, 1:2, :]) + modulation_ref[b, 0:1, :]
            ).astype(BF16)
        return carry

    lax.fori_loop(0, slots // chunk, normalise, 0)

    if share % 16 == 0:
        for s in range(senders):
            source = pl.ds(pl.multiple_of(s * capacity + first, 16), share)
            target = slice(s * share, (s + 1) * share)
            acc_ref[target, :] = hidden_ref[source, :] * total
            for b in range(branches):
                normed_q_ref[b, target, :] = normed_ref[b, source, :]
    else:
        row = iota((queries, slots), 0)
        wanted_slot = (row // share) * capacity + first + row % share
        chooser = (wanted_slot == iota((queries, slots), 1)).astype(F32)
        picked = jnp.dot(
            chooser, hidden_ref[...], preferred_element_type=F32, precision=lax.Precision.HIGHEST
        )
        acc_ref[...] = picked * total
        for b in range(branches):
            normed_q_ref[b] = dot(chooser.astype(BF16), normed_ref[b]).astype(BF16)

    bias = bias_ref[0:1, :]
    g_coefficients = coefficients

    def branch(b, carry):
        def weight(part, columns, is_query):
            source = normed_q_ref[b] if is_query else normed_ref[b]
            place = slice(part * group + columns.start, part * group + columns.stop)
            return dot(source, w_ref[:, place])

        attend_branch(None, None, weight, gain_ref, bias, head_size, att_ref)
        scale = jnp.where(
            b == 0, g_coefficients[0], jnp.where(b == 1, g_coefficients[1], g_coefficients[2])
        )
        acc_ref[...] += dot(att_ref[...], w_out_ref[...]) * (scale * modulation_ref[b, 2:3, :])
        return carry

    lax.fori_loop(0, branches, branch, 0)


def other_kernel(
    head_size,
    out_parts,
    guidance_ref,
    normed_ref,
    normed_q_ref,
    acc_ref,
    bias_ref,
    modulation_ref,
    mine_ref,
    theirs_ref,
    gain_ref,
    out_mine_ref,
    out_theirs_ref,
    out_ref,
    att_ref,
    sum_ref,
):
    branches, slots, width = normed_ref.shape
    group = att_ref.shape[1]
    half = mine_ref.shape[0]
    wide = out_mine_ref.shape[1]
    cfg = lax.axis_index("cfg")
    here = pl.ds(pl.multiple_of(cfg * half, 128), half)
    there = pl.ds(pl.multiple_of((1 - cfg) * half, 128), half)
    out_here = pl.ds(pl.multiple_of(cfg * wide, 128), wide)
    out_there = pl.ds(pl.multiple_of((1 - cfg) * wide, 128), wide)
    g0, g1 = guidance_ref[0], guidance_ref[1]
    bias = bias_ref[0:1, :]
    sum_ref[...] = acc_ref[...]

    def branch(b, carry):
        def weight(part, columns, is_query):
            source = normed_q_ref if is_query else normed_ref
            place = slice(part * group + columns.start, part * group + columns.stop)
            return dot(source[b, :, here], mine_ref[:, place]) + dot(
                source[b, :, there], theirs_ref[:, place]
            )

        attend_branch(None, None, weight, gain_ref, bias, head_size, att_ref)
        scale = jnp.where(b == 0, 1.0 - g0, jnp.where(b == 1, g0 - g1, g1))
        sum_ref[:, out_here] += dot(att_ref[...], out_mine_ref[...]) * (
            scale * modulation_ref[b, 2:3, out_here]
        )
        sum_ref[:, out_there] += dot(att_ref[...], out_theirs_ref[...]) * (
            scale * modulation_ref[b, 2:3, out_there]
        )
        return carry

    lax.fori_loop(0, branches, branch, 0)
    if out_parts is None:
        out_ref[...] = sum_ref[...].astype(out_ref.dtype)
    else:
        senders, heads, share, columns = out_parts
        for h in range(heads):
            piece = sum_ref[:, h * columns : (h + 1) * columns].astype(BF16)
            out_ref[:, h] = piece.reshape(senders, share, columns)


def return_kernel(placing_ref, rows_ref, out_ref):
    out_ref[...] = dot(placing_ref[...], rows_ref[...]).astype(BF16)


def on_device(x_latent, windows, coords, modulation, w_qkv, w_out, qk_gain, guidance):
    voxels, width = x_latent.shape
    group = w_qkv.shape[2]
    head_size = width // HEADS
    branches = modulation.shape[0]
    senders = lax.axis_size(("cfg", "vox"))
    heads = lax.axis_size("head")
    cores = lax.axis_size("cfg")
    capacity = SLOTS // senders
    queries = SLOTS // heads
    share = capacity // heads

    outgoing, placing = pl.pallas_call(
        functools.partial(place_kernel, senders, capacity),
        out_shape=(
            jax.ShapeDtypeStruct((SLOTS, width + EXTRA), BF16),
            jax.ShapeDtypeStruct((SLOTS, voxels), BF16),
        ),
        in_specs=[VMEM] * 3,
        out_specs=(VMEM, VMEM),
        compiler_params=params(24),
        name="place",
    )(windows.reshape(1, voxels), coords, x_latent)
    arrived = lax.all_to_all(
        outgoing.reshape(senders, capacity, width + EXTRA),
        ("cfg", "vox"),
        split_axis=0,
        concat_axis=0,
        tiled=True,
    ).reshape(SLOTS, width + EXTRA)

    core = lax.axis_index("cfg")
    flat = w_qkv.reshape(width, 3 * group)
    half = lax.dynamic_slice_in_dim(flat, core * (width // cores), width // cores, 0)
    out_half = lax.dynamic_slice_in_dim(w_out, core * (width // cores), width // cores, 1)
    swap = [(c, (c + 1) % cores) for c in range(cores)]
    others = []
    for distance in range(1, heads):
        turn = [(h, (h + distance) % heads) for h in range(heads)]
        mine = lax.ppermute(half, "head", turn)
        gain = lax.ppermute(qk_gain, "head", turn)
        out_mine = lax.ppermute(out_half, "head", turn)
        theirs = lax.ppermute(mine, "cfg", swap)
        out_theirs = lax.ppermute(out_mine, "cfg", swap)
        others.append((mine, theirs, gain, out_mine, out_theirs))

    table = position_parts(width)
    normed, normed_q, acc, bias = pl.pallas_call(
        functools.partial(own_kernel, senders, head_size),
        out_shape=(
            jax.ShapeDtypeStruct((branches, SLOTS, width), BF16),
            jax.ShapeDtypeStruct((branches, queries, width), BF16),
            jax.ShapeDtypeStruct((queries, width), F32),
            jax.ShapeDtypeStruct((8, SLOTS), F32),
        ),
        in_specs=[SMEM] + [VMEM] * 6,
        out_specs=(VMEM,) * 4,
        scratch_shapes=[pltpu.VMEM((SLOTS, width), F32), pltpu.VMEM((queries, group), BF16)],
        compiler_params=params(44),
        name="own_heads",
    )(guidance, arrived, table, modulation, flat, qk_gain, w_out)

    for number, (mine, theirs, gain, out_mine, out_theirs) in enumerate(others):
        last = number == len(others) - 1
        parts = None
        shape = jax.ShapeDtypeStruct((queries, width), BF16 if last else F32)
        if last and share % 16 == 0:
            parts = (senders, heads, share, width // heads)
            shape = jax.ShapeDtypeStruct(parts, BF16)
        acc = pl.pallas_call(
            functools.partial(other_kernel, head_size, parts),
            out_shape=shape,
            in_specs=[SMEM] + [VMEM] * 10,
            out_specs=VMEM,
            scratch_shapes=[pltpu.VMEM((queries, group), BF16), pltpu.VMEM((queries, width), F32)],
            compiler_params=params(44),
            name="other_heads",
        )(
            guidance,
            normed,
            normed_q,
            acc,
            bias,
            modulation,
            mine,
            theirs,
            gain,
            out_mine,
            out_theirs,
        )
    if share % 16 != 0:
        acc = acc.reshape(senders, share, heads, width // heads).transpose(0, 2, 1, 3)
    back = lax.all_to_all(
        acc.reshape(senders * heads, share, width // heads),
        ("cfg", "vox", "head"),
        split_axis=0,
        concat_axis=0,
        tiled=True,
    )
    return pl.pallas_call(
        return_kernel,
        out_shape=jax.ShapeDtypeStruct((voxels, width // heads), BF16),
        in_specs=[VMEM] * 2,
        out_specs=VMEM,
        compiler_params=params(24),
        name="return_rows",
    )(placing.T, back.reshape(SLOTS, width // heads))


def solution(mesh):
    placed = (
        P(("cfg", "vox"), None),
        P(("cfg", "vox")),
        P(None, ("cfg", "vox")),
        P(),
        P(None, None, "head"),
        P("head", None),
        P(None, "head"),
        P(),
    )
    return jax.shard_map(
        on_device, mesh=mesh, in_specs=placed, out_specs=P(("cfg", "vox"), "head"), check_vma=False
    )
```

```python
import functools

import jax
import jax.numpy as jnp
from jax import lax
from jax.experimental import pallas as pl
from jax.experimental.pallas import tpu as pltpu
from jax.sharding import PartitionSpec as P

HEADS = 16
SLOTS = 512
GRID = 64
EXTRA = 128
BF16 = jnp.bfloat16
F32 = jnp.float32
VMEM = pl.BlockSpec(memory_space=pltpu.VMEM)
SMEM = pl.BlockSpec(memory_space=pltpu.SMEM)
NT = (((1,), (1,)), ((), ()))
TN = (((0,), (0,)), ((), ()))


def params(megabytes):
    return pltpu.CompilerParams(vmem_limit_bytes=megabytes * 1024 * 1024)


def iota(shape, dim):
    return lax.broadcasted_iota(jnp.int32, shape, dim)


def dot(a, b):
    return jnp.dot(a, b, preferred_element_type=F32)


def position_parts(model_width):
    freq_count = model_width // 3 // 2
    frequency = 1.0 / 10000.0 ** (jnp.arange(freq_count, dtype=F32) / freq_count)
    angles = jnp.arange(GRID, dtype=F32)[:, None] * frequency[None, :]
    block = jnp.concatenate([jnp.sin(angles), jnp.cos(angles)], axis=1)
    width = 2 * freq_count
    rows = [
        jnp.pad(block, ((0, 0), (c * width, model_width - (c + 1) * width))) for c in range(3)
    ]
    table = jnp.concatenate(rows, axis=0)
    top = lax.reduce_precision(table, 8, 7)
    rest = table - top
    middle = lax.reduce_precision(rest, 8, 7)
    low = rest - middle
    return jnp.concatenate([top, middle, low], axis=0).astype(BF16)


def place_kernel(senders, capacity, windows_ref, coords_ref, x_ref, out_ref, placing_ref):
    windows = windows_ref[...]
    voxels = windows.shape[1]
    width = x_ref.shape[1]
    member = windows == iota((senders, voxels), 0)
    earlier = (iota((voxels, voxels), 0) < iota((voxels, voxels), 1)).astype(F32).astype(BF16)
    member_f = member.astype(F32)
    before = dot(member_f.astype(BF16), earlier)
    rank = jnp.sum(before * member_f, axis=0, keepdims=True).astype(jnp.int32)
    placed = windows * capacity + rank
    placing = (placed == iota((SLOTS, voxels), 0)).astype(F32).astype(BF16)
    placing_ref[...] = placing
    row = iota((EXTRA, voxels), 0)
    extra = jnp.where(row == 3, 1.0, 0.0).astype(F32)
    for c in range(3):
        extra = jnp.where(row == c, coords_ref[c : c + 1, :].astype(F32), extra)
    out_ref[:, :width] = dot(placing, x_ref[...]).astype(BF16)
    out_ref[:, width:] = lax.dot_general(
        placing, extra.astype(BF16), NT, preferred_element_type=F32
    ).astype(BF16)


def column_norm(rows, gain, head_size):
    blocks = []
    for start in range(0, rows.shape[0], head_size):
        block = rows[start : start + head_size]
        mean = jnp.sum(block * block, axis=0, keepdims=True) * (1.0 / head_size)
        blocks.append(block * lax.rsqrt(mean + 1e-06) * gain[start : start + head_size])
    return jnp.concatenate(blocks, axis=0).astype(BF16)


def attend_tile(normed, normed_q, w_query, w_key, w_value, gain_ref, features, bias, head_size):
    queries, tile = normed_q.shape[0], w_query.shape[0]
    query = lax.dot_general(w_query, normed_q, NT, preferred_element_type=F32)
    query = column_norm(query, gain_ref[0, features, :], head_size)
    key = lax.dot_general(w_key, normed, NT, preferred_element_type=F32)
    key = column_norm(key, gain_ref[1, features, :], head_size)
    value = lax.dot_general(normed, w_value, NT, preferred_element_type=F32).astype(BF16)
    query = (query.astype(F32) * (1.0 / head_size**0.5)).T
    lane_head = iota((queries, tile), 1) // head_size
    count = tile // head_size

    def score(head):
        return dot(jnp.where(lane_head == head, query, 0.0).astype(BF16), key)

    scores = score(0)
    mixed = jnp.zeros((queries, tile), F32)
    step = min(32, queries)
    for head in range(count):
        following = score(head + 1) if head + 1 < count else None
        pieces = []
        for r in range(0, queries, step):
            piece = scores[r : r + step] + bias
            weights = jnp.exp(piece - jnp.max(piece, axis=1, keepdims=True))
            total = jnp.sum(weights, axis=1, keepdims=True)
            pieces.append((weights * (1.0 / total)).astype(BF16))
        attend = jnp.concatenate(pieces, axis=0)
        mixed = jnp.where(lane_head == head, dot(attend, value), mixed)
        scores = following
    return mixed.astype(BF16)


def branch_scales(guidance_ref):
    g0, g1 = guidance_ref[0], guidance_ref[1]
    return 1.0 - g0, g0 - g1, g1


def pick_scale(b, scales):
    return jnp.where(b == 0, scales[0], jnp.where(b == 1, scales[1], scales[2]))


def own_kernel(
    senders,
    head_size,
    guidance_ref,
    rows_ref,
    table_ref,
    modulation_ref,
    w_ref,
    gain_ref,
    w_out_ref,
    normed_ref,
    normed_q_ref,
    acc_ref,
    bias_ref,
    hidden_ref,
    att_ref,
):
    branches, slots, width = normed_ref.shape
    queries = normed_q_ref.shape[1]
    group = att_ref.shape[1]
    capacity = slots // senders
    share = queries // senders
    first = lax.axis_index("head") * share
    scales = branch_scales(guidance_ref)
    total = (scales[0] + scales[1]) + scales[2]

    extra = rows_ref[:, width:]
    pick = ((iota((8, EXTRA), 1) == 3)).astype(F32).astype(BF16)
    live = lax.dot_general(pick, extra, NT, preferred_element_type=F32)
    bias_ref[...] = jnp.where(live > 0.5, 0.0, -1e30)

    spots = extra.astype(F32)
    lane = iota((slots, 3 * GRID), 1)
    wanted = jnp.where(
        lane < GRID,
        spots[:, 0:1],
        jnp.where(lane < 2 * GRID, spots[:, 1:2], spots[:, 2:3]),
    )
    chosen = (wanted == (lane % GRID).astype(F32)).astype(F32).astype(BF16)
    chosen = jnp.concatenate([chosen, chosen, chosen], axis=1)
    hidden_ref[...] = dot(chosen, table_ref[...]) + rows_ref[:, :width].astype(F32)

    chunk = 32

    def normalise(i, carry):
        rows = pl.ds(pl.multiple_of(i * chunk, chunk), chunk)
        hidden = hidden_ref[rows, :]
        centred = hidden - jnp.mean(hidden, axis=1, keepdims=True)
        spread = jnp.mean(centred * centred, axis=1, keepdims=True)
        normal = centred * lax.rsqrt(spread + 1e-06)
        for b in range(branches):
            normed_ref[b, rows, :] = (
                normal * (1.0 + modulation_ref[b, 1:2, :]) + modulation_ref[b, 0:1, :]
            ).astype(BF16)
        return carry

    lax.fori_loop(0, slots // chunk, normalise, 0, unroll=2)

    if share % 16 == 0:
        for s in range(senders):
            source = pl.ds(pl.multiple_of(s * capacity + first, 16), share)
            target = slice(s * share, (s + 1) * share)
            acc_ref[target, :] = hidden_ref[source, :] * total
            for b in range(branches):
                normed_q_ref[b, target, :] = normed_ref[b, source, :]
    else:
        row = iota((queries, slots), 0)
        wanted_slot = (row // share) * capacity + first + row % share
        chooser = (wanted_slot == iota((queries, slots), 1)).astype(F32)
        picked = jnp.dot(
            chooser, hidden_ref[...], preferred_element_type=F32, precision=lax.Precision.HIGHEST
        )
        acc_ref[...] = picked * total
        for b in range(branches):
            normed_q_ref[b] = dot(chooser.astype(BF16), normed_ref[b]).astype(BF16)

    bias = bias_ref[0:1, :]
    tile = min(256, group)

    def branch(b, carry):
        for start in range(0, group, tile):
            features = slice(start, start + tile)
            att_ref[:, features] = attend_tile(
                normed_ref[b],
                normed_q_ref[b],
                w_ref[0, features, :],
                w_ref[1, features, :],
                w_ref[2, features, :],
                gain_ref,
                features,
                bias,
                head_size,
            )
        acc_ref[...] += dot(att_ref[...], w_out_ref[...]) * (
            pick_scale(b, scales) * modulation_ref[b, 2:3, :]
        )
        return carry

    lax.fori_loop(0, branches, branch, 0)


def other_kernel(head_size, normed_ref, normed_q_ref, bias_ref, w_ref, gain_ref, att_ref):
    branches, tile = att_ref.shape[0], att_ref.shape[2]
    bias = bias_ref[0:1, :]

    def branch(b, carry):
        att_ref[b] = attend_tile(
            normed_ref[b],
            normed_q_ref[b],
            w_ref[0],
            w_ref[1],
            w_ref[2],
            gain_ref,
            slice(0, tile),
            bias,
            head_size,
        )
        return carry

    lax.fori_loop(0, branches, branch, 0)


def finish_kernel(out_parts, guidance_ref, acc_ref, modulation_ref, *refs):
    out_ref, pairs = refs[-1], refs[:-1]
    half = len(pairs) // 2
    scales = branch_scales(guidance_ref)
    total = acc_ref[...]
    for b in range(modulation_ref.shape[0]):
        part = dot(pairs[0][b], pairs[half][...])
        for n in range(1, half):
            part = part + dot(pairs[n][b], pairs[half + n][...])
        total = total + part * (scales[b] * modulation_ref[b, 2:3, :])
    if out_parts is None:
        out_ref[...] = total.astype(BF16)
    else:
        senders, heads, share, columns = out_parts
        for h in range(heads):
            piece = total[:, h * columns : (h + 1) * columns].astype(BF16)
            out_ref[:, h] = piece.reshape(senders, share, columns)


def return_kernel(placing_ref, rows_ref, out_ref):
    out_ref[...] = dot(placing_ref[...], rows_ref[...]).astype(BF16)


def on_device(x_latent, windows, coords, modulation, w_qkv, w_out, qk_gain, guidance):
    voxels, width = x_latent.shape
    group = w_qkv.shape[2]
    head_size = width // HEADS
    branches = modulation.shape[0]
    senders = lax.axis_size(("cfg", "vox"))
    heads = lax.axis_size("head")
    cores = lax.axis_size("cfg")
    capacity = SLOTS // senders
    queries = SLOTS // heads
    share = capacity // heads

    outgoing, placing = pl.pallas_call(
        functools.partial(place_kernel, senders, capacity),
        out_shape=(
            jax.ShapeDtypeStruct((SLOTS, width + EXTRA), BF16),
            jax.ShapeDtypeStruct((SLOTS, voxels), BF16),
        ),
        in_specs=[VMEM] * 3,
        out_specs=(VMEM, VMEM),
        compiler_params=params(16),
        name="place",
    )(windows.reshape(1, voxels), coords, x_latent)
    arrived = lax.all_to_all(
        outgoing.reshape(senders, capacity, width + EXTRA),
        ("cfg", "vox"),
        split_axis=0,
        concat_axis=0,
        tiled=True,
    ).reshape(SLOTS, width + EXTRA)

    w_qkv, w_out_sent, qk_gain, outgoing_done = lax.optimization_barrier(
        (w_qkv, w_out, qk_gain, outgoing)
    )
    del outgoing_done
    tile = group // cores
    start = lax.axis_index("cfg") * tile
    half = jnp.transpose(lax.dynamic_slice_in_dim(w_qkv, start, tile, 2), (1, 2, 0))
    out_half = lax.dynamic_slice_in_dim(w_out_sent, start, tile, 0)
    gain_half = lax.dynamic_slice_in_dim(qk_gain, start, tile, 1)
    swap = [(c, (c + 1) % cores) for c in range(cores)]
    fetched = []
    for distance in range(1, heads):
        turn = [(h, (h + distance) % heads) for h in range(heads)]
        fetched.append(tuple(lax.ppermute(a, "head", turn) for a in (half, gain_half, out_half)))

    table = position_parts(width)
    normed, normed_q, acc, bias = pl.pallas_call(
        functools.partial(own_kernel, senders, head_size),
        out_shape=(
            jax.ShapeDtypeStruct((branches, SLOTS, width), BF16),
            jax.ShapeDtypeStruct((branches, queries, width), BF16),
            jax.ShapeDtypeStruct((queries, width), F32),
            jax.ShapeDtypeStruct((8, SLOTS), F32),
        ),
        in_specs=[SMEM] + [VMEM] * 6,
        out_specs=(VMEM,) * 4,
        scratch_shapes=[pltpu.VMEM((SLOTS, width), F32), pltpu.VMEM((queries, group), BF16)],
        compiler_params=params(26),
        name="own_heads",
    )(
        guidance,
        arrived,
        table,
        modulation,
        jnp.transpose(w_qkv, (1, 2, 0)),
        qk_gain[:, :, None],
        w_out,
    )

    def attend(weights, gain):
        return pl.pallas_call(
            functools.partial(other_kernel, head_size),
            out_shape=jax.ShapeDtypeStruct((branches, queries, tile), BF16),
            in_specs=[VMEM] * 5,
            out_specs=VMEM,
            compiler_params=params(20),
            name="other_heads",
        )(normed, normed_q, bias, weights, gain[:, :, None])

    attended, outs = [], []
    ahead = bias
    for weights, gain, out_rows in fetched:
        weights, gain, ahead = lax.optimization_barrier((weights, gain, ahead))
        swapped = lax.ppermute(weights, "cfg", swap), lax.ppermute(gain, "cfg", swap)
        mine = attend(weights, gain)
        out_rows, mine = lax.optimization_barrier((out_rows, mine))
        out_swapped = lax.ppermute(out_rows, "cfg", swap)
        theirs = attend(*swapped)
        ahead = theirs
        attended += [mine, theirs]
        outs += [out_rows, out_swapped]

    parts = None
    shape = jax.ShapeDtypeStruct((queries, width), BF16)
    if share % 16 == 0:
        parts = (senders, heads, share, width // heads)
        shape = jax.ShapeDtypeStruct(parts, BF16)
    acc = pl.pallas_call(
        functools.partial(finish_kernel, parts),
        out_shape=shape,
        in_specs=[SMEM] + [VMEM] * (2 + 2 * len(outs)),
        out_specs=VMEM,
        compiler_params=params(20),
        name="finish",
    )(guidance, acc, modulation, *attended, *outs)
    if share % 16 != 0:
        acc = acc.reshape(senders, share, heads, width // heads).transpose(0, 2, 1, 3)
    back = lax.all_to_all(
        acc.reshape(senders * heads, share, width // heads),
        ("cfg", "vox", "head"),
        split_axis=0,
        concat_axis=0,
        tiled=True,
    )
    return pl.pallas_call(
        return_kernel,
        out_shape=jax.ShapeDtypeStruct((voxels, width // heads), BF16),
        in_specs=[VMEM] * 2,
        out_specs=VMEM,
        compiler_params=params(16),
        name="return_rows",
    )(placing.T, back.reshape(SLOTS, width // heads))


def solution(mesh):
    placed = (
        P(("cfg", "vox"), None),
        P(("cfg", "vox")),
        P(None, ("cfg", "vox")),
        P(),
        P(None, None, "head"),
        P("head", None),
        P(None, "head"),
        P(),
    )
    return jax.shard_map(
        on_device, mesh=mesh, in_specs=placed, out_specs=P(("cfg", "vox"), "head"), check_vma=False
    )
```

```python
import functools

import jax
import jax.numpy as jnp
from jax import lax
from jax.experimental import pallas as pl
from jax.experimental.pallas import tpu as pltpu
from jax.sharding import PartitionSpec as P

HEADS = 16
SLOTS = 512
GRID = 64
EXTRA = 128
BF16 = jnp.bfloat16
F32 = jnp.float32
VMEM = pl.BlockSpec(memory_space=pltpu.VMEM)
SMEM = pl.BlockSpec(memory_space=pltpu.SMEM)
HBM = pl.BlockSpec(memory_space=pltpu.HBM)
NT = (((1,), (1,)), ((), ()))
TN = (((0,), (0,)), ((), ()))


def params(megabytes):
    return pltpu.CompilerParams(vmem_limit_bytes=megabytes * 1024 * 1024)


def iota(shape, dim):
    return lax.broadcasted_iota(jnp.int32, shape, dim)


def dot(a, b):
    return jnp.dot(a, b, preferred_element_type=F32)


def position_parts(model_width):
    freq_count = model_width // 3 // 2
    frequency = 1.0 / 10000.0 ** (jnp.arange(freq_count, dtype=F32) / freq_count)
    angles = jnp.arange(GRID, dtype=F32)[:, None] * frequency[None, :]
    block = jnp.concatenate([jnp.sin(angles), jnp.cos(angles)], axis=1)
    width = 2 * freq_count
    rows = [
        jnp.pad(block, ((0, 0), (c * width, model_width - (c + 1) * width))) for c in range(3)
    ]
    table = jnp.concatenate(rows, axis=0)
    top = lax.reduce_precision(table, 8, 7)
    rest = table - top
    middle = lax.reduce_precision(rest, 8, 7)
    low = rest - middle
    return jnp.concatenate([top, middle, low], axis=0).astype(BF16)


def place_kernel(senders, capacity, windows_ref, coords_ref, x_hbm, out_ref, placed_ref, x_ref, sem):
    load = pltpu.make_async_copy(x_hbm, x_ref, sem)
    load.start()
    voxels, width = x_hbm.shape
    windows = windows_ref[...].reshape(1, voxels)
    member = windows == iota((senders, voxels), 0)
    earlier = (iota((voxels, voxels), 0) < iota((voxels, voxels), 1)).astype(F32).astype(BF16)
    member_f = member.astype(F32)
    before = dot(member_f.astype(BF16), earlier)
    rank = jnp.sum(before * member_f, axis=0, keepdims=True).astype(jnp.int32)
    placed = windows * capacity + rank
    placed_ref[...] = placed.astype(F32)
    placing = (placed == iota((SLOTS, voxels), 0)).astype(F32).astype(BF16)
    row = iota((EXTRA, voxels), 0)
    extra = jnp.where(row == 3, 1.0, 0.0).astype(F32)
    for c in range(3):
        extra = jnp.where(row == c, coords_ref[c : c + 1, :].astype(F32), extra)
    out_ref[:, width:] = lax.dot_general(
        placing, extra.astype(BF16), NT, preferred_element_type=F32
    ).astype(BF16)
    load.wait()
    out_ref[:, :width] = dot(placing, x_ref[...]).astype(BF16)


def column_norm(rows, gain, head_size):
    blocks = []
    for start in range(0, rows.shape[0], head_size):
        block = rows[start : start + head_size]
        mean = jnp.sum(block * block, axis=0, keepdims=True) * (1.0 / head_size)
        blocks.append(block * lax.rsqrt(mean + 1e-06) * gain[start : start + head_size])
    return jnp.concatenate(blocks, axis=0).astype(BF16)


def attend_tile(normed, normed_q, w_query, w_key, w_value, gains, bias, head_size):
    queries, tile = normed_q.shape[0], w_query.shape[0]
    query = lax.dot_general(w_query, normed_q, NT, preferred_element_type=F32)
    query = column_norm(query, gains[:, 0:1], head_size)
    key = lax.dot_general(w_key, normed, NT, preferred_element_type=F32)
    key = column_norm(key, gains[:, 1:2], head_size)
    value = lax.dot_general(normed, w_value, NT, preferred_element_type=F32).astype(BF16)
    query = (query.astype(F32) * (1.0 / head_size**0.5)).T
    lane_head = iota((queries, tile), 1) // head_size
    count = tile // head_size

    def score(head):
        return dot(jnp.where(lane_head == head, query, 0.0).astype(BF16), key)

    scores = score(0)
    mixed = jnp.zeros((queries, tile), F32)
    step = min(32, queries)
    for head in range(count):
        following = score(head + 1) if head + 1 < count else None
        pieces = []
        for r in range(0, queries, step):
            piece = scores[r : r + step] + bias
            weights = jnp.exp(piece - jnp.max(piece, axis=1, keepdims=True))
            total = jnp.sum(weights, axis=1, keepdims=True)
            pieces.append((weights * (1.0 / total)).astype(BF16))
        attend = jnp.concatenate(pieces, axis=0)
        mixed = jnp.where(lane_head == head, dot(attend, value), mixed)
        scores = following
    return mixed.astype(BF16)


def branch_scales(guidance_ref):
    g0, g1 = guidance_ref[0], guidance_ref[1]
    return 1.0 - g0, g0 - g1, g1


def pick_scale(b, scales):
    return jnp.where(b == 0, scales[0], jnp.where(b == 1, scales[1], scales[2]))


def own_kernel(
    senders,
    head_size,
    guidance_ref,
    modulation_ref,
    rows_hbm,
    table_hbm,
    w_hbm,
    gain_hbm,
    w_out_hbm,
    normed_hbm,
    normed_q_hbm,
    acc_hbm,
    bias_hbm,
    rows_ref,
    table_ref,
    w_ref,
    gain_ref,
    w_out_ref,
    normed_ref,
    normed_q_ref,
    acc_ref,
    bias_ref,
    hidden_ref,
    att_ref,
    in_sems,
    out_sems,
):
    loads = [
        pltpu.make_async_copy(source, target, in_sems.at[n])
        for n, (source, target) in enumerate(
            (
                (rows_hbm, rows_ref),
                (table_hbm, table_ref),
                (w_hbm, w_ref),
                (gain_hbm, gain_ref),
                (w_out_hbm, w_out_ref),
            )
        )
    ]
    stores = [
        pltpu.make_async_copy(source, target, out_sems.at[n])
        for n, (source, target) in enumerate(
            (
                (normed_ref, normed_hbm),
                (normed_q_ref, normed_q_hbm),
                (bias_ref, bias_hbm),
                (acc_ref, acc_hbm),
            )
        )
    ]
    for load in loads:
        load.start()
    branches, slots, width = normed_ref.shape
    queries = normed_q_ref.shape[1]
    group = att_ref.shape[1]
    capacity = slots // senders
    share = queries // senders
    first = lax.axis_index("head") * share
    scales = branch_scales(guidance_ref)
    total = (scales[0] + scales[1]) + scales[2]

    loads[0].wait()
    extra = rows_ref[:, width:]
    pick = ((iota((8, EXTRA), 1) == 3)).astype(F32).astype(BF16)
    live = lax.dot_general(pick, extra, NT, preferred_element_type=F32)
    bias_ref[...] = jnp.where(live > 0.5, 0.0, -1e30)

    spots = extra.astype(F32)
    lane = iota((slots, 3 * GRID), 1)
    wanted = jnp.where(
        lane < GRID,
        spots[:, 0:1],
        jnp.where(lane < 2 * GRID, spots[:, 1:2], spots[:, 2:3]),
    )
    chosen = (wanted == (lane % GRID).astype(F32)).astype(F32).astype(BF16)
    chosen = jnp.concatenate([chosen, chosen, chosen], axis=1)
    loads[1].wait()
    hidden_ref[...] = dot(chosen, table_ref[...]) + rows_ref[:, :width].astype(F32)

    chunk = 32

    def normalise(i, carry):
        rows = pl.ds(pl.multiple_of(i * chunk, chunk), chunk)
        hidden = hidden_ref[rows, :]
        centred = hidden - jnp.mean(hidden, axis=1, keepdims=True)
        spread = jnp.mean(centred * centred, axis=1, keepdims=True)
        normal = centred * lax.rsqrt(spread + 1e-06)
        for b in range(branches):
            normed_ref[b, rows, :] = (
                normal * (1.0 + modulation_ref[b, 1:2, :]) + modulation_ref[b, 0:1, :]
            ).astype(BF16)
        return carry

    lax.fori_loop(0, slots // chunk, normalise, 0, unroll=2)
    stores[0].start()
    stores[2].start()

    if share % 16 == 0:
        for s in range(senders):
            source = pl.ds(pl.multiple_of(s * capacity + first, 16), share)
            target = slice(s * share, (s + 1) * share)
            acc_ref[target, :] = hidden_ref[source, :] * total
            for b in range(branches):
                normed_q_ref[b, target, :] = normed_ref[b, source, :]
    else:
        row = iota((queries, slots), 0)
        wanted_slot = (row // share) * capacity + first + row % share
        chooser = (wanted_slot == iota((queries, slots), 1)).astype(F32)
        picked = jnp.dot(
            chooser, hidden_ref[...], preferred_element_type=F32, precision=lax.Precision.HIGHEST
        )
        acc_ref[...] = picked * total
        for b in range(branches):
            normed_q_ref[b] = dot(chooser.astype(BF16), normed_ref[b]).astype(BF16)
    stores[1].start()

    bias = bias_ref[0:1, :]
    tile = min(256, group)
    for load in loads[2:]:
        load.wait()

    def branch(b, carry):
        for start in range(0, group, tile):
            features = slice(start, start + tile)
            att_ref[:, features] = attend_tile(
                normed_ref[b],
                normed_q_ref[b],
                w_ref[0, features, :],
                w_ref[1, features, :],
                w_ref[2, features, :],
                gain_ref[features, :],
                bias,
                head_size,
            )
        acc_ref[...] += dot(att_ref[...], w_out_ref[...]) * (
            pick_scale(b, scales) * modulation_ref[b, 2:3, :]
        )
        return carry

    lax.fori_loop(0, branches, branch, 0)
    stores[3].start()
    for store in stores:
        store.wait()


def other_kernel(
    head_size,
    swapped,
    normed_hbm,
    normed_q_hbm,
    bias_hbm,
    w_hbm,
    gain_hbm,
    att_hbm,
    normed_ref,
    normed_q_ref,
    bias_ref,
    w_ref,
    gain_ref,
    att_ref,
    in_sems,
    normed_sems,
    normed_q_sems,
    out_sems,
):
    branches, tile = att_ref.shape[0], att_ref.shape[2]
    small = [
        pltpu.make_async_copy(source, target, in_sems.at[n])
        for n, (source, target) in enumerate(
            ((w_hbm, w_ref), (bias_hbm, bias_ref), (gain_hbm, gain_ref))
        )
    ]

    def load(b):
        return (
            pltpu.make_async_copy(normed_q_hbm.at[b], normed_q_ref.at[b], normed_q_sems.at[b]),
            pltpu.make_async_copy(normed_hbm.at[b], normed_ref.at[b], normed_sems.at[b]),
        )

    def store(b):
        return pltpu.make_async_copy(att_ref.at[b], att_hbm.at[b], out_sems.at[b])

    for copy in small:
        copy.start()
    for b in range(branches):
        for copy in load(b):
            copy.start()
    core = lax.axis_index("cfg")
    core = 1 - core if swapped else core
    features = pl.ds(pl.multiple_of(core * tile, tile), tile)
    for copy in small:
        copy.wait()
    bias = bias_ref[0:1, :]
    gains = gain_ref[features, :]

    def branch(b, carry):
        for copy in load(b):
            copy.wait()
        att_ref[b] = attend_tile(
            normed_ref[b], normed_q_ref[b], w_ref[0], w_ref[1], w_ref[2], gains, bias, head_size
        )
        store(b).start()
        return carry

    lax.fori_loop(0, branches, branch, 0)
    for b in range(branches):
        store(b).wait()


def finish_kernel(out_parts, count, guidance_ref, modulation_ref, acc_hbm, *refs):
    sources = refs[: 2 * count] + (acc_hbm,)
    out_ref, held, sems = refs[2 * count], refs[2 * count + 1 : -1], refs[-1]
    loads = [
        pltpu.make_async_copy(source, target, sems.at[n])
        for n, (source, target) in enumerate(zip(sources, held))
    ]
    for load in loads:
        load.start()
    scales = branch_scales(guidance_ref)
    for load in loads:
        load.wait()
    total = held[-1][...]
    for b in range(modulation_ref.shape[0]):
        part = dot(held[0][b], held[count][...])
        for n in range(1, count):
            part = part + dot(held[n][b], held[count + n][...])
        total = total + part * (scales[b] * modulation_ref[b, 2:3, :])
    if out_parts is None:
        out_ref[...] = total.astype(BF16)
    else:
        senders, heads, share, columns = out_parts
        for h in range(heads):
            piece = total[:, h * columns : (h + 1) * columns].astype(BF16)
            out_ref[:, h] = piece.reshape(senders, share, columns)


def return_kernel(placed_ref, rows_hbm, out_ref, rows_ref, sem):
    load = pltpu.make_async_copy(rows_hbm, rows_ref, sem)
    load.start()
    voxels = placed_ref.shape[1]
    column = jnp.broadcast_to(placed_ref[...], (128, voxels)).T
    column = column.astype(jnp.int32)
    lane = iota((voxels, 128), 1)
    placing = jnp.concatenate(
        [(column == lane + start).astype(F32).astype(BF16) for start in range(0, SLOTS, 128)], axis=1
    )
    load.wait()
    out_ref[...] = dot(placing, rows_ref[...]).astype(BF16)


def on_device(x_latent, windows, coords, modulation, w_qkv, w_out, qk_gain, guidance):
    voxels, width = x_latent.shape
    group = w_qkv.shape[2]
    head_size = width // HEADS
    branches = modulation.shape[0]
    senders = lax.axis_size(("cfg", "vox"))
    heads = lax.axis_size("head")
    cores = lax.axis_size("cfg")
    capacity = SLOTS // senders
    queries = SLOTS // heads
    share = capacity // heads

    tile = group // cores
    vmem, dma = pltpu.VMEM, pltpu.SemaphoreType.DMA
    outgoing, placed = pl.pallas_call(
        functools.partial(place_kernel, senders, capacity),
        out_shape=(
            jax.ShapeDtypeStruct((SLOTS, width + EXTRA), BF16),
            jax.ShapeDtypeStruct((1, voxels), F32),
        ),
        in_specs=[VMEM, VMEM, HBM],
        out_specs=(VMEM, VMEM),
        scratch_shapes=[vmem((voxels, width), BF16), dma(())],
        compiler_params=params(16),
        name="place",
    )(windows, coords, x_latent)
    arrived = lax.all_to_all(
        outgoing.reshape(senders, capacity, width + EXTRA),
        ("cfg", "vox"),
        split_axis=0,
        concat_axis=0,
        tiled=True,
    ).reshape(SLOTS, width + EXTRA)

    w_qkv, w_out_sent, qk_gain, outgoing_done = lax.optimization_barrier(
        (w_qkv, w_out, qk_gain, outgoing)
    )
    del outgoing_done
    start = lax.axis_index("cfg") * tile
    half = jnp.transpose(lax.dynamic_slice_in_dim(w_qkv, start, tile, 2), (1, 2, 0))
    out_half = lax.dynamic_slice_in_dim(w_out_sent, start, tile, 0)
    swap = [(c, (c + 1) % cores) for c in range(cores)]
    fetched, gain_columns = [], []
    for distance in range(1, heads):
        turn = [(h, (h + distance) % heads) for h in range(heads)]
        fetched.append((lax.ppermute(half, "head", turn), lax.ppermute(out_half, "head", turn)))
        gain_columns.append(lax.ppermute(qk_gain, "head", turn).T)
    own_gain = qk_gain.T
    table = position_parts(width)
    arrived, own_gain, table, *gain_columns = lax.optimization_barrier(
        (arrived, own_gain, table, *gain_columns)
    )

    normed, normed_q, acc, bias = pl.pallas_call(
        functools.partial(own_kernel, senders, head_size),
        out_shape=(
            jax.ShapeDtypeStruct((branches, SLOTS, width), BF16),
            jax.ShapeDtypeStruct((branches, queries, width), BF16),
            jax.ShapeDtypeStruct((queries, width), F32),
            jax.ShapeDtypeStruct((8, SLOTS), F32),
        ),
        in_specs=[SMEM, VMEM] + [HBM] * 5,
        out_specs=(HBM,) * 4,
        scratch_shapes=[
            vmem((SLOTS, width + EXTRA), BF16),
            vmem(table.shape, BF16),
            vmem((3, group, width), BF16),
            vmem((group, 2), F32),
            vmem((group, width), BF16),
            vmem((branches, SLOTS, width), BF16),
            vmem((branches, queries, width), BF16),
            vmem((queries, width), F32),
            vmem((8, SLOTS), F32),
            vmem((SLOTS, width), F32),
            vmem((queries, group), BF16),
            dma((5,)),
            dma((4,)),
        ],
        compiler_params=params(40),
        name="own_heads",
    )(
        guidance,
        modulation,
        arrived,
        table,
        jnp.transpose(w_qkv, (1, 2, 0)),
        own_gain,
        w_out,
    )

    def attend(weights, gain, swapped):
        return pl.pallas_call(
            functools.partial(other_kernel, head_size, swapped),
            out_shape=jax.ShapeDtypeStruct((branches, queries, tile), BF16),
            in_specs=[HBM] * 5,
            out_specs=HBM,
            scratch_shapes=[
                vmem((branches, SLOTS, width), BF16),
                vmem((branches, queries, width), BF16),
                vmem((8, SLOTS), F32),
                vmem((3, tile, width), BF16),
                vmem((group, 2), F32),
                vmem((branches, queries, tile), BF16),
                dma((3,)),
                dma((branches,)),
                dma((branches,)),
                dma((branches,)),
            ],
            compiler_params=params(32),
            name="other_heads",
        )(normed, normed_q, bias, weights, gain)

    attended, outs = [], []
    ahead = bias
    for (weights, out_rows), gain in zip(fetched, gain_columns):
        weights, ahead = lax.optimization_barrier((weights, ahead))
        swapped = lax.ppermute(weights, "cfg", swap)
        mine = attend(weights, gain, False)
        out_rows, mine = lax.optimization_barrier((out_rows, mine))
        out_swapped = lax.ppermute(out_rows, "cfg", swap)
        theirs = attend(swapped, gain, True)
        ahead = theirs
        attended += [mine, theirs]
        outs += [out_rows, out_swapped]

    parts = None
    shape = jax.ShapeDtypeStruct((queries, width), BF16)
    if share % 16 == 0:
        parts = (senders, heads, share, width // heads)
        shape = jax.ShapeDtypeStruct(parts, BF16)
    count = len(outs)
    acc = pl.pallas_call(
        functools.partial(finish_kernel, parts, count),
        out_shape=shape,
        in_specs=[SMEM, VMEM] + [HBM] * (1 + 2 * count),
        out_specs=VMEM,
        scratch_shapes=[vmem((branches, queries, tile), BF16)] * count
        + [vmem((tile, width), BF16)] * count
        + [vmem((queries, width), F32), dma((2 * count + 1,))],
        compiler_params=params(32),
        name="finish",
    )(guidance, modulation, acc, *attended, *outs)
    if share % 16 != 0:
        acc = acc.reshape(senders, share, heads, width // heads).transpose(0, 2, 1, 3)
    back = lax.all_to_all(
        acc.reshape(senders * heads, share, width // heads),
        ("cfg", "vox", "head"),
        split_axis=0,
        concat_axis=0,
        tiled=True,
    )
    return pl.pallas_call(
        return_kernel,
        out_shape=jax.ShapeDtypeStruct((voxels, width // heads), BF16),
        in_specs=[VMEM, HBM],
        out_specs=VMEM,
        scratch_shapes=[vmem((SLOTS, width // heads), BF16), dma(())],
        compiler_params=params(16),
        name="return_rows",
    )(placed, back.reshape(SLOTS, width // heads))


def solution(mesh):
    placed = (
        P(("cfg", "vox"), None),
        P(("cfg", "vox")),
        P(None, ("cfg", "vox")),
        P(),
        P(None, None, "head"),
        P("head", None),
        P(None, "head"),
        P(),
    )
    return jax.shard_map(
        on_device, mesh=mesh, in_specs=placed, out_specs=P(("cfg", "vox"), "head"), check_vma=False
    )
```

```python
import functools

import jax
import jax.numpy as jnp
from jax import lax
from jax.experimental import pallas as pl
from jax.experimental.pallas import tpu as pltpu
from jax.sharding import PartitionSpec as P

HEADS = 16
SLOTS = 512
GRID = 64
EXTRA = 128
BF16 = jnp.bfloat16
F32 = jnp.float32
VMEM = pl.BlockSpec(memory_space=pltpu.VMEM)
SMEM = pl.BlockSpec(memory_space=pltpu.SMEM)
HBM = pl.BlockSpec(memory_space=pltpu.HBM)
LITTLE = pl.CostEstimate(flops=1, bytes_accessed=1, transcendentals=1)
NT = (((1,), (1,)), ((), ()))


def params(megabytes):
    return pltpu.CompilerParams(vmem_limit_bytes=megabytes * 1024 * 1024)


def iota(shape, dim):
    return lax.broadcasted_iota(jnp.int32, shape, dim)


def dot(a, b):
    return jnp.dot(a, b, preferred_element_type=F32)


def position_parts(model_width):
    freq_count = model_width // 3 // 2
    frequency = 1.0 / 10000.0 ** (jnp.arange(freq_count, dtype=F32) / freq_count)
    angles = jnp.arange(GRID, dtype=F32)[:, None] * frequency[None, :]
    block = jnp.concatenate([jnp.sin(angles), jnp.cos(angles)], axis=1)
    width = 2 * freq_count
    rows = [
        jnp.pad(block, ((0, 0), (c * width, model_width - (c + 1) * width))) for c in range(3)
    ]
    table = jnp.concatenate(rows, axis=0)
    top = lax.reduce_precision(table, 8, 7)
    rest = table - top
    middle = lax.reduce_precision(rest, 8, 7)
    low = rest - middle
    return jnp.concatenate([top, middle, low], axis=0).astype(BF16)


def place_kernel(
    senders,
    capacity,
    windows_hbm,
    coords_hbm,
    x_hbm,
    out_ref,
    placed_ref,
    x_ref,
    windows_ref,
    coords_ref,
    sems,
):
    loads = [
        pltpu.make_async_copy(source, target, sems.at[n])
        for n, (source, target) in enumerate(
            ((windows_hbm, windows_ref), (coords_hbm, coords_ref), (x_hbm, x_ref))
        )
    ]
    for load in loads:
        load.start()
    voxels, width = x_hbm.shape
    loads[0].wait()
    windows = windows_ref[...].reshape(1, voxels)
    member = windows == iota((senders, voxels), 0)
    earlier = (iota((voxels, voxels), 0) < iota((voxels, voxels), 1)).astype(F32).astype(BF16)
    member_f = member.astype(F32)
    before = dot(member_f.astype(BF16), earlier)
    rank = jnp.sum(before * member_f, axis=0, keepdims=True).astype(jnp.int32)
    placed = windows * capacity + rank
    placed_ref[...] = placed.astype(F32)
    placing = (placed == iota((SLOTS, voxels), 0)).astype(F32).astype(BF16)
    loads[1].wait()
    row = iota((EXTRA, voxels), 0)
    extra = jnp.where(row == 3, 1.0, 0.0).astype(F32)
    for c in range(3):
        extra = jnp.where(row == c, coords_ref[c : c + 1, :].astype(F32), extra)
    out_ref[:, width:] = lax.dot_general(
        placing, extra.astype(BF16), NT, preferred_element_type=F32
    ).astype(BF16)
    loads[2].wait()
    out_ref[:, :width] = dot(placing, x_ref[...]).astype(BF16)


def column_norm(rows, gain, head_size):
    blocks = []
    for start in range(0, rows.shape[0], head_size):
        block = rows[start : start + head_size]
        mean = jnp.sum(block * block, axis=0, keepdims=True) * (1.0 / head_size)
        blocks.append(block * lax.rsqrt(mean + 1e-06) * gain[start : start + head_size])
    return jnp.concatenate(blocks, axis=0).astype(BF16)


def attend_tile(normed, normed_q, w_query, w_key, w_value, gains, bias, head_size):
    queries, tile = normed_q.shape[0], w_query.shape[0]
    query = lax.dot_general(w_query, normed_q, NT, preferred_element_type=F32)
    query = column_norm(query, gains[:, 0:1], head_size)
    key = lax.dot_general(w_key, normed, NT, preferred_element_type=F32)
    key = column_norm(key, gains[:, 1:2], head_size)
    value = lax.dot_general(normed, w_value, NT, preferred_element_type=F32).astype(BF16)
    query = (query.astype(F32) * (1.0 / head_size**0.5)).T
    lane_head = iota((queries, tile), 1) // head_size
    count = tile // head_size

    def score(head):
        return dot(jnp.where(lane_head == head, query, 0.0).astype(BF16), key)

    scores = score(0)
    mixed = jnp.zeros((queries, tile), F32)
    step = min(32, queries)
    for head in range(count):
        following = score(head + 1) if head + 1 < count else None
        pieces = []
        for r in range(0, queries, step):
            piece = scores[r : r + step] + bias
            weights = jnp.exp(piece - jnp.max(piece, axis=1, keepdims=True))
            total = jnp.sum(weights, axis=1, keepdims=True)
            pieces.append((weights * (1.0 / total)).astype(BF16))
        attend = jnp.concatenate(pieces, axis=0)
        mixed = jnp.where(lane_head == head, dot(attend, value), mixed)
        scores = following
    return mixed.astype(BF16)


def branch_scales(guidance_ref):
    g0, g1 = guidance_ref[0], guidance_ref[1]
    return 1.0 - g0, g0 - g1, g1


def pick_scale(b, scales):
    return jnp.where(b == 0, scales[0], jnp.where(b == 1, scales[1], scales[2]))


def own_kernel(
    senders,
    head_size,
    guidance_ref,
    modulation_ref,
    rows_hbm,
    table_hbm,
    w_hbm,
    gain_hbm,
    w_out_hbm,
    normed_hbm,
    normed_q_hbm,
    acc_hbm,
    bias_hbm,
    rows_ref,
    table_ref,
    w_ref,
    gain_ref,
    w_out_ref,
    normed_ref,
    normed_q_ref,
    acc_ref,
    bias_ref,
    hidden_ref,
    att_ref,
    in_sems,
    out_sems,
):
    loads = [
        pltpu.make_async_copy(source, target, in_sems.at[n])
        for n, (source, target) in enumerate(
            (
                (rows_hbm, rows_ref),
                (table_hbm, table_ref),
                (w_hbm, w_ref),
                (gain_hbm, gain_ref),
                (w_out_hbm, w_out_ref),
            )
        )
    ]
    stores = [
        pltpu.make_async_copy(source, target, out_sems.at[n])
        for n, (source, target) in enumerate(
            (
                (normed_ref, normed_hbm),
                (normed_q_ref, normed_q_hbm),
                (bias_ref, bias_hbm),
                (acc_ref, acc_hbm),
            )
        )
    ]
    for load in loads:
        load.start()
    branches, slots, width = normed_ref.shape
    queries = normed_q_ref.shape[1]
    group = att_ref.shape[1]
    capacity = slots // senders
    share = queries // senders
    first = lax.axis_index("head") * share
    scales = branch_scales(guidance_ref)
    total = (scales[0] + scales[1]) + scales[2]

    loads[0].wait()
    extra = rows_ref[:, width:]
    pick = ((iota((8, EXTRA), 1) == 3)).astype(F32).astype(BF16)
    live = lax.dot_general(pick, extra, NT, preferred_element_type=F32)
    bias_ref[...] = jnp.where(live > 0.5, 0.0, -1e30)

    spots = extra.astype(F32)
    lane = iota((slots, 3 * GRID), 1)
    wanted = jnp.where(
        lane < GRID,
        spots[:, 0:1],
        jnp.where(lane < 2 * GRID, spots[:, 1:2], spots[:, 2:3]),
    )
    chosen = (wanted == (lane % GRID).astype(F32)).astype(F32).astype(BF16)
    chosen = jnp.concatenate([chosen, chosen, chosen], axis=1)
    loads[1].wait()
    hidden_ref[...] = dot(chosen, table_ref[...]) + rows_ref[:, :width].astype(F32)

    chunk = 32

    def normalise(i, carry):
        rows = pl.ds(pl.multiple_of(i * chunk, chunk), chunk)
        hidden = hidden_ref[rows, :]
        centred = hidden - jnp.mean(hidden, axis=1, keepdims=True)
        spread = jnp.mean(centred * centred, axis=1, keepdims=True)
        normal = centred * lax.rsqrt(spread + 1e-06)
        for b in range(branches):
            normed_ref[b, rows, :] = (
                normal * (1.0 + modulation_ref[b, 1:2, :]) + modulation_ref[b, 0:1, :]
            ).astype(BF16)
        return carry

    lax.fori_loop(0, slots // chunk, normalise, 0, unroll=2)
    stores[0].start()
    stores[2].start()

    if share % 16 == 0:
        for s in range(senders):
            source = pl.ds(pl.multiple_of(s * capacity + first, 16), share)
            target = slice(s * share, (s + 1) * share)
            acc_ref[target, :] = hidden_ref[source, :] * total
            for b in range(branches):
                normed_q_ref[b, target, :] = normed_ref[b, source, :]
    else:
        row = iota((queries, slots), 0)
        wanted_slot = (row // share) * capacity + first + row % share
        chooser = (wanted_slot == iota((queries, slots), 1)).astype(F32)
        picked = jnp.dot(
            chooser, hidden_ref[...], preferred_element_type=F32, precision=lax.Precision.HIGHEST
        )
        acc_ref[...] = picked * total
        for b in range(branches):
            normed_q_ref[b] = dot(chooser.astype(BF16), normed_ref[b]).astype(BF16)
    stores[1].start()

    bias = bias_ref[0:1, :]
    tile = min(256, group)
    for load in loads[2:]:
        load.wait()

    def branch(b, carry):
        for start in range(0, group, tile):
            features = slice(start, start + tile)
            att_ref[:, features] = attend_tile(
                normed_ref[b],
                normed_q_ref[b],
                w_ref[0, features, :],
                w_ref[1, features, :],
                w_ref[2, features, :],
                gain_ref[features, :],
                bias,
                head_size,
            )
        acc_ref[...] += dot(att_ref[...], w_out_ref[...]) * (
            pick_scale(b, scales) * modulation_ref[b, 2:3, :]
        )
        return carry

    lax.fori_loop(0, branches, branch, 0)
    stores[3].start()
    for store in stores:
        store.wait()


def other_kernel(
    head_size,
    swapped,
    normed_hbm,
    normed_q_hbm,
    bias_hbm,
    w_hbm,
    gain_hbm,
    att_hbm,
    normed_ref,
    normed_q_ref,
    bias_ref,
    w_ref,
    gain_ref,
    att_ref,
    in_sems,
    normed_sems,
    normed_q_sems,
    out_sems,
):
    branches, tile = att_ref.shape[0], att_ref.shape[2]
    small = [
        pltpu.make_async_copy(source, target, in_sems.at[n])
        for n, (source, target) in enumerate(
            ((w_hbm, w_ref), (bias_hbm, bias_ref), (gain_hbm, gain_ref))
        )
    ]

    def load(b):
        return (
            pltpu.make_async_copy(normed_q_hbm.at[b], normed_q_ref.at[b], normed_q_sems.at[b]),
            pltpu.make_async_copy(normed_hbm.at[b], normed_ref.at[b], normed_sems.at[b]),
        )

    def store(b):
        return pltpu.make_async_copy(att_ref.at[b], att_hbm.at[b], out_sems.at[b])

    for copy in small:
        copy.start()
    for b in range(branches):
        for copy in load(b):
            copy.start()
    core = lax.axis_index("cfg")
    core = 1 - core if swapped else core
    features = pl.ds(pl.multiple_of(core * tile, tile), tile)
    for copy in small:
        copy.wait()
    bias = bias_ref[0:1, :]
    gains = gain_ref[features, :]

    def branch(b, carry):
        for copy in load(b):
            copy.wait()
        att_ref[b] = attend_tile(
            normed_ref[b], normed_q_ref[b], w_ref[0], w_ref[1], w_ref[2], gains, bias, head_size
        )
        store(b).start()
        return carry

    lax.fori_loop(0, branches, branch, 0)
    for b in range(branches):
        store(b).wait()


def finish_kernel(out_parts, count, guidance_ref, modulation_ref, acc_hbm, *refs):
    arrays = (len(refs) - 2) // 2
    sources = refs[:arrays] + (acc_hbm,)
    out_ref, held, sems = refs[arrays], refs[arrays + 1 : -1], refs[-1]
    loads = [
        pltpu.make_async_copy(source, target, sems.at[n])
        for n, (source, target) in enumerate(zip(sources, held))
    ]
    for load in loads:
        load.start()
    scales = branch_scales(guidance_ref)
    tile = held[0].shape[2]
    core = lax.axis_index("cfg")
    rows = [
        pl.ds(pl.multiple_of(core * tile, tile), tile),
        pl.ds(pl.multiple_of((1 - core) * tile, tile), tile),
    ]
    for load in loads:
        load.wait()
    total = held[-1][...]
    for b in range(modulation_ref.shape[0]):
        part = None
        for n in range(count):
            term = dot(held[n][b], held[count + n // 2][rows[n % 2], :])
            part = term if part is None else part + term
        total = total + part * (scales[b] * modulation_ref[b, 2:3, :])
    if out_parts is None:
        out_ref[...] = total.astype(BF16)
    else:
        senders, heads, share, columns = out_parts
        for h in range(heads):
            piece = total[:, h * columns : (h + 1) * columns].astype(BF16)
            out_ref[:, h] = piece.reshape(senders, share, columns)


def return_kernel(placed_ref, rows_hbm, out_ref, rows_ref, sem):
    load = pltpu.make_async_copy(rows_hbm, rows_ref, sem)
    load.start()
    voxels = placed_ref.shape[1]
    column = jnp.broadcast_to(placed_ref[...], (128, voxels)).T
    column = column.astype(jnp.int32)
    lane = iota((voxels, 128), 1)
    placing = jnp.concatenate(
        [(column == lane + start).astype(F32).astype(BF16) for start in range(0, SLOTS, 128)], axis=1
    )
    load.wait()
    out_ref[...] = dot(placing, rows_ref[...]).astype(BF16)


def on_device(x_latent, windows, coords, modulation, w_qkv, w_out, qk_gain, guidance):
    voxels, width = x_latent.shape
    group = w_qkv.shape[2]
    head_size = width // HEADS
    branches = modulation.shape[0]
    senders = lax.axis_size(("cfg", "vox"))
    heads = lax.axis_size("head")
    cores = lax.axis_size("cfg")
    capacity = SLOTS // senders
    queries = SLOTS // heads
    share = capacity // heads

    tile = group // cores
    vmem, dma = pltpu.VMEM, pltpu.SemaphoreType.DMA
    outgoing, placed = pl.pallas_call(
        functools.partial(place_kernel, senders, capacity),
        out_shape=(
            jax.ShapeDtypeStruct((SLOTS, width + EXTRA), BF16),
            jax.ShapeDtypeStruct((1, voxels), F32),
        ),
        in_specs=[HBM] * 3,
        out_specs=(VMEM, VMEM),
        scratch_shapes=[
            vmem((voxels, width), BF16),
            vmem(windows.shape, jnp.int32),
            vmem(coords.shape, jnp.int32),
            dma((3,)),
        ],
        compiler_params=params(64),
        name="place",
    )(windows, coords, x_latent)
    arrived = lax.all_to_all(
        outgoing.reshape(senders, capacity, width + EXTRA),
        ("cfg", "vox"),
        split_axis=0,
        concat_axis=0,
        tiled=True,
    ).reshape(SLOTS, width + EXTRA)

    w_qkv, w_out_sent, qk_gain, outgoing_done = lax.optimization_barrier(
        (w_qkv, w_out, qk_gain, outgoing)
    )
    del outgoing_done
    start = lax.axis_index("cfg") * tile
    half = jnp.transpose(lax.dynamic_slice_in_dim(w_qkv, start, tile, 2), (1, 2, 0))
    swap = [(c, (c + 1) % cores) for c in range(cores)]
    turns = [[(h, (h + d) % heads) for h in range(heads)] for d in range(1, heads)]
    count = group // senders
    piece = lax.dynamic_slice_in_dim(w_out_sent, lax.axis_index(("cfg", "vox")) * count, count, 0)
    first = [(lax.ppermute(qk_gain, "head", t), lax.ppermute(piece, "head", t)) for t in turns]
    half, first = lax.optimization_barrier((half, first))
    gain_columns = [gain.T for gain, _ in first]
    fetched = [lax.ppermute(half, "head", turn) for turn in turns]
    own_gain = qk_gain.T
    table = position_parts(width)
    pieces = [p for _, p in first]
    arrived, own_gain, table, gain_columns, pieces = lax.optimization_barrier(
        (arrived, own_gain, table, gain_columns, pieces)
    )
    outs = [lax.all_gather(p, ("cfg", "vox"), axis=0, tiled=True) for p in pieces]

    normed, normed_q, acc, bias = pl.pallas_call(
        functools.partial(own_kernel, senders, head_size),
        out_shape=(
            jax.ShapeDtypeStruct((branches, SLOTS, width), BF16),
            jax.ShapeDtypeStruct((branches, queries, width), BF16),
            jax.ShapeDtypeStruct((queries, width), F32),
            jax.ShapeDtypeStruct((8, SLOTS), F32),
        ),
        in_specs=[SMEM, VMEM] + [HBM] * 5,
        out_specs=(HBM,) * 4,
        scratch_shapes=[
            vmem((SLOTS, width + EXTRA), BF16),
            vmem(table.shape, BF16),
            vmem((3, group, width), BF16),
            vmem((group, 2), F32),
            vmem((group, width), BF16),
            vmem((branches, SLOTS, width), BF16),
            vmem((branches, queries, width), BF16),
            vmem((queries, width), F32),
            vmem((8, SLOTS), F32),
            vmem((SLOTS, width), F32),
            vmem((queries, group), BF16),
            dma((5,)),
            dma((4,)),
        ],
        compiler_params=params(64),
        cost_estimate=LITTLE,
        name="own_heads",
    )(
        guidance,
        modulation,
        arrived,
        table,
        jnp.transpose(w_qkv, (1, 2, 0)),
        own_gain,
        w_out,
    )

    def attend(weights, gain, swapped):
        return pl.pallas_call(
            functools.partial(other_kernel, head_size, swapped),
            out_shape=jax.ShapeDtypeStruct((branches, queries, tile), BF16),
            in_specs=[HBM] * 5,
            out_specs=HBM,
            scratch_shapes=[
                vmem((branches, SLOTS, width), BF16),
                vmem((branches, queries, width), BF16),
                vmem((8, SLOTS), F32),
                vmem((3, tile, width), BF16),
                vmem((group, 2), F32),
                vmem((branches, queries, tile), BF16),
                dma((3,)),
                dma((branches,)),
                dma((branches,)),
                dma((branches,)),
            ],
            compiler_params=params(64),
            cost_estimate=LITTLE,
            name="other_heads",
        )(normed, normed_q, bias, weights, gain)

    attended = []
    ahead = bias
    for weights, gain in zip(fetched, gain_columns):
        weights, ahead = lax.optimization_barrier((weights, ahead))
        swapped = lax.ppermute(weights, "cfg", swap)
        attended.append(attend(weights, gain, False))
        ahead = attend(swapped, gain, True)
        attended.append(ahead)

    parts = None
    shape = jax.ShapeDtypeStruct((queries, width), BF16)
    if share % 16 == 0:
        parts = (senders, heads, share, width // heads)
        shape = jax.ShapeDtypeStruct(parts, BF16)
    count = len(attended)
    acc = pl.pallas_call(
        functools.partial(finish_kernel, parts, count),
        out_shape=shape,
        in_specs=[SMEM, VMEM] + [HBM] * (1 + count + len(outs)),
        out_specs=VMEM,
        scratch_shapes=[vmem((branches, queries, tile), BF16)] * count
        + [vmem((group, width), BF16)] * len(outs)
        + [vmem((queries, width), F32), dma((count + len(outs) + 1,))],
        compiler_params=params(64),
        name="finish",
    )(guidance, modulation, acc, *attended, *outs)
    if share % 16 != 0:
        acc = acc.reshape(senders, share, heads, width // heads).transpose(0, 2, 1, 3)
    back = lax.all_to_all(
        acc.reshape(senders * heads, share, width // heads),
        ("cfg", "vox", "head"),
        split_axis=0,
        concat_axis=0,
        tiled=True,
    )
    return pl.pallas_call(
        return_kernel,
        out_shape=jax.ShapeDtypeStruct((voxels, width // heads), BF16),
        in_specs=[VMEM, HBM],
        out_specs=VMEM,
        scratch_shapes=[vmem((SLOTS, width // heads), BF16), dma(())],
        compiler_params=params(64),
        name="return_rows",
    )(placed, back.reshape(SLOTS, width // heads))


def solution(mesh):
    placed = (
        P(("cfg", "vox"), None),
        P(("cfg", "vox")),
        P(None, ("cfg", "vox")),
        P(),
        P(None, None, "head"),
        P("head", None),
        P(None, "head"),
        P(),
    )
    return jax.shard_map(
        on_device, mesh=mesh, in_specs=placed, out_specs=P(("cfg", "vox"), "head"), check_vma=False
    )
```

```python
import functools

import jax
import jax.numpy as jnp
from jax import lax
from jax.experimental import pallas as pl
from jax.experimental.pallas import tpu as pltpu
from jax.sharding import PartitionSpec as P

HEADS = 16
SLOTS = 512
GRID = 64
EXTRA = 128
BF16 = jnp.bfloat16
F32 = jnp.float32
VMEM = pl.BlockSpec(memory_space=pltpu.VMEM)
SMEM = pl.BlockSpec(memory_space=pltpu.SMEM)
HBM = pl.BlockSpec(memory_space=pltpu.HBM)
NT = (((1,), (1,)), ((), ()))


def params(megabytes):
    return pltpu.CompilerParams(vmem_limit_bytes=megabytes * 1024 * 1024)


def iota(shape, dim):
    return lax.broadcasted_iota(jnp.int32, shape, dim)


def dot(a, b):
    return jnp.dot(a, b, preferred_element_type=F32)


def position_parts(model_width):
    freq_count = model_width // 3 // 2
    frequency = 1.0 / 10000.0 ** (jnp.arange(freq_count, dtype=F32) / freq_count)
    angles = jnp.arange(GRID, dtype=F32)[:, None] * frequency[None, :]
    block = jnp.concatenate([jnp.sin(angles), jnp.cos(angles)], axis=1)
    width = 2 * freq_count
    rows = [
        jnp.pad(block, ((0, 0), (c * width, model_width - (c + 1) * width))) for c in range(3)
    ]
    table = jnp.concatenate(rows, axis=0)
    top = lax.reduce_precision(table, 8, 7)
    rest = table - top
    middle = lax.reduce_precision(rest, 8, 7)
    low = rest - middle
    return jnp.concatenate([top, middle, low], axis=0).astype(BF16)


def place_kernel(
    senders,
    capacity,
    windows_hbm,
    coords_hbm,
    x_hbm,
    out_ref,
    placed_ref,
    x_ref,
    windows_ref,
    coords_ref,
    sems,
):
    loads = [
        pltpu.make_async_copy(source, target, sems.at[n])
        for n, (source, target) in enumerate(
            ((windows_hbm, windows_ref), (coords_hbm, coords_ref), (x_hbm, x_ref))
        )
    ]
    for load in loads:
        load.start()
    voxels, width = x_hbm.shape
    loads[0].wait()
    windows = windows_ref[...].reshape(1, voxels)
    member = windows == iota((senders, voxels), 0)
    earlier = (iota((voxels, voxels), 0) < iota((voxels, voxels), 1)).astype(F32).astype(BF16)
    member_f = member.astype(F32)
    before = dot(member_f.astype(BF16), earlier)
    rank = jnp.sum(before * member_f, axis=0, keepdims=True).astype(jnp.int32)
    placed = windows * capacity + rank
    placed_ref[...] = placed.astype(F32)
    placing = (placed == iota((SLOTS, voxels), 0)).astype(F32).astype(BF16)
    loads[1].wait()
    row = iota((EXTRA, voxels), 0)
    extra = jnp.where(row == 3, 1.0, 0.0).astype(F32)
    for c in range(3):
        extra = jnp.where(row == c, coords_ref[c : c + 1, :].astype(F32), extra)
    out_ref[:, width:] = lax.dot_general(
        placing, extra.astype(BF16), NT, preferred_element_type=F32
    ).astype(BF16)
    loads[2].wait()
    out_ref[:, :width] = dot(placing, x_ref[...]).astype(BF16)


def column_norm(rows, gain, head_size):
    blocks = []
    for start in range(0, rows.shape[0], head_size):
        block = rows[start : start + head_size]
        mean = jnp.sum(block * block, axis=0, keepdims=True) * (1.0 / head_size)
        blocks.append(block * lax.rsqrt(mean + 1e-06) * gain[start : start + head_size])
    return jnp.concatenate(blocks, axis=0).astype(BF16)


def project_keys(normed, w_key, gain, head_size):
    key = lax.dot_general(w_key, normed, NT, preferred_element_type=F32)
    return column_norm(key, gain, head_size)


def project_values(normed, w_value):
    return lax.dot_general(normed, w_value, NT, preferred_element_type=F32).astype(BF16)


def attend_tile(normed_q, w_query, gain, key, value, bias, head_size):
    queries, tile = normed_q.shape[0], w_query.shape[0]
    query = lax.dot_general(w_query, normed_q, NT, preferred_element_type=F32)
    query = column_norm(query, gain, head_size)
    query = (query.astype(F32) * (1.0 / head_size**0.5)).T
    lane_head = iota((queries, tile), 1) // head_size
    count = tile // head_size

    def score(head):
        return dot(jnp.where(lane_head == head, query, 0.0).astype(BF16), key)

    scores = score(0)
    mixed = jnp.zeros((queries, tile), F32)
    step = min(32, queries)
    for head in range(count):
        following = score(head + 1) if head + 1 < count else None
        pieces = []
        for r in range(0, queries, step):
            piece = scores[r : r + step] + bias
            weights = jnp.exp(piece - jnp.max(piece, axis=1, keepdims=True))
            total = jnp.sum(weights, axis=1, keepdims=True)
            pieces.append((weights * (1.0 / total)).astype(BF16))
        attend = jnp.concatenate(pieces, axis=0)
        mixed = jnp.where(lane_head == head, dot(attend, value), mixed)
        scores = following
    return mixed.astype(BF16)


def branch_scales(guidance_ref):
    g0, g1 = guidance_ref[0], guidance_ref[1]
    return 1.0 - g0, g0 - g1, g1


def pick_scale(b, scales):
    return jnp.where(b == 0, scales[0], jnp.where(b == 1, scales[1], scales[2]))


def copies(pairs, sems):
    return [
        pltpu.make_async_copy(source, target, sems.at[n])
        for n, (source, target) in enumerate(pairs)
    ]


def first_kernel(
    senders,
    head_size,
    guidance_ref,
    modulation_ref,
    rows_hbm,
    table_hbm,
    w_hbm,
    gain_hbm,
    w_out_hbm,
    normed_q_hbm,
    keys_hbm,
    values_hbm,
    residual_hbm,
    bias_hbm,
    sent_hbm,
    rows_ref,
    table_ref,
    w_ref,
    gain_ref,
    w_out_ref,
    normed_ref,
    normed_q_ref,
    keys_ref,
    values_ref,
    residual_ref,
    bias_ref,
    sent_ref,
    hidden_ref,
    att_ref,
    sum_ref,
    in_sems,
    out_sems,
    key_sems,
    value_sems,
):
    loads = copies(
        (
            (rows_hbm, rows_ref),
            (table_hbm, table_ref),
            (w_hbm, w_ref),
            (gain_hbm, gain_ref),
            (w_out_hbm, w_out_ref),
        ),
        in_sems,
    )
    stores = copies(
        (
            (normed_q_ref, normed_q_hbm),
            (bias_ref, bias_hbm),
            (residual_ref, residual_hbm),
            (sent_ref, sent_hbm),
        ),
        out_sems,
    )
    for load in loads:
        load.start()
    branches, slots, width = normed_ref.shape
    heads, _, queries, _ = normed_q_ref.shape
    group = att_ref.shape[1]
    capacity = slots // senders
    share = queries // senders
    me = lax.axis_index("head")
    scales = branch_scales(guidance_ref)
    total = (scales[0] + scales[1]) + scales[2]

    loads[0].wait()
    extra = rows_ref[:, width:]
    pick = ((iota((8, EXTRA), 1) == 3)).astype(F32).astype(BF16)
    live = lax.dot_general(pick, extra, NT, preferred_element_type=F32)
    bias_ref[...] = jnp.where(live > 0.5, 0.0, -1e30)
    stores[1].start()

    spots = extra.astype(F32)
    lane = iota((slots, 3 * GRID), 1)
    wanted = jnp.where(
        lane < GRID,
        spots[:, 0:1],
        jnp.where(lane < 2 * GRID, spots[:, 1:2], spots[:, 2:3]),
    )
    chosen = (wanted == (lane % GRID).astype(F32)).astype(F32).astype(BF16)
    chosen = jnp.concatenate([chosen, chosen, chosen], axis=1)
    loads[1].wait()
    hidden_ref[...] = dot(chosen, table_ref[...]) + rows_ref[:, :width].astype(F32)

    chunk = 32

    def normalise(i, carry):
        rows = pl.ds(pl.multiple_of(i * chunk, chunk), chunk)
        hidden = hidden_ref[rows, :]
        centred = hidden - jnp.mean(hidden, axis=1, keepdims=True)
        spread = jnp.mean(centred * centred, axis=1, keepdims=True)
        normal = centred * lax.rsqrt(spread + 1e-06)
        for b in range(branches):
            normed_ref[b, rows, :] = (
                normal * (1.0 + modulation_ref[b, 1:2, :]) + modulation_ref[b, 0:1, :]
            ).astype(BF16)
        return carry

    lax.fori_loop(0, slots // chunk, normalise, 0, unroll=2)

    for d in range(heads):
        first = lax.rem(me + d + 1, heads) * share
        if share % 16 == 0:
            for s in range(senders):
                source = pl.ds(pl.multiple_of(s * capacity + first, 16), share)
                target = slice(s * share, (s + 1) * share)
                if d == heads - 1:
                    residual_ref[target, :] = hidden_ref[source, :] * total
                for b in range(branches):
                    normed_q_ref[d, b, target, :] = normed_ref[b, source, :]
        else:
            row = iota((queries, slots), 0)
            wanted_slot = (row // share) * capacity + first + row % share
            chooser = (wanted_slot == iota((queries, slots), 1)).astype(F32)
            if d == heads - 1:
                picked = jnp.dot(
                    chooser,
                    hidden_ref[...],
                    preferred_element_type=F32,
                    precision=lax.Precision.HIGHEST,
                )
                residual_ref[...] = picked * total
            for b in range(branches):
                normed_q_ref[d, b] = dot(chooser.astype(BF16), normed_ref[b]).astype(BF16)
    stores[0].start()
    stores[2].start()

    bias = bias_ref[0:1, :]
    tile = min(256, group)
    for load in loads[2:]:
        load.wait()
    sum_ref[...] = jnp.zeros_like(sum_ref)

    def store(b):
        return (
            pltpu.make_async_copy(keys_ref.at[b], keys_hbm.at[b], key_sems.at[b]),
            pltpu.make_async_copy(values_ref.at[b], values_hbm.at[b], value_sems.at[b]),
        )

    def branch(b, carry):
        for start in range(0, group, tile):
            features = slice(start, start + tile)
            gains = gain_ref[features, :]
            key = project_keys(normed_ref[b], w_ref[1, features, :], gains[:, 1:2], head_size)
            value = project_values(normed_ref[b], w_ref[2, features, :])
            keys_ref[b, features, :] = key
            values_ref[b, :, features] = value
            att_ref[:, features] = attend_tile(
                normed_q_ref[0, b],
                w_ref[0, features, :],
                gains[:, 0:1],
                key,
                value,
                bias,
                head_size,
            )
        for copy in store(b):
            copy.start()
        sum_ref[...] += dot(att_ref[...], w_out_ref[...]) * (
            pick_scale(b, scales) * modulation_ref[b, 2:3, :]
        )
        return carry

    lax.fori_loop(0, branches, branch, 0)
    sent_ref[...] = sum_ref[...].astype(BF16)
    stores[3].start()
    for copy in stores:
        copy.wait()
    for b in range(branches):
        for copy in store(b):
            copy.wait()


def query_kernel(
    head_size,
    distance,
    guidance_ref,
    modulation_ref,
    normed_q_hbm,
    keys_hbm,
    values_hbm,
    bias_hbm,
    w_hbm,
    gain_hbm,
    w_out_hbm,
    out_hbm,
    normed_q_ref,
    keys_ref,
    values_ref,
    bias_ref,
    w_ref,
    gain_ref,
    w_out_ref,
    sum_ref,
    out_ref,
    att_ref,
    in_sems,
    query_sems,
    key_sems,
    value_sems,
    out_sem,
):
    branches, _, slots = keys_ref.shape
    group = att_ref.shape[1]
    loads = copies(
        (
            (w_hbm.at[0], w_ref),
            (gain_hbm, gain_ref),
            (bias_hbm, bias_ref),
            (w_out_hbm, w_out_ref),
        ),
        in_sems,
    )

    def load(b):
        return (
            pltpu.make_async_copy(
                normed_q_hbm.at[distance, b], normed_q_ref.at[b], query_sems.at[b]
            ),
            pltpu.make_async_copy(keys_hbm.at[b], keys_ref.at[b], key_sems.at[b]),
            pltpu.make_async_copy(values_hbm.at[b], values_ref.at[b], value_sems.at[b]),
        )

    loads[0].start()
    for copy in load(0):
        copy.start()
    for copy in loads[1:]:
        copy.start()
    for b in range(1, branches):
        for copy in load(b):
            copy.start()
    scales = branch_scales(guidance_ref)
    tile = min(256, group)
    sum_ref[...] = jnp.zeros_like(sum_ref)
    for copy in loads:
        copy.wait()
    bias = bias_ref[0:1, :]

    def branch(b, carry):
        for copy in load(b):
            copy.wait()
        for start in range(0, group, tile):
            features = slice(start, start + tile)
            att_ref[:, features] = attend_tile(
                normed_q_ref[b],
                w_ref[features, :],
                gain_ref[features, 0:1],
                keys_ref[b, features, :],
                values_ref[b, :, features],
                bias,
                head_size,
            )
        sum_ref[...] += dot(att_ref[...], w_out_ref[...]) * (
            pick_scale(b, scales) * modulation_ref[b, 2:3, :]
        )
        return carry

    lax.fori_loop(0, branches, branch, 0)
    out_ref[...] = sum_ref[...].astype(out_ref.dtype)
    store = pltpu.make_async_copy(out_ref, out_hbm, out_sem)
    store.start()
    store.wait()


def finish_kernel(out_parts, *refs):
    arrays = (len(refs) - 2) // 2
    out_ref, held, sems = refs[arrays], refs[arrays + 1 : -1], refs[-1]
    loads = copies(zip(refs[:arrays], held), sems)
    for load in loads:
        load.start()
    for load in loads:
        load.wait()
    step = 32 if out_parts is not None else held[0].shape[0]
    for r in range(0, held[0].shape[0], step):
        total = held[0][r : r + step, :]
        for term in held[1:]:
            total = total + term[r : r + step, :].astype(F32)
        if out_parts is None:
            out_ref[r : r + step, :] = total.astype(BF16)
        else:
            senders, heads, share, columns = out_parts
            for h in range(heads):
                piece = total[:, h * columns : (h + 1) * columns].astype(BF16)
                first = r // share
                out_ref[first : first + step // share, h] = piece.reshape(
                    step // share, share, columns
                )


def return_kernel(placed_ref, rows_hbm, out_ref, rows_ref, sem):
    load = pltpu.make_async_copy(rows_hbm, rows_ref, sem)
    load.start()
    voxels = placed_ref.shape[1]
    column = jnp.broadcast_to(placed_ref[...], (128, voxels)).T
    column = column.astype(jnp.int32)
    lane = iota((voxels, 128), 1)
    placing = jnp.concatenate(
        [(column == lane + start).astype(F32).astype(BF16) for start in range(0, SLOTS, 128)], axis=1
    )
    load.wait()
    out_ref[...] = dot(placing, rows_ref[...]).astype(BF16)


def on_device(x_latent, windows, coords, modulation, w_qkv, w_out, qk_gain, guidance):
    voxels, width = x_latent.shape
    group = w_qkv.shape[2]
    head_size = width // HEADS
    branches = modulation.shape[0]
    senders = lax.axis_size(("cfg", "vox"))
    heads = lax.axis_size("head")
    capacity = SLOTS // senders
    queries = SLOTS // heads
    share = capacity // heads

    vmem, dma = pltpu.VMEM, pltpu.SemaphoreType.DMA
    outgoing, placed = pl.pallas_call(
        functools.partial(place_kernel, senders, capacity),
        out_shape=(
            jax.ShapeDtypeStruct((SLOTS, width + EXTRA), BF16),
            jax.ShapeDtypeStruct((1, voxels), F32),
        ),
        in_specs=[HBM] * 3,
        out_specs=(VMEM, VMEM),
        scratch_shapes=[
            vmem((voxels, width), BF16),
            vmem(windows.shape, jnp.int32),
            vmem(coords.shape, jnp.int32),
            dma((3,)),
        ],
        compiler_params=params(64),
        name="place",
    )(windows, coords, x_latent)
    arrived = lax.all_to_all(
        outgoing.reshape(senders, capacity, width + EXTRA),
        ("cfg", "vox"),
        split_axis=0,
        concat_axis=0,
        tiled=True,
    ).reshape(SLOTS, width + EXTRA)

    own_gain = qk_gain.T
    table = position_parts(width)
    flat = jnp.transpose(w_qkv, (1, 2, 0))
    arrived, own_gain, table, flat = lax.optimization_barrier((arrived, own_gain, table, flat))

    shapes = dict(
        normed_q=((heads, branches, queries, width), BF16),
        keys=((branches, group, SLOTS), BF16),
        values=((branches, SLOTS, group), BF16),
        residual=((queries, width), F32),
        bias=((8, SLOTS), F32),
        sent=((queries, width), BF16),
    )
    made = pl.pallas_call(
        functools.partial(first_kernel, senders, head_size),
        out_shape=tuple(jax.ShapeDtypeStruct(*shape) for shape in shapes.values()),
        in_specs=[SMEM, VMEM] + [HBM] * 5,
        out_specs=(HBM,) * 6,
        scratch_shapes=[
            vmem((SLOTS, width + EXTRA), BF16),
            vmem(table.shape, BF16),
            vmem((3, group, width), BF16),
            vmem((group, 2), F32),
            vmem((group, width), BF16),
            vmem((branches, SLOTS, width), BF16),
        ]
        + [vmem(*shape) for shape in shapes.values()]
        + [
            vmem((SLOTS, width), F32),
            vmem((queries, group), BF16),
            vmem((queries, width), F32),
            dma((5,)),
            dma((4,)),
            dma((branches,)),
            dma((branches,)),
        ],
        compiler_params=params(64),
        name="first_queries",
    )(guidance, modulation, arrived, table, flat, own_gain, w_out)
    normed_q, keys, values, residual, bias, partial = made

    def attend(distance, dtype):
        return pl.pallas_call(
            functools.partial(query_kernel, head_size, distance),
            out_shape=jax.ShapeDtypeStruct((queries, width), dtype),
            in_specs=[SMEM, VMEM] + [HBM] * 7,
            out_specs=HBM,
            scratch_shapes=[
                vmem((branches, queries, width), BF16),
                vmem(*shapes["keys"]),
                vmem(*shapes["values"]),
                vmem(*shapes["bias"]),
                vmem((group, width), BF16),
                vmem((group, 2), F32),
                vmem((group, width), BF16),
                vmem((queries, width), F32),
                vmem((queries, width), dtype),
                vmem((queries, group), BF16),
                dma((4,)),
                dma((branches,)),
                dma((branches,)),
                dma((branches,)),
                dma(()),
            ],
            compiler_params=params(64),
            name="more_queries",
        )(guidance, modulation, normed_q, keys, values, bias, flat, own_gain, w_out)

    terms = []
    for distance in range(1, heads):
        turn = [(h, (h + distance) % heads) for h in range(heads)]
        terms.append(lax.ppermute(partial, "head", turn))
        last = distance == heads - 1
        partial = attend(distance, F32 if last else BF16)
    terms = [residual, partial] + terms

    parts = None
    shape = jax.ShapeDtypeStruct((queries, width), BF16)
    if share % 16 == 0:
        parts = (senders, heads, share, width // heads)
        shape = jax.ShapeDtypeStruct(parts, BF16)
    acc = pl.pallas_call(
        functools.partial(finish_kernel, parts),
        out_shape=shape,
        in_specs=[HBM] * len(terms),
        out_specs=VMEM,
        scratch_shapes=[vmem((queries, width), term.dtype) for term in terms] + [dma((len(terms),))],
        compiler_params=params(64),
        name="finish",
    )(*terms)
    if share % 16 != 0:
        acc = acc.reshape(senders, share, heads, width // heads).transpose(0, 2, 1, 3)
    back = lax.all_to_all(
        acc.reshape(senders * heads, share, width // heads),
        ("cfg", "vox", "head"),
        split_axis=0,
        concat_axis=0,
        tiled=True,
    )
    return pl.pallas_call(
        return_kernel,
        out_shape=jax.ShapeDtypeStruct((voxels, width // heads), BF16),
        in_specs=[VMEM, HBM],
        out_specs=VMEM,
        scratch_shapes=[vmem((SLOTS, width // heads), BF16), dma(())],
        compiler_params=params(64),
        name="return_rows",
    )(placed, back.reshape(SLOTS, width // heads))


def solution(mesh):
    placed = (
        P(("cfg", "vox"), None),
        P(("cfg", "vox")),
        P(None, ("cfg", "vox")),
        P(),
        P(None, None, "head"),
        P("head", None),
        P(None, "head"),
        P(),
    )
    return jax.shard_map(
        on_device, mesh=mesh, in_specs=placed, out_specs=P(("cfg", "vox"), "head"), check_vma=False
    )
```

```python
import functools

import jax
import jax.numpy as jnp
from jax import lax
from jax.experimental import pallas as pl
from jax.experimental.pallas import tpu as pltpu
from jax.sharding import PartitionSpec as P

HEADS = 16
SLOTS = 512
GRID = 64
EXTRA = 128
BF16 = jnp.bfloat16
F32 = jnp.float32
VMEM = pl.BlockSpec(memory_space=pltpu.VMEM)
SMEM = pl.BlockSpec(memory_space=pltpu.SMEM)
HBM = pl.BlockSpec(memory_space=pltpu.HBM)
SENT_SCALE = 2.0**-7
NT = (((1,), (1,)), ((), ()))


def params(megabytes):
    return pltpu.CompilerParams(vmem_limit_bytes=megabytes * 1024 * 1024)


def iota(shape, dim):
    return lax.broadcasted_iota(jnp.int32, shape, dim)


def dot(a, b):
    return jnp.dot(a, b, preferred_element_type=F32)


def position_parts(model_width):
    freq_count = model_width // 3 // 2
    frequency = 1.0 / 10000.0 ** (jnp.arange(freq_count, dtype=F32) / freq_count)
    angles = jnp.arange(GRID, dtype=F32)[:, None] * frequency[None, :]
    block = jnp.concatenate([jnp.sin(angles), jnp.cos(angles)], axis=1)
    width = 2 * freq_count
    rows = [
        jnp.pad(block, ((0, 0), (c * width, model_width - (c + 1) * width))) for c in range(3)
    ]
    table = jnp.concatenate(rows, axis=0)
    top = lax.reduce_precision(table, 8, 7)
    rest = table - top
    middle = lax.reduce_precision(rest, 8, 7)
    low = rest - middle
    return jnp.concatenate([top, middle, low], axis=0).astype(BF16)


def place_kernel(
    senders,
    capacity,
    windows_hbm,
    coords_hbm,
    x_hbm,
    out_ref,
    placed_ref,
    x_ref,
    windows_ref,
    coords_ref,
    sems,
):
    loads = [
        pltpu.make_async_copy(source, target, sems.at[n])
        for n, (source, target) in enumerate(
            ((windows_hbm, windows_ref), (coords_hbm, coords_ref), (x_hbm, x_ref))
        )
    ]
    for load in loads:
        load.start()
    voxels, width = x_hbm.shape
    loads[0].wait()
    windows = windows_ref[...].reshape(1, voxels)
    member = windows == iota((senders, voxels), 0)
    earlier = (iota((voxels, voxels), 0) < iota((voxels, voxels), 1)).astype(F32).astype(BF16)
    member_f = member.astype(F32)
    before = dot(member_f.astype(BF16), earlier)
    rank = jnp.sum(before * member_f, axis=0, keepdims=True).astype(jnp.int32)
    placed = windows * capacity + rank
    placed_ref[...] = placed.astype(F32)
    placing = (placed == iota((SLOTS, voxels), 0)).astype(F32).astype(BF16)
    loads[1].wait()
    row = iota((EXTRA, voxels), 0)
    extra = jnp.where(row == 3, 1.0, 0.0).astype(F32)
    for c in range(3):
        extra = jnp.where(row == c, coords_ref[c : c + 1, :].astype(F32), extra)
    out_ref[:, width:] = lax.dot_general(
        placing, extra.astype(BF16), NT, preferred_element_type=F32
    ).astype(BF16)
    loads[2].wait()
    out_ref[:, :width] = dot(placing, x_ref[...]).astype(BF16)


def column_norm(rows, gain, head_size):
    blocks = []
    for start in range(0, rows.shape[0], head_size):
        block = rows[start : start + head_size]
        mean = jnp.sum(block * block, axis=0, keepdims=True) * (1.0 / head_size)
        blocks.append(block * lax.rsqrt(mean + 1e-06) * gain[start : start + head_size])
    return jnp.concatenate(blocks, axis=0).astype(BF16)


def project_keys(normed, w_key, gain, head_size):
    key = lax.dot_general(w_key, normed, NT, preferred_element_type=F32)
    return column_norm(key, gain, head_size)


def project_values(normed, w_value):
    return lax.dot_general(normed, w_value, NT, preferred_element_type=F32).astype(BF16)


def attend_tile(normed_q, w_query, gain, key, value, bias, head_size):
    queries, tile = normed_q.shape[0], w_query.shape[0]
    query = lax.dot_general(w_query, normed_q, NT, preferred_element_type=F32)
    query = column_norm(query, gain, head_size)
    query = (query.astype(F32) * (1.0 / head_size**0.5)).T
    lane_head = iota((queries, tile), 1) // head_size
    count = tile // head_size

    def score(head):
        return dot(jnp.where(lane_head == head, query, 0.0).astype(BF16), key)

    scores = score(0)
    mixed = jnp.zeros((queries, tile), F32)
    step = min(32, queries)
    for head in range(count):
        following = score(head + 1) if head + 1 < count else None
        pieces = []
        for r in range(0, queries, step):
            piece = scores[r : r + step] + bias
            weights = jnp.exp(piece - jnp.max(piece, axis=1, keepdims=True))
            total = jnp.sum(weights, axis=1, keepdims=True)
            pieces.append((weights * (1.0 / total)).astype(BF16))
        attend = jnp.concatenate(pieces, axis=0)
        mixed = jnp.where(lane_head == head, dot(attend, value), mixed)
        scores = following
    return mixed.astype(BF16)


def branch_scales(guidance_ref):
    g0, g1 = guidance_ref[0], guidance_ref[1]
    return 1.0 - g0, g0 - g1, g1


def pick_scale(b, scales):
    return jnp.where(b == 0, scales[0], jnp.where(b == 1, scales[1], scales[2]))


def copies(pairs, sems):
    return [
        pltpu.make_async_copy(source, target, sems.at[n])
        for n, (source, target) in enumerate(pairs)
    ]


def first_kernel(
    senders,
    head_size,
    guidance_ref,
    modulation_ref,
    rows_hbm,
    table_hbm,
    w_hbm,
    gain_hbm,
    w_out_hbm,
    normed_q_hbm,
    keys_hbm,
    values_hbm,
    residual_hbm,
    bias_hbm,
    sent_hbm,
    rows_ref,
    table_ref,
    w_ref,
    gain_ref,
    w_out_ref,
    normed_ref,
    normed_q_ref,
    keys_ref,
    values_ref,
    residual_ref,
    bias_ref,
    sent_ref,
    hidden_ref,
    att_ref,
    sum_ref,
    in_sems,
    out_sems,
    key_sems,
    value_sems,
):
    loads = copies(
        (
            (rows_hbm, rows_ref),
            (table_hbm, table_ref),
            (w_hbm, w_ref),
            (gain_hbm, gain_ref),
            (w_out_hbm, w_out_ref),
        ),
        in_sems,
    )
    stores = copies(
        (
            (normed_q_ref, normed_q_hbm),
            (bias_ref, bias_hbm),
            (residual_ref, residual_hbm),
            (sent_ref, sent_hbm),
        ),
        out_sems,
    )
    for load in loads:
        load.start()
    branches, slots, width = normed_ref.shape
    heads, _, queries, _ = normed_q_ref.shape
    group = att_ref.shape[1]
    capacity = slots // senders
    share = queries // senders
    me = lax.axis_index("head")
    scales = branch_scales(guidance_ref)
    total = (scales[0] + scales[1]) + scales[2]

    loads[0].wait()
    extra = rows_ref[:, width:]
    pick = ((iota((8, EXTRA), 1) == 3)).astype(F32).astype(BF16)
    live = lax.dot_general(pick, extra, NT, preferred_element_type=F32)
    bias_ref[...] = jnp.where(live > 0.5, 0.0, -1e30)
    stores[1].start()

    spots = extra.astype(F32)
    lane = iota((slots, 3 * GRID), 1)
    wanted = jnp.where(
        lane < GRID,
        spots[:, 0:1],
        jnp.where(lane < 2 * GRID, spots[:, 1:2], spots[:, 2:3]),
    )
    chosen = (wanted == (lane % GRID).astype(F32)).astype(F32).astype(BF16)
    chosen = jnp.concatenate([chosen, chosen, chosen], axis=1)
    loads[1].wait()
    hidden_ref[...] = dot(chosen, table_ref[...]) + rows_ref[:, :width].astype(F32)

    chunk = 32

    def normalise(i, carry):
        rows = pl.ds(pl.multiple_of(i * chunk, chunk), chunk)
        hidden = hidden_ref[rows, :]
        centred = hidden - jnp.mean(hidden, axis=1, keepdims=True)
        spread = jnp.mean(centred * centred, axis=1, keepdims=True)
        normal = centred * lax.rsqrt(spread + 1e-06)
        for b in range(branches):
            normed_ref[b, rows, :] = (
                normal * (1.0 + modulation_ref[b, 1:2, :]) + modulation_ref[b, 0:1, :]
            ).astype(BF16)
        return carry

    lax.fori_loop(0, slots // chunk, normalise, 0, unroll=2)

    for d in range(heads):
        first = lax.rem(me + d + 1, heads) * share
        if share % 16 == 0:
            for s in range(senders):
                source = pl.ds(pl.multiple_of(s * capacity + first, 16), share)
                target = slice(s * share, (s + 1) * share)
                if d == heads - 1:
                    residual_ref[target, :] = hidden_ref[source, :] * total
                for b in range(branches):
                    normed_q_ref[d, b, target, :] = normed_ref[b, source, :]
        else:
            row = iota((queries, slots), 0)
            wanted_slot = (row // share) * capacity + first + row % share
            chooser = (wanted_slot == iota((queries, slots), 1)).astype(F32)
            if d == heads - 1:
                picked = jnp.dot(
                    chooser,
                    hidden_ref[...],
                    preferred_element_type=F32,
                    precision=lax.Precision.HIGHEST,
                )
                residual_ref[...] = picked * total
            for b in range(branches):
                normed_q_ref[d, b] = dot(chooser.astype(BF16), normed_ref[b]).astype(BF16)
    stores[0].start()
    stores[2].start()

    bias = bias_ref[0:1, :]
    tile = min(256, group)
    for load in loads[2:]:
        load.wait()
    sum_ref[...] = jnp.zeros_like(sum_ref)

    def store(b):
        return (
            pltpu.make_async_copy(keys_ref.at[b], keys_hbm.at[b], key_sems.at[b]),
            pltpu.make_async_copy(values_ref.at[b], values_hbm.at[b], value_sems.at[b]),
        )

    def branch(b, carry):
        for start in range(0, group, tile):
            features = slice(start, start + tile)
            gains = gain_ref[features, :]
            key = project_keys(normed_ref[b], w_ref[1, features, :], gains[:, 1:2], head_size)
            value = project_values(normed_ref[b], w_ref[2, features, :])
            keys_ref[b, features, :] = key
            values_ref[b, :, features] = value
            att_ref[:, features] = attend_tile(
                normed_q_ref[0, b],
                w_ref[0, features, :],
                gains[:, 0:1],
                key,
                value,
                bias,
                head_size,
            )
        for copy in store(b):
            copy.start()
        sum_ref[...] += dot(att_ref[...], w_out_ref[...]) * (
            pick_scale(b, scales) * modulation_ref[b, 2:3, :]
        )
        return carry

    lax.fori_loop(0, branches, branch, 0)
    sent_ref[...] = sum_ref[...] * SENT_SCALE
    stores[3].start()
    for copy in stores:
        copy.wait()
    for b in range(branches):
        for copy in store(b):
            copy.wait()


def query_kernel(
    head_size,
    distance,
    last,
    guidance_ref,
    modulation_ref,
    normed_q_hbm,
    keys_hbm,
    values_hbm,
    bias_hbm,
    w_hbm,
    gain_hbm,
    w_out_hbm,
    start_hbm,
    out_hbm,
    normed_q_ref,
    keys_ref,
    values_ref,
    bias_ref,
    w_ref,
    gain_ref,
    w_out_ref,
    sum_ref,
    out_ref,
    att_ref,
    in_sems,
    query_sems,
    key_sems,
    value_sems,
    out_sem,
):
    branches, _, slots = keys_ref.shape
    group = att_ref.shape[1]
    loads = copies(
        (
            (w_hbm.at[0], w_ref),
            (gain_hbm, gain_ref),
            (bias_hbm, bias_ref),
            (w_out_hbm, w_out_ref),
            (start_hbm, sum_ref),
        ),
        in_sems,
    )
    if not last:
        loads = loads[:-1]

    def load(b):
        return (
            pltpu.make_async_copy(
                normed_q_hbm.at[distance, b], normed_q_ref.at[b], query_sems.at[b]
            ),
            pltpu.make_async_copy(keys_hbm.at[b], keys_ref.at[b], key_sems.at[b]),
            pltpu.make_async_copy(values_hbm.at[b], values_ref.at[b], value_sems.at[b]),
        )

    loads[0].start()
    for copy in load(0):
        copy.start()
    for copy in loads[1:]:
        copy.start()
    for b in range(1, branches):
        for copy in load(b):
            copy.start()
    scales = branch_scales(guidance_ref)
    tile = min(256, group)
    if not last:
        sum_ref[...] = jnp.zeros_like(sum_ref)
    for copy in loads:
        copy.wait()
    bias = bias_ref[0:1, :]

    def branch(b, carry):
        for copy in load(b):
            copy.wait()
        for start in range(0, group, tile):
            features = slice(start, start + tile)
            att_ref[:, features] = attend_tile(
                normed_q_ref[b],
                w_ref[features, :],
                gain_ref[features, 0:1],
                keys_ref[b, features, :],
                values_ref[b, :, features],
                bias,
                head_size,
            )
        sum_ref[...] += dot(att_ref[...], w_out_ref[...]) * (
            pick_scale(b, scales) * modulation_ref[b, 2:3, :]
        )
        return carry

    lax.fori_loop(0, branches, branch, 0)
    if last:
        out_ref[...] = sum_ref[...]
    else:
        out_ref[...] = sum_ref[...] * SENT_SCALE
    store = pltpu.make_async_copy(out_ref, out_hbm, out_sem)
    store.start()
    store.wait()


def return_kernel(placed_ref, rows_hbm, out_ref, rows_ref, sem):
    load = pltpu.make_async_copy(rows_hbm, rows_ref, sem)
    load.start()
    voxels = placed_ref.shape[1]
    column = jnp.broadcast_to(placed_ref[...], (128, voxels)).T
    column = column.astype(jnp.int32)
    lane = iota((voxels, 128), 1)
    placing = jnp.concatenate(
        [(column == lane + start).astype(F32).astype(BF16) for start in range(0, SLOTS, 128)], axis=1
    )
    load.wait()
    out_ref[...] = dot(placing, rows_ref[...]).astype(BF16)


def on_device(x_latent, windows, coords, modulation, w_qkv, w_out, qk_gain, guidance):
    voxels, width = x_latent.shape
    group = w_qkv.shape[2]
    head_size = width // HEADS
    branches = modulation.shape[0]
    senders = lax.axis_size(("cfg", "vox"))
    heads = lax.axis_size("head")
    capacity = SLOTS // senders
    queries = SLOTS // heads
    share = capacity // heads

    vmem, dma = pltpu.VMEM, pltpu.SemaphoreType.DMA
    outgoing, placed = pl.pallas_call(
        functools.partial(place_kernel, senders, capacity),
        out_shape=(
            jax.ShapeDtypeStruct((SLOTS, width + EXTRA), BF16),
            jax.ShapeDtypeStruct((1, voxels), F32),
        ),
        in_specs=[HBM] * 3,
        out_specs=(VMEM, VMEM),
        scratch_shapes=[
            vmem((voxels, width), BF16),
            vmem(windows.shape, jnp.int32),
            vmem(coords.shape, jnp.int32),
            dma((3,)),
        ],
        compiler_params=params(64),
        name="place",
    )(windows, coords, x_latent)
    arrived = lax.all_to_all(
        outgoing.reshape(senders, capacity, width + EXTRA),
        ("cfg", "vox"),
        split_axis=0,
        concat_axis=0,
        tiled=True,
    ).reshape(SLOTS, width + EXTRA)

    own_gain = qk_gain.T
    table = position_parts(width)
    flat = jnp.transpose(w_qkv, (1, 2, 0))
    arrived, own_gain, table, flat = lax.optimization_barrier((arrived, own_gain, table, flat))

    shapes = dict(
        normed_q=((heads, branches, queries, width), BF16),
        keys=((branches, group, SLOTS), BF16),
        values=((branches, SLOTS, group), BF16),
        residual=((queries, width), F32),
        bias=((8, SLOTS), F32),
        sent=((queries, width), F32),
    )
    made = pl.pallas_call(
        functools.partial(first_kernel, senders, head_size),
        out_shape=tuple(jax.ShapeDtypeStruct(*shape) for shape in shapes.values()),
        in_specs=[SMEM, VMEM] + [HBM] * 5,
        out_specs=(HBM,) * 6,
        scratch_shapes=[
            vmem((SLOTS, width + EXTRA), BF16),
            vmem(table.shape, BF16),
            vmem((3, group, width), BF16),
            vmem((group, 2), F32),
            vmem((group, width), BF16),
            vmem((branches, SLOTS, width), BF16),
        ]
        + [vmem(*shape) for shape in shapes.values()]
        + [
            vmem((SLOTS, width), F32),
            vmem((queries, group), BF16),
            vmem((queries, width), F32),
            dma((5,)),
            dma((4,)),
            dma((branches,)),
            dma((branches,)),
        ],
        compiler_params=params(64),
        name="first_queries",
    )(guidance, modulation, arrived, table, flat, own_gain, w_out)
    normed_q, keys, values, residual, bias, partial = made

    def attend(distance, last):
        return pl.pallas_call(
            functools.partial(query_kernel, head_size, distance, last),
            out_shape=jax.ShapeDtypeStruct((queries, width), F32),
            in_specs=[SMEM, VMEM] + [HBM] * 8,
            out_specs=HBM,
            scratch_shapes=[
                vmem((branches, queries, width), BF16),
                vmem(*shapes["keys"]),
                vmem(*shapes["values"]),
                vmem(*shapes["bias"]),
                vmem((group, width), BF16),
                vmem((group, 2), F32),
                vmem((group, width), BF16),
                vmem((queries, width), F32),
                vmem((queries, width), F32),
                vmem((queries, group), BF16),
                dma((5,)),
                dma((branches,)),
                dma((branches,)),
                dma((branches,)),
                dma(()),
            ],
            compiler_params=params(64),
            name="more_queries",
        )(guidance, modulation, normed_q, keys, values, bias, flat, own_gain, w_out, residual)

    terms = []
    for distance in range(1, heads):
        turn = [(h, (h + distance) % heads) for h in range(heads)]
        terms.append(lax.ppermute(partial.astype(jnp.float16), "head", turn))
        partial = attend(distance, distance == heads - 1)
    for term in terms:
        partial = partial + term.astype(F32) * (1.0 / SENT_SCALE)
    columns = width // heads
    rows = jnp.concatenate(
        [
            partial[:, h * columns : (h + 1) * columns].reshape(senders, 1, share, columns)
            for h in range(heads)
        ],
        axis=1,
    ).astype(BF16)
    back = lax.all_to_all(
        rows.reshape(senders * heads, share, width // heads),
        ("cfg", "vox", "head"),
        split_axis=0,
        concat_axis=0,
        tiled=True,
    )
    return pl.pallas_call(
        return_kernel,
        out_shape=jax.ShapeDtypeStruct((voxels, width // heads), BF16),
        in_specs=[VMEM, HBM],
        out_specs=VMEM,
        scratch_shapes=[vmem((SLOTS, width // heads), BF16), dma(())],
        compiler_params=params(64),
        name="return_rows",
    )(placed, back.reshape(SLOTS, width // heads))


def solution(mesh):
    placed = (
        P(("cfg", "vox"), None),
        P(("cfg", "vox")),
        P(None, ("cfg", "vox")),
        P(),
        P(None, None, "head"),
        P("head", None),
        P(None, "head"),
        P(),
    )
    return jax.shard_map(
        on_device, mesh=mesh, in_specs=placed, out_specs=P(("cfg", "vox"), "head"), check_vma=False
    )
```

```python
import functools

import jax
import jax.numpy as jnp
from jax import lax
from jax.experimental import pallas as pl
from jax.experimental.pallas import tpu as pltpu
from jax.sharding import PartitionSpec as P

HEADS = 16
SLOTS = 512
GRID = 64
EXTRA = 128
BF16 = jnp.bfloat16
F32 = jnp.float32
VMEM = pl.BlockSpec(memory_space=pltpu.VMEM)
SMEM = pl.BlockSpec(memory_space=pltpu.SMEM)
HBM = pl.BlockSpec(memory_space=pltpu.HBM)
SENT_SCALE = 2.0**-7
NT = (((1,), (1,)), ((), ()))


def params(megabytes):
    return pltpu.CompilerParams(vmem_limit_bytes=megabytes * 1024 * 1024)


def iota(shape, dim):
    return lax.broadcasted_iota(jnp.int32, shape, dim)


def dot(a, b):
    return jnp.dot(a, b, preferred_element_type=F32)


def position_parts(model_width):
    freq_count = model_width // 3 // 2
    frequency = 1.0 / 10000.0 ** (jnp.arange(freq_count, dtype=F32) / freq_count)
    angles = jnp.arange(GRID, dtype=F32)[:, None] * frequency[None, :]
    block = jnp.concatenate([jnp.sin(angles), jnp.cos(angles)], axis=1)
    width = 2 * freq_count
    rows = [
        jnp.pad(block, ((0, 0), (c * width, model_width - (c + 1) * width))) for c in range(3)
    ]
    table = jnp.concatenate(rows, axis=0)
    top = lax.reduce_precision(table, 8, 7)
    rest = table - top
    middle = lax.reduce_precision(rest, 8, 7)
    low = rest - middle
    return jnp.concatenate([top, middle, low], axis=0).astype(BF16)


def place_kernel(
    senders,
    capacity,
    windows_hbm,
    coords_hbm,
    x_hbm,
    out_ref,
    placed_ref,
    x_ref,
    windows_ref,
    coords_ref,
    sems,
):
    loads = [
        pltpu.make_async_copy(source, target, sems.at[n])
        for n, (source, target) in enumerate(
            ((windows_hbm, windows_ref), (coords_hbm, coords_ref), (x_hbm, x_ref))
        )
    ]
    for load in loads:
        load.start()
    voxels, width = x_hbm.shape
    loads[0].wait()
    windows = windows_ref[...].reshape(1, voxels)
    member = windows == iota((senders, voxels), 0)
    earlier = (iota((voxels, voxels), 0) < iota((voxels, voxels), 1)).astype(F32).astype(BF16)
    member_f = member.astype(F32)
    before = dot(member_f.astype(BF16), earlier)
    rank = jnp.sum(before * member_f, axis=0, keepdims=True).astype(jnp.int32)
    placed = windows * capacity + rank
    placed_ref[...] = placed.astype(F32)
    placing = (placed == iota((SLOTS, voxels), 0)).astype(F32).astype(BF16)
    loads[1].wait()
    row = iota((EXTRA, voxels), 0)
    extra = jnp.where(row == 3, 1.0, 0.0).astype(F32)
    for c in range(3):
        extra = jnp.where(row == c, coords_ref[c : c + 1, :].astype(F32), extra)
    out_ref[:, width:] = lax.dot_general(
        placing, extra.astype(BF16), NT, preferred_element_type=F32
    ).astype(BF16)
    loads[2].wait()
    out_ref[:, :width] = dot(placing, x_ref[...]).astype(BF16)


def column_norm(rows, gain, head_size):
    blocks = []
    for start in range(0, rows.shape[0], head_size):
        block = rows[start : start + head_size]
        mean = jnp.sum(block * block, axis=0, keepdims=True) * (1.0 / head_size)
        blocks.append(block * lax.rsqrt(mean + 1e-06) * gain[start : start + head_size])
    return jnp.concatenate(blocks, axis=0).astype(BF16)


def project_keys(normed, w_key, gain, head_size):
    key = lax.dot_general(w_key, normed, NT, preferred_element_type=F32)
    return column_norm(key, gain, head_size)


def project_values(normed, w_value):
    return lax.dot_general(normed, w_value, NT, preferred_element_type=F32).astype(BF16)


def attend_heads(query, key, value, before_head, att_ref, bias, tile, head_size):
    queries, group = att_ref.shape
    lane_head = iota((queries, tile), 1) // head_size
    per_tile = tile // head_size
    heads = group // head_size

    def score(i):
        one = jnp.where(lane_head == i % per_tile, query(i // per_tile), 0.0).astype(BF16)
        return dot(one, key(i // per_tile))

    scores = score(0)
    mixed = jnp.zeros((queries, tile), F32)
    step = min(32, queries)
    for i in range(heads):
        before_head(i)
        following = score(i + 1) if i + 1 < heads else None
        pieces = []
        for r in range(0, queries, step):
            piece = scores[r : r + step] + bias
            weights = jnp.exp(piece - jnp.max(piece, axis=1, keepdims=True))
            total = jnp.sum(weights, axis=1, keepdims=True)
            pieces.append((weights * (1.0 / total)).astype(BF16))
        attend = jnp.concatenate(pieces, axis=0)
        mixed = jnp.where(lane_head == i % per_tile, dot(attend, value(i // per_tile)), mixed)
        if (i + 1) % per_tile == 0:
            start = i // per_tile * tile
            att_ref[:, start : start + tile] = mixed.astype(BF16)
        scores = following


def project_query(normed_q, w_query, gain, head_size):
    query = lax.dot_general(w_query, normed_q, NT, preferred_element_type=F32)
    query = column_norm(query, gain, head_size)
    return (query.astype(F32) * (1.0 / head_size**0.5)).T


def branch_scales(guidance_ref):
    g0, g1 = guidance_ref[0], guidance_ref[1]
    return 1.0 - g0, g0 - g1, g1


def pick_scale(b, scales):
    return jnp.where(b == 0, scales[0], jnp.where(b == 1, scales[1], scales[2]))


def copies(pairs, sems):
    return [
        pltpu.make_async_copy(source, target, sems.at[n])
        for n, (source, target) in enumerate(pairs)
    ]


def first_kernel(
    senders,
    head_size,
    guidance_ref,
    modulation_ref,
    rows_hbm,
    table_hbm,
    w_hbm,
    gain_hbm,
    w_out_hbm,
    normed_q_hbm,
    keys_hbm,
    values_hbm,
    residual_hbm,
    bias_hbm,
    sent_hbm,
    rows_ref,
    table_ref,
    w_ref,
    gain_ref,
    w_out_ref,
    normed_ref,
    normed_q_ref,
    keys_ref,
    values_ref,
    residual_ref,
    bias_ref,
    sent_ref,
    hidden_ref,
    att_ref,
    sum_ref,
    in_sems,
    out_sems,
    key_sems,
    value_sems,
):
    loads = copies(
        (
            (rows_hbm, rows_ref),
            (table_hbm, table_ref),
            (w_hbm, w_ref),
            (gain_hbm, gain_ref),
            (w_out_hbm, w_out_ref),
        ),
        in_sems,
    )
    stores = copies(
        (
            (normed_q_ref.at[pl.ds(1, normed_q_hbm.shape[0])], normed_q_hbm),
            (bias_ref, bias_hbm),
            (residual_ref, residual_hbm),
            (sent_ref, sent_hbm),
        ),
        out_sems,
    )
    for load in loads:
        load.start()
    branches, slots, width = normed_ref.shape
    heads, _, queries, _ = normed_q_ref.shape
    group = att_ref.shape[1]
    capacity = slots // senders
    share = queries // senders
    me = lax.axis_index("head")
    scales = branch_scales(guidance_ref)
    total = (scales[0] + scales[1]) + scales[2]

    loads[0].wait()
    extra = rows_ref[:, width:]
    pick = ((iota((8, EXTRA), 1) == 3)).astype(F32).astype(BF16)
    live = lax.dot_general(pick, extra, NT, preferred_element_type=F32)
    bias_ref[...] = jnp.where(live > 0.5, 0.0, -1e30)
    stores[1].start()

    spots = extra.astype(F32)
    lane = iota((slots, 3 * GRID), 1)
    wanted = jnp.where(
        lane < GRID,
        spots[:, 0:1],
        jnp.where(lane < 2 * GRID, spots[:, 1:2], spots[:, 2:3]),
    )
    chosen = (wanted == (lane % GRID).astype(F32)).astype(F32).astype(BF16)
    chosen = jnp.concatenate([chosen, chosen, chosen], axis=1)
    loads[1].wait()
    chunk = min(128, slots)
    shifts = [modulation_ref[b, 0:1, :] for b in range(branches)]
    stretches = [1.0 + modulation_ref[b, 1:2, :] for b in range(branches)]
    for start in range(0, slots, chunk):
        rows = slice(start, start + chunk)
        hidden = dot(chosen[rows], table_ref[...]) + rows_ref[rows, :width].astype(F32)
        hidden_ref[rows, :] = hidden
        centred = hidden - jnp.mean(hidden, axis=1, keepdims=True)
        spread = jnp.mean(centred * centred, axis=1, keepdims=True)
        normal = centred * lax.rsqrt(spread + 1e-06)
        for b in range(branches):
            normed_ref[b, rows, :] = (normal * stretches[b] + shifts[b]).astype(BF16)

    for d in range(heads):
        first = lax.rem(me + d + 1, heads) * share
        if share % 16 == 0:
            for s in range(senders):
                source = pl.ds(pl.multiple_of(s * capacity + first, 16), share)
                target = slice(s * share, (s + 1) * share)
                if d == heads - 1:
                    residual_ref[target, :] = hidden_ref[source, :] * total
                for b in range(branches):
                    normed_q_ref[d, b, target, :] = normed_ref[b, source, :]
        else:
            row = iota((queries, slots), 0)
            wanted_slot = (row // share) * capacity + first + row % share
            chooser = (wanted_slot == iota((queries, slots), 1)).astype(F32)
            if d == heads - 1:
                picked = jnp.dot(
                    chooser,
                    hidden_ref[...],
                    preferred_element_type=F32,
                    precision=lax.Precision.HIGHEST,
                )
                residual_ref[...] = picked * total
            for b in range(branches):
                normed_q_ref[d, b] = dot(chooser.astype(BF16), normed_ref[b]).astype(BF16)
    stores[0].start()
    stores[2].start()

    bias = bias_ref[0:1, :]
    tile = min(256, group)
    for load in loads[2:4]:
        load.wait()

    def store(b):
        return (
            pltpu.make_async_copy(keys_ref.at[b], keys_hbm.at[b], key_sems.at[b]),
            pltpu.make_async_copy(values_ref.at[b], values_hbm.at[b], value_sems.at[b]),
        )

    for b in range(branches):
        made = {}

        def make(kind, t):
            features = slice(t * tile, (t + 1) * tile)
            if kind == "query":
                array = project_query(
                    normed_q_ref[0, b], w_ref[0, features, :], gain_ref[features, 0:1], head_size
                )
            elif kind == "key":
                array = project_keys(
                    normed_ref[b], w_ref[1, features, :], gain_ref[features, 1:2], head_size
                )
                keys_ref[b, features, :] = array
            else:
                array = project_values(normed_ref[b], w_ref[2, features, :])
                values_ref[b, :, features] = array
            made[kind, t] = array

        def get(kind, t):
            if (kind, t) not in made:
                make(kind, t)
            return made[kind, t]

        for kind in ("query", "key", "value"):
            make(kind, 0)
        waiting = [(kind, t) for t in range(1, group // tile) for kind in ("query", "key", "value")]

        def before_head(i):
            if i < len(waiting):
                get(*waiting[i])

        attend_heads(
            functools.partial(get, "query"),
            functools.partial(get, "key"),
            functools.partial(get, "value"),
            before_head,
            att_ref,
            bias,
            tile,
            head_size,
        )
        for copy in store(b):
            copy.start()
        if b == 0:
            loads[4].wait()
        term = dot(att_ref[...], w_out_ref[...]) * (scales[b] * modulation_ref[b, 2:3, :])
        if b == 0:
            sum_ref[...] = term
        else:
            sum_ref[...] += term
    sent_ref[...] = sum_ref[...] * SENT_SCALE
    stores[3].start()
    for copy in stores:
        copy.wait()
    for b in range(branches):
        for copy in store(b):
            copy.wait()


def query_kernel(
    head_size,
    distance,
    last,
    guidance_ref,
    modulation_ref,
    normed_q_hbm,
    keys_hbm,
    values_hbm,
    bias_hbm,
    w_hbm,
    gain_hbm,
    w_out_hbm,
    start_hbm,
    out_hbm,
    normed_q_ref,
    keys_ref,
    values_ref,
    bias_ref,
    w_ref,
    gain_ref,
    w_out_ref,
    sum_ref,
    att_ref,
    in_sems,
    query_sems,
    key_sems,
    value_sems,
    out_sem,
):
    branches, _, slots = keys_ref.shape
    group = att_ref.shape[1]
    loads = copies(
        (
            (w_hbm.at[0], w_ref),
            (gain_hbm, gain_ref),
            (bias_hbm, bias_ref),
            (w_out_hbm, w_out_ref),
            (start_hbm, sum_ref),
        ),
        in_sems,
    )
    if not last:
        loads = loads[:-1]

    def load(b):
        return (
            pltpu.make_async_copy(
                normed_q_hbm.at[distance - 1, b], normed_q_ref.at[b], query_sems.at[b]
            ),
            pltpu.make_async_copy(keys_hbm.at[b], keys_ref.at[b], key_sems.at[b]),
            pltpu.make_async_copy(values_hbm.at[b], values_ref.at[b], value_sems.at[b]),
        )

    for copy in load(0)[:1] + (loads[0], loads[1]) + load(0)[1:] + (loads[2], loads[3]):
        copy.start()
    if last:
        loads[4].start()
    for b in range(1, branches):
        for copy in load(b):
            copy.start()
    scales = branch_scales(guidance_ref)
    tile = min(256, group)
    if not last:
        sum_ref[...] = jnp.zeros_like(sum_ref)
    for copy in loads[:3]:
        copy.wait()
    bias = bias_ref[0:1, :]

    for b in range(branches):
        for copy in load(b):
            copy.wait()
        made = {}

        def query(t):
            if t not in made:
                features = slice(t * tile, (t + 1) * tile)
                made[t] = project_query(
                    normed_q_ref[b], w_ref[features, :], gain_ref[features, 0:1], head_size
                )
            return made[t]

        attend_heads(
            query,
            lambda t: keys_ref[b, t * tile : (t + 1) * tile, :],
            lambda t: values_ref[b, :, t * tile : (t + 1) * tile],
            lambda i: query(min(i, group // tile - 1)),
            att_ref,
            bias,
            tile,
            head_size,
        )
        if b == 0:
            for copy in loads[3:]:
                copy.wait()
        sum_ref[...] += dot(att_ref[...], w_out_ref[...]) * (
            scales[b] * modulation_ref[b, 2:3, :]
        )
    if not last:
        sum_ref[...] = sum_ref[...] * SENT_SCALE
    store = pltpu.make_async_copy(sum_ref, out_hbm, out_sem)
    store.start()
    store.wait()


def return_kernel(placed_ref, rows_ref, out_ref):
    voxels = placed_ref.shape[1]
    column = jnp.broadcast_to(placed_ref[...], (128, voxels)).T
    column = column.astype(jnp.int32)
    lane = iota((voxels, 128), 1)
    placing = jnp.concatenate(
        [(column == lane + start).astype(F32).astype(BF16) for start in range(0, SLOTS, 128)], axis=1
    )
    out_ref[...] = dot(placing, rows_ref[...]).astype(BF16)


def on_device(x_latent, windows, coords, modulation, w_qkv, w_out, qk_gain, guidance):
    voxels, width = x_latent.shape
    group = w_qkv.shape[2]
    head_size = width // HEADS
    branches = modulation.shape[0]
    senders = lax.axis_size(("cfg", "vox"))
    heads = lax.axis_size("head")
    capacity = SLOTS // senders
    queries = SLOTS // heads
    share = capacity // heads

    vmem, dma = pltpu.VMEM, pltpu.SemaphoreType.DMA
    outgoing, placed = pl.pallas_call(
        functools.partial(place_kernel, senders, capacity),
        out_shape=(
            jax.ShapeDtypeStruct((SLOTS, width + EXTRA), BF16),
            jax.ShapeDtypeStruct((1, voxels), F32),
        ),
        in_specs=[HBM] * 3,
        out_specs=(VMEM, VMEM),
        scratch_shapes=[
            vmem((voxels, width), BF16),
            vmem(windows.shape, jnp.int32),
            vmem(coords.shape, jnp.int32),
            dma((3,)),
        ],
        compiler_params=params(64),
        name="place",
    )(windows, coords, x_latent)
    arrived = lax.all_to_all(
        outgoing.reshape(senders, capacity, width + EXTRA),
        ("cfg", "vox"),
        split_axis=0,
        concat_axis=0,
        tiled=True,
    ).reshape(SLOTS, width + EXTRA)

    own_gain = qk_gain.T
    table = position_parts(width)
    flat = jnp.transpose(w_qkv, (1, 2, 0))
    arrived, own_gain, table, flat = lax.optimization_barrier((arrived, own_gain, table, flat))

    shapes = dict(
        normed_q=((heads - 1, branches, queries, width), BF16),
        keys=((branches, group, SLOTS), BF16),
        values=((branches, SLOTS, group), BF16),
        residual=((queries, width), F32),
        bias=((8, SLOTS), F32),
        sent=((queries, width), F32),
    )
    made = pl.pallas_call(
        functools.partial(first_kernel, senders, head_size),
        out_shape=tuple(jax.ShapeDtypeStruct(*shape) for shape in shapes.values()),
        in_specs=[SMEM, VMEM] + [HBM] * 5,
        out_specs=(HBM,) * 6,
        scratch_shapes=[
            vmem((SLOTS, width + EXTRA), BF16),
            vmem(table.shape, BF16),
            vmem((3, group, width), BF16),
            vmem((group, 2), F32),
            vmem((group, width), BF16),
            vmem((branches, SLOTS, width), BF16),
        ]
        + [vmem((heads, branches, queries, width), BF16)]
        + [vmem(*shape) for name, shape in shapes.items() if name != "normed_q"]
        + [
            vmem((SLOTS, width), F32),
            vmem((queries, group), BF16),
            vmem((queries, width), F32),
            dma((5,)),
            dma((4,)),
            dma((branches,)),
            dma((branches,)),
        ],
        compiler_params=params(64),
        name="first_queries",
    )(guidance, modulation, arrived, table, flat, own_gain, w_out)
    normed_q, keys, values, residual, bias, partial = made

    def attend(distance, last):
        return pl.pallas_call(
            functools.partial(query_kernel, head_size, distance, last),
            out_shape=jax.ShapeDtypeStruct((queries, width), F32),
            in_specs=[SMEM, VMEM] + [HBM] * 8,
            out_specs=HBM,
            scratch_shapes=[
                vmem((branches, queries, width), BF16),
                vmem(*shapes["keys"]),
                vmem(*shapes["values"]),
                vmem(*shapes["bias"]),
                vmem((group, width), BF16),
                vmem((group, 2), F32),
                vmem((group, width), BF16),
                vmem((queries, width), F32),
                vmem((queries, group), BF16),
                dma((5,)),
                dma((branches,)),
                dma((branches,)),
                dma((branches,)),
                dma(()),
            ],
            compiler_params=params(64),
            name="more_queries",
        )(guidance, modulation, normed_q, keys, values, bias, flat, own_gain, w_out, residual)

    terms = []
    for distance in range(1, heads):
        turn = [(h, (h + distance) % heads) for h in range(heads)]
        terms.append(lax.ppermute(partial.astype(jnp.float16), "head", turn))
        partial = attend(distance, distance == heads - 1)
    for term in terms:
        partial = partial + term.astype(F32) * (1.0 / SENT_SCALE)
    columns = width // heads
    rows = jnp.concatenate(
        [
            partial[:, h * columns : (h + 1) * columns].reshape(senders, 1, share, columns)
            for h in range(heads)
        ],
        axis=1,
    ).astype(BF16)
    back = lax.all_to_all(
        rows.reshape(senders * heads, share, width // heads),
        ("cfg", "vox", "head"),
        split_axis=0,
        concat_axis=0,
        tiled=True,
    )
    return pl.pallas_call(
        return_kernel,
        out_shape=jax.ShapeDtypeStruct((voxels, width // heads), BF16),
        in_specs=[VMEM, VMEM],
        out_specs=VMEM,
        compiler_params=params(16),
        name="return_rows",
    )(placed, back.reshape(SLOTS, width // heads))


def solution(mesh):
    placed = (
        P(("cfg", "vox"), None),
        P(("cfg", "vox")),
        P(None, ("cfg", "vox")),
        P(),
        P(None, None, "head"),
        P("head", None),
        P(None, "head"),
        P(),
    )
    return jax.shard_map(
        on_device, mesh=mesh, in_specs=placed, out_specs=P(("cfg", "vox"), "head"), check_vma=False
    )
```

```python
import functools

import jax
import jax.numpy as jnp
from jax import lax
from jax.experimental import pallas as pl
from jax.experimental.pallas import tpu as pltpu
from jax.sharding import PartitionSpec as P

HEADS = 16
SLOTS = 512
GRID = 64
EXTRA = 128
BF16 = jnp.bfloat16
F32 = jnp.float32
VMEM = pl.BlockSpec(memory_space=pltpu.VMEM)
SMEM = pl.BlockSpec(memory_space=pltpu.SMEM)
HBM = pl.BlockSpec(memory_space=pltpu.HBM)
SENT_SCALE = 2.0**-7
NT = (((1,), (1,)), ((), ()))


def params(megabytes):
    return pltpu.CompilerParams(vmem_limit_bytes=megabytes * 1024 * 1024)


def iota(shape, dim):
    return lax.broadcasted_iota(jnp.int32, shape, dim)


def dot(a, b):
    return jnp.dot(a, b, preferred_element_type=F32)


def position_parts(model_width):
    freq_count = model_width // 3 // 2
    frequency = 1.0 / 10000.0 ** (jnp.arange(freq_count, dtype=F32) / freq_count)
    angles = jnp.arange(GRID, dtype=F32)[:, None] * frequency[None, :]
    block = jnp.concatenate([jnp.sin(angles), jnp.cos(angles)], axis=1)
    width = 2 * freq_count
    rows = [
        jnp.pad(block, ((0, 0), (c * width, model_width - (c + 1) * width))) for c in range(3)
    ]
    table = jnp.concatenate(rows, axis=0)
    top = lax.reduce_precision(table, 8, 7)
    rest = table - top
    middle = lax.reduce_precision(rest, 8, 7)
    low = rest - middle
    return jnp.concatenate([top, middle, low], axis=0).astype(BF16)


def place_kernel(
    senders,
    capacity,
    windows_hbm,
    coords_hbm,
    x_hbm,
    out_ref,
    placed_ref,
    x_ref,
    windows_ref,
    coords_ref,
    sems,
):
    loads = [
        pltpu.make_async_copy(source, target, sems.at[n])
        for n, (source, target) in enumerate(
            ((windows_hbm, windows_ref), (coords_hbm, coords_ref), (x_hbm, x_ref))
        )
    ]
    for load in loads:
        load.start()
    voxels, width = x_hbm.shape
    loads[0].wait()
    windows = windows_ref[...].reshape(1, voxels)
    member = windows == iota((senders, voxels), 0)
    earlier = (iota((voxels, voxels), 0) < iota((voxels, voxels), 1)).astype(F32).astype(BF16)
    member_f = member.astype(F32)
    before = dot(member_f.astype(BF16), earlier)
    rank = jnp.sum(before * member_f, axis=0, keepdims=True).astype(jnp.int32)
    placed = windows * capacity + rank
    placed_ref[...] = placed.astype(F32)
    placing = (placed == iota((SLOTS, voxels), 0)).astype(F32).astype(BF16)
    loads[1].wait()
    row = iota((EXTRA, voxels), 0)
    extra = jnp.where(row == 3, 1.0, 0.0).astype(F32)
    for c in range(3):
        extra = jnp.where(row == c, coords_ref[c : c + 1, :].astype(F32), extra)
    out_ref[:, width:] = lax.dot_general(
        placing, extra.astype(BF16), NT, preferred_element_type=F32
    ).astype(BF16)
    loads[2].wait()
    out_ref[:, :width] = dot(placing, x_ref[...]).astype(BF16)


def column_norm(rows, gain, head_size):
    blocks = []
    for start in range(0, rows.shape[0], head_size):
        block = rows[start : start + head_size]
        mean = jnp.sum(block * block, axis=0, keepdims=True) * (1.0 / head_size)
        blocks.append(block * lax.rsqrt(mean + 1e-06) * gain[start : start + head_size])
    return jnp.concatenate(blocks, axis=0).astype(BF16)


def project_keys(normed, w_key, gain, head_size):
    key = lax.dot_general(w_key, normed, NT, preferred_element_type=F32)
    return column_norm(key, gain, head_size)


def project_values(normed, w_value):
    return lax.dot_general(normed, w_value, NT, preferred_element_type=F32).astype(BF16)


def attend_heads(query, key, value, before_head, att_ref, bias, tile, head_size):
    queries, group = att_ref.shape
    lane_head = iota((queries, tile), 1) // head_size
    per_tile = tile // head_size
    heads = group // head_size

    def score(i):
        one = jnp.where(lane_head == i % per_tile, query(i // per_tile), 0.0).astype(BF16)
        return dot(one, key(i // per_tile))

    scores = score(0)
    mixed = jnp.zeros((queries, tile), F32)
    step = min(32, queries)
    for i in range(heads):
        before_head(i)
        following = score(i + 1) if i + 1 < heads else None
        pieces = []
        for r in range(0, queries, step):
            piece = scores[r : r + step] + bias
            weights = jnp.exp(piece - jnp.max(piece, axis=1, keepdims=True))
            total = jnp.sum(weights, axis=1, keepdims=True)
            pieces.append((weights * (1.0 / total)).astype(BF16))
        attend = jnp.concatenate(pieces, axis=0)
        mixed = jnp.where(lane_head == i % per_tile, dot(attend, value(i // per_tile)), mixed)
        if (i + 1) % per_tile == 0:
            start = i // per_tile * tile
            att_ref[:, start : start + tile] = mixed.astype(BF16)
        scores = following


def project_query(normed_q, w_query, gain, head_size):
    query = lax.dot_general(w_query, normed_q, NT, preferred_element_type=F32)
    query = column_norm(query, gain, head_size)
    return (query.astype(F32) * (1.0 / head_size**0.5)).T


def branch_scales(guidance_ref):
    g0, g1 = guidance_ref[0], guidance_ref[1]
    return 1.0 - g0, g0 - g1, g1


def pick_scale(b, scales):
    return jnp.where(b == 0, scales[0], jnp.where(b == 1, scales[1], scales[2]))


def copies(pairs, sems):
    return [
        pltpu.make_async_copy(source, target, sems.at[n])
        for n, (source, target) in enumerate(pairs)
    ]


def gain_columns(gain_rows_ref):
    rows = gain_rows_ref[...]
    return jnp.concatenate([rows, rows, rows, rows], axis=0).T


def first_kernel(
    senders,
    head_size,
    guidance_ref,
    modulation_ref,
    gain_rows_ref,
    rows_ref,
    table_hbm,
    w_hbm,
    w_out_hbm,
    normed_q_hbm,
    keys_hbm,
    values_hbm,
    residual_hbm,
    bias_hbm,
    sent_ref,
    table_ref,
    w_ref,
    gain_ref,
    w_out_ref,
    normed_ref,
    normed_q_ref,
    keys_ref,
    values_ref,
    residual_ref,
    bias_ref,
    hidden_ref,
    att_ref,
    sum_ref,
    in_sems,
    out_sems,
    key_sems,
    value_sems,
):
    loads = copies(
        (
            (table_hbm, table_ref),
            (w_hbm, w_ref),
            (w_out_hbm, w_out_ref),
        ),
        in_sems,
    )
    stores = copies(
        (
            (normed_q_ref.at[pl.ds(1, normed_q_hbm.shape[0])], normed_q_hbm),
            (bias_ref, bias_hbm),
            (residual_ref, residual_hbm),
        ),
        out_sems,
    )
    for load in loads:
        load.start()
    branches, slots, width = normed_ref.shape
    heads, _, queries, _ = normed_q_ref.shape
    group = att_ref.shape[1]
    capacity = slots // senders
    share = queries // senders
    me = lax.axis_index("head")
    scales = branch_scales(guidance_ref)
    total = (scales[0] + scales[1]) + scales[2]

    gain_ref[...] = gain_columns(gain_rows_ref)
    extra = rows_ref[:, width:]
    pick = ((iota((8, EXTRA), 1) == 3)).astype(F32).astype(BF16)
    live = lax.dot_general(pick, extra, NT, preferred_element_type=F32)
    bias_ref[...] = jnp.where(live > 0.5, 0.0, -1e30)
    stores[1].start()

    spots = extra.astype(F32)
    lane = iota((slots, 3 * GRID), 1)
    wanted = jnp.where(
        lane < GRID,
        spots[:, 0:1],
        jnp.where(lane < 2 * GRID, spots[:, 1:2], spots[:, 2:3]),
    )
    chosen = (wanted == (lane % GRID).astype(F32)).astype(F32).astype(BF16)
    chosen = jnp.concatenate([chosen, chosen, chosen], axis=1)
    loads[0].wait()
    chunk = min(128, slots)
    shifts = [modulation_ref[b, 0:1, :] for b in range(branches)]
    stretches = [1.0 + modulation_ref[b, 1:2, :] for b in range(branches)]
    for start in range(0, slots, chunk):
        rows = slice(start, start + chunk)
        hidden = dot(chosen[rows], table_ref[...]) + rows_ref[rows, :width].astype(F32)
        hidden_ref[rows, :] = hidden
        centred = hidden - jnp.mean(hidden, axis=1, keepdims=True)
        spread = jnp.mean(centred * centred, axis=1, keepdims=True)
        normal = centred * lax.rsqrt(spread + 1e-06)
        for b in range(branches):
            normed_ref[b, rows, :] = (normal * stretches[b] + shifts[b]).astype(BF16)

    for d in range(heads):
        first = lax.rem(me + d + 1, heads) * share
        if share % 16 == 0:
            for s in range(senders):
                source = pl.ds(pl.multiple_of(s * capacity + first, 16), share)
                target = slice(s * share, (s + 1) * share)
                if d == heads - 1:
                    residual_ref[target, :] = hidden_ref[source, :] * total
                for b in range(branches):
                    normed_q_ref[d, b, target, :] = normed_ref[b, source, :]
        else:
            row = iota((queries, slots), 0)
            wanted_slot = (row // share) * capacity + first + row % share
            chooser = (wanted_slot == iota((queries, slots), 1)).astype(F32)
            if d == heads - 1:
                picked = jnp.dot(
                    chooser,
                    hidden_ref[...],
                    preferred_element_type=F32,
                    precision=lax.Precision.HIGHEST,
                )
                residual_ref[...] = picked * total
            for b in range(branches):
                normed_q_ref[d, b] = dot(chooser.astype(BF16), normed_ref[b]).astype(BF16)
    stores[0].start()
    stores[2].start()

    bias = bias_ref[0:1, :]
    tile = min(256, group)
    loads[1].wait()

    def store(b):
        return (
            pltpu.make_async_copy(keys_ref.at[b], keys_hbm.at[b], key_sems.at[b]),
            pltpu.make_async_copy(values_ref.at[b], values_hbm.at[b], value_sems.at[b]),
        )

    for b in range(branches):
        made = {}

        def make(kind, t):
            features = slice(t * tile, (t + 1) * tile)
            if kind == "query":
                array = project_query(
                    normed_q_ref[0, b], w_ref[0, features, :], gain_ref[features, 0:1], head_size
                )
            elif kind == "key":
                array = project_keys(
                    normed_ref[b], w_ref[1, features, :], gain_ref[features, 1:2], head_size
                )
                keys_ref[b, features, :] = array
            else:
                array = project_values(normed_ref[b], w_ref[2, features, :])
                values_ref[b, :, features] = array
            made[kind, t] = array

        def get(kind, t):
            if (kind, t) not in made:
                make(kind, t)
            return made[kind, t]

        for kind in ("query", "key", "value"):
            make(kind, 0)
        waiting = [(kind, t) for t in range(1, group // tile) for kind in ("query", "key", "value")]

        def before_head(i):
            if i < len(waiting):
                get(*waiting[i])

        attend_heads(
            functools.partial(get, "query"),
            functools.partial(get, "key"),
            functools.partial(get, "value"),
            before_head,
            att_ref,
            bias,
            tile,
            head_size,
        )
        for copy in store(b):
            copy.start()
        if b == 0:
            loads[2].wait()
        term = dot(att_ref[...], w_out_ref[...]) * (scales[b] * modulation_ref[b, 2:3, :])
        if b == 0:
            sum_ref[...] = term
        else:
            sum_ref[...] += term
    sent_ref[...] = sum_ref[...] * SENT_SCALE
    for copy in stores:
        copy.wait()
    for b in range(branches):
        for copy in store(b):
            copy.wait()


def query_kernel(
    head_size,
    distance,
    last,
    guidance_ref,
    modulation_ref,
    gain_rows_ref,
    normed_q_hbm,
    keys_hbm,
    values_hbm,
    bias_hbm,
    w_hbm,
    w_out_hbm,
    start_hbm,
    out_hbm,
    normed_q_ref,
    keys_ref,
    values_ref,
    bias_ref,
    w_ref,
    gain_ref,
    w_out_ref,
    sum_ref,
    att_ref,
    in_sems,
    query_sems,
    key_sems,
    value_sems,
    out_sem,
):
    branches, _, slots = keys_ref.shape
    group = att_ref.shape[1]
    loads = copies(
        (
            (w_hbm.at[0], w_ref),
            (bias_hbm, bias_ref),
            (w_out_hbm, w_out_ref),
            (start_hbm, sum_ref),
        ),
        in_sems,
    )
    if not last:
        loads = loads[:-1]

    def load(b):
        return (
            pltpu.make_async_copy(
                normed_q_hbm.at[distance - 1, b], normed_q_ref.at[b], query_sems.at[b]
            ),
            pltpu.make_async_copy(keys_hbm.at[b], keys_ref.at[b], key_sems.at[b]),
            pltpu.make_async_copy(values_hbm.at[b], values_ref.at[b], value_sems.at[b]),
        )

    for copy in load(0)[:1] + (loads[0], loads[1]) + load(0)[1:] + tuple(loads[2:]):
        copy.start()
    for b in range(1, branches):
        for copy in load(b):
            copy.start()
    scales = branch_scales(guidance_ref)
    tile = min(256, group)
    if not last:
        sum_ref[...] = jnp.zeros_like(sum_ref)
    gain_ref[...] = gain_columns(gain_rows_ref)
    for copy in loads[:2]:
        copy.wait()
    bias = bias_ref[0:1, :]

    for b in range(branches):
        for copy in load(b):
            copy.wait()
        made = {}

        def query(t):
            if t not in made:
                features = slice(t * tile, (t + 1) * tile)
                made[t] = project_query(
                    normed_q_ref[b], w_ref[features, :], gain_ref[features, 0:1], head_size
                )
            return made[t]

        attend_heads(
            query,
            lambda t: keys_ref[b, t * tile : (t + 1) * tile, :],
            lambda t: values_ref[b, :, t * tile : (t + 1) * tile],
            lambda i: query(min(i, group // tile - 1)),
            att_ref,
            bias,
            tile,
            head_size,
        )
        if b == 0:
            for copy in loads[2:]:
                copy.wait()
        sum_ref[...] += dot(att_ref[...], w_out_ref[...]) * (
            scales[b] * modulation_ref[b, 2:3, :]
        )
    if not last:
        sum_ref[...] = sum_ref[...] * SENT_SCALE
    store = pltpu.make_async_copy(sum_ref, out_hbm, out_sem)
    store.start()
    store.wait()


def return_kernel(placed_ref, rows_ref, out_ref):
    voxels = placed_ref.shape[1]
    column = jnp.broadcast_to(placed_ref[...], (128, voxels)).T
    column = column.astype(jnp.int32)
    lane = iota((voxels, 128), 1)
    placing = jnp.concatenate(
        [(column == lane + start).astype(F32).astype(BF16) for start in range(0, SLOTS, 128)], axis=1
    )
    out_ref[...] = dot(placing, rows_ref[...]).astype(BF16)


def on_device(x_latent, windows, coords, modulation, w_qkv, w_out, qk_gain, guidance):
    voxels, width = x_latent.shape
    group = w_qkv.shape[2]
    head_size = width // HEADS
    branches = modulation.shape[0]
    senders = lax.axis_size(("cfg", "vox"))
    heads = lax.axis_size("head")
    capacity = SLOTS // senders
    queries = SLOTS // heads
    share = capacity // heads

    vmem, dma = pltpu.VMEM, pltpu.SemaphoreType.DMA
    outgoing, placed = pl.pallas_call(
        functools.partial(place_kernel, senders, capacity),
        out_shape=(
            jax.ShapeDtypeStruct((SLOTS, width + EXTRA), BF16),
            jax.ShapeDtypeStruct((1, voxels), F32),
        ),
        in_specs=[HBM] * 3,
        out_specs=(VMEM, VMEM),
        scratch_shapes=[
            vmem((voxels, width), BF16),
            vmem(windows.shape, jnp.int32),
            vmem(coords.shape, jnp.int32),
            dma((3,)),
        ],
        compiler_params=params(64),
        name="place",
    )(windows, coords, x_latent)
    arrived = lax.all_to_all(
        outgoing.reshape(senders, capacity, width + EXTRA),
        ("cfg", "vox"),
        split_axis=0,
        concat_axis=0,
        tiled=True,
    ).reshape(SLOTS, width + EXTRA)

    table = position_parts(width)
    flat = jnp.transpose(w_qkv, (1, 2, 0))
    shapes = dict(
        normed_q=((heads - 1, branches, queries, width), BF16),
        keys=((branches, group, SLOTS), BF16),
        values=((branches, SLOTS, group), BF16),
        residual=((queries, width), F32),
        bias=((8, SLOTS), F32),
        sent=((queries, width), F32),
    )
    made = pl.pallas_call(
        functools.partial(first_kernel, senders, head_size),
        out_shape=tuple(jax.ShapeDtypeStruct(*shape) for shape in shapes.values()),
        in_specs=[SMEM, VMEM, VMEM, VMEM] + [HBM] * 3,
        out_specs=(HBM,) * 5 + (VMEM,),
        scratch_shapes=[
            vmem(table.shape, BF16),
            vmem((3, group, width), BF16),
            vmem((group, 8), F32),
            vmem((group, width), BF16),
            vmem((branches, SLOTS, width), BF16),
        ]
        + [vmem((heads, branches, queries, width), BF16)]
        + [vmem(*shape) for name, shape in shapes.items() if name not in ("normed_q", "sent")]
        + [
            vmem((SLOTS, width), F32),
            vmem((queries, group), BF16),
            vmem((queries, width), F32),
            dma((3,)),
            dma((3,)),
            dma((branches,)),
            dma((branches,)),
        ],
        compiler_params=params(46),
        name="first_queries",
    )(guidance, modulation, qk_gain, arrived, table, flat, w_out)
    normed_q, keys, values, residual, bias, partial = made

    def attend(distance, last):
        return pl.pallas_call(
            functools.partial(query_kernel, head_size, distance, last),
            out_shape=jax.ShapeDtypeStruct((queries, width), F32),
            in_specs=[SMEM, VMEM, VMEM] + [HBM] * 7,
            out_specs=HBM,
            scratch_shapes=[
                vmem((branches, queries, width), BF16),
                vmem(*shapes["keys"]),
                vmem(*shapes["values"]),
                vmem(*shapes["bias"]),
                vmem((group, width), BF16),
                vmem((group, 8), F32),
                vmem((group, width), BF16),
                vmem((queries, width), F32),
                vmem((queries, group), BF16),
                dma((4,)),
                dma((branches,)),
                dma((branches,)),
                dma((branches,)),
                dma(()),
            ],
            compiler_params=params(46),
            name="more_queries",
        )(guidance, modulation, qk_gain, normed_q, keys, values, bias, flat, w_out, residual)

    terms = []
    for distance in range(1, heads):
        turn = [(h, (h + distance) % heads) for h in range(heads)]
        terms.append(lax.ppermute(partial.astype(jnp.float16), "head", turn))
        partial = attend(distance, distance == heads - 1)
    for term in terms:
        partial = partial + term.astype(F32) * (1.0 / SENT_SCALE)
    columns = width // heads
    rows = jnp.concatenate(
        [
            partial[:, h * columns : (h + 1) * columns].reshape(senders, 1, share, columns)
            for h in range(heads)
        ],
        axis=1,
    ).astype(BF16)
    back = lax.all_to_all(
        rows.reshape(senders * heads, share, width // heads),
        ("cfg", "vox", "head"),
        split_axis=0,
        concat_axis=0,
        tiled=True,
    )
    return pl.pallas_call(
        return_kernel,
        out_shape=jax.ShapeDtypeStruct((voxels, width // heads), BF16),
        in_specs=[VMEM, VMEM],
        out_specs=VMEM,
        compiler_params=params(16),
        name="return_rows",
    )(placed, back.reshape(SLOTS, width // heads))


def solution(mesh):
    placed = (
        P(("cfg", "vox"), None),
        P(("cfg", "vox")),
        P(None, ("cfg", "vox")),
        P(),
        P(None, None, "head"),
        P("head", None),
        P(None, "head"),
        P(),
    )
    return jax.shard_map(
        on_device, mesh=mesh, in_specs=placed, out_specs=P(("cfg", "vox"), "head"), check_vma=False
    )
```

```python
import functools

import jax
import jax.numpy as jnp
from jax import lax
from jax.experimental import pallas as pl
from jax.experimental.pallas import tpu as pltpu
from jax.sharding import PartitionSpec as P

HEADS = 16
SLOTS = 512
GRID = 64
EXTRA = 128
BF16 = jnp.bfloat16
F32 = jnp.float32
VMEM = pl.BlockSpec(memory_space=pltpu.VMEM)
SMEM = pl.BlockSpec(memory_space=pltpu.SMEM)
HBM = pl.BlockSpec(memory_space=pltpu.HBM)
SENT_SCALE = 2.0**-7
NT = (((1,), (1,)), ((), ()))


def params(megabytes):
    return pltpu.CompilerParams(vmem_limit_bytes=megabytes * 1024 * 1024)


def iota(shape, dim):
    return lax.broadcasted_iota(jnp.int32, shape, dim)


def dot(a, b):
    return jnp.dot(a, b, preferred_element_type=F32)


def position_parts(model_width):
    freq_count = model_width // 3 // 2
    frequency = 1.0 / 10000.0 ** (jnp.arange(freq_count, dtype=F32) / freq_count)
    angles = jnp.arange(GRID, dtype=F32)[:, None] * frequency[None, :]
    block = jnp.concatenate([jnp.sin(angles), jnp.cos(angles)], axis=1)
    width = 2 * freq_count
    rows = [
        jnp.pad(block, ((0, 0), (c * width, model_width - (c + 1) * width))) for c in range(3)
    ]
    table = jnp.concatenate(rows, axis=0)
    top = lax.reduce_precision(table, 8, 7)
    rest = table - top
    middle = lax.reduce_precision(rest, 8, 7)
    low = rest - middle
    return jnp.concatenate([top, middle, low], axis=0).astype(BF16)


def place_kernel(
    senders,
    capacity,
    windows_hbm,
    coords_hbm,
    x_hbm,
    out_ref,
    placed_ref,
    x_ref,
    windows_ref,
    coords_ref,
    sems,
):
    loads = [
        pltpu.make_async_copy(source, target, sems.at[n])
        for n, (source, target) in enumerate(
            ((windows_hbm, windows_ref), (coords_hbm, coords_ref), (x_hbm, x_ref))
        )
    ]
    for load in loads:
        load.start()
    voxels, width = x_hbm.shape
    loads[0].wait()
    windows = windows_ref[...].reshape(1, voxels)
    member = windows == iota((senders, voxels), 0)
    earlier = (iota((voxels, voxels), 0) < iota((voxels, voxels), 1)).astype(F32).astype(BF16)
    member_f = member.astype(F32)
    before = dot(member_f.astype(BF16), earlier)
    rank = jnp.sum(before * member_f, axis=0, keepdims=True).astype(jnp.int32)
    placed = windows * capacity + rank
    placed_ref[...] = placed.astype(F32)
    placing = (placed == iota((SLOTS, voxels), 0)).astype(F32).astype(BF16)
    loads[1].wait()
    row = iota((EXTRA, voxels), 0)
    extra = jnp.where(row == 3, 1.0, 0.0).astype(F32)
    for c in range(3):
        extra = jnp.where(row == c, coords_ref[c : c + 1, :].astype(F32), extra)
    out_ref[:, width:] = lax.dot_general(
        placing, extra.astype(BF16), NT, preferred_element_type=F32
    ).astype(BF16)
    loads[2].wait()
    out_ref[:, :width] = dot(placing, x_ref[...]).astype(BF16)


def column_norm(rows, gain, head_size):
    blocks = []
    for start in range(0, rows.shape[0], head_size):
        block = rows[start : start + head_size]
        mean = jnp.sum(block * block, axis=0, keepdims=True) * (1.0 / head_size)
        blocks.append(block * lax.rsqrt(mean + 1e-06) * gain[start : start + head_size])
    return jnp.concatenate(blocks, axis=0).astype(BF16)


def project_keys(normed, w_key, gain, head_size):
    key = lax.dot_general(w_key, normed, NT, preferred_element_type=F32)
    return column_norm(key, gain, head_size)


def project_values(normed, w_value):
    return lax.dot_general(normed, w_value, NT, preferred_element_type=F32).astype(BF16)


def attend_heads(query, key, value, before_head, att_ref, bias, tile, head_size):
    queries, group = att_ref.shape
    lane_head = iota((queries, tile), 1) // head_size
    per_tile = tile // head_size
    heads = group // head_size

    def score(i):
        one = jnp.where(lane_head == i % per_tile, query(i // per_tile), 0.0).astype(BF16)
        return dot(one, key(i // per_tile))

    scores = score(0)
    mixed = jnp.zeros((queries, tile), F32)
    step = min(32, queries)
    for i in range(heads):
        before_head(i)
        following = score(i + 1) if i + 1 < heads else None
        pieces = []
        for r in range(0, queries, step):
            piece = scores[r : r + step] + bias
            weights = jnp.exp(piece - jnp.max(piece, axis=1, keepdims=True))
            total = jnp.sum(weights, axis=1, keepdims=True)
            pieces.append((weights * (1.0 / total)).astype(BF16))
        attend = jnp.concatenate(pieces, axis=0)
        mixed = jnp.where(lane_head == i % per_tile, dot(attend, value(i // per_tile)), mixed)
        if (i + 1) % per_tile == 0:
            start = i // per_tile * tile
            att_ref[:, start : start + tile] = mixed.astype(BF16)
        scores = following


def project_query(normed_q, w_query, gain, head_size):
    query = lax.dot_general(w_query, normed_q, NT, preferred_element_type=F32)
    query = column_norm(query, gain, head_size)
    return (query.astype(F32) * (1.0 / head_size**0.5)).T


def branch_scales(guidance_ref):
    g0, g1 = guidance_ref[0], guidance_ref[1]
    return 1.0 - g0, g0 - g1, g1


def pick_scale(b, scales):
    return jnp.where(b == 0, scales[0], jnp.where(b == 1, scales[1], scales[2]))


def copies(pairs, sems):
    return [
        pltpu.make_async_copy(source, target, sems.at[n])
        for n, (source, target) in enumerate(pairs)
    ]


def gain_columns(gain_rows_ref):
    rows = gain_rows_ref[...]
    return jnp.concatenate([rows, rows, rows, rows], axis=0).T


def first_kernel(
    senders,
    head_size,
    guidance_ref,
    modulation_ref,
    gain_rows_ref,
    rows_ref,
    table_hbm,
    w_hbm,
    w_out_hbm,
    later_q_ref,
    keys_ref,
    values_ref,
    residual_ref,
    bias_ref,
    sent_ref,
    table_ref,
    w_ref,
    gain_ref,
    w_out_ref,
    normed_ref,
    next_q_ref,
    hidden_ref,
    att_ref,
    sum_ref,
    in_sems,
):
    loads = copies(
        (
            (table_hbm, table_ref),
            (w_hbm, w_ref),
            (w_out_hbm, w_out_ref),
        ),
        in_sems,
    )
    for load in loads:
        load.start()
    branches, slots, width = normed_ref.shape
    queries, heads = next_q_ref.shape[1], later_q_ref.shape[0] + 1
    group = att_ref.shape[1]
    capacity = slots // senders
    share = queries // senders
    me = lax.axis_index("head")
    scales = branch_scales(guidance_ref)
    total = (scales[0] + scales[1]) + scales[2]

    gain_ref[...] = gain_columns(gain_rows_ref)
    extra = rows_ref[:, width:]
    pick = ((iota((8, EXTRA), 1) == 3)).astype(F32).astype(BF16)
    live = lax.dot_general(pick, extra, NT, preferred_element_type=F32)
    bias_ref[...] = jnp.where(live > 0.5, 0.0, -1e30)

    spots = extra.astype(F32)
    lane = iota((slots, 3 * GRID), 1)
    wanted = jnp.where(
        lane < GRID,
        spots[:, 0:1],
        jnp.where(lane < 2 * GRID, spots[:, 1:2], spots[:, 2:3]),
    )
    chosen = (wanted == (lane % GRID).astype(F32)).astype(F32).astype(BF16)
    chosen = jnp.concatenate([chosen, chosen, chosen], axis=1)
    loads[0].wait()
    chunk = min(128, slots)
    shifts = [modulation_ref[b, 0:1, :] for b in range(branches)]
    stretches = [1.0 + modulation_ref[b, 1:2, :] for b in range(branches)]
    for start in range(0, slots, chunk):
        rows = slice(start, start + chunk)
        hidden = dot(chosen[rows], table_ref[...]) + rows_ref[rows, :width].astype(F32)
        hidden_ref[rows, :] = hidden
        centred = hidden - jnp.mean(hidden, axis=1, keepdims=True)
        spread = jnp.mean(centred * centred, axis=1, keepdims=True)
        normal = centred * lax.rsqrt(spread + 1e-06)
        for b in range(branches):
            normed_ref[b, rows, :] = (normal * stretches[b] + shifts[b]).astype(BF16)

    for d in range(heads):
        normed_q_ref = next_q_ref if d == 0 else later_q_ref.at[d - 1]
        first = lax.rem(me + d + 1, heads) * share
        if share % 16 == 0:
            for s in range(senders):
                source = pl.ds(pl.multiple_of(s * capacity + first, 16), share)
                target = slice(s * share, (s + 1) * share)
                if d == heads - 1:
                    residual_ref[target, :] = hidden_ref[source, :] * total
                for b in range(branches):
                    normed_q_ref[b, target, :] = normed_ref[b, source, :]
        else:
            row = iota((queries, slots), 0)
            wanted_slot = (row // share) * capacity + first + row % share
            chooser = (wanted_slot == iota((queries, slots), 1)).astype(F32)
            if d == heads - 1:
                picked = jnp.dot(
                    chooser,
                    hidden_ref[...],
                    preferred_element_type=F32,
                    precision=lax.Precision.HIGHEST,
                )
                residual_ref[...] = picked * total
            for b in range(branches):
                normed_q_ref[b] = dot(chooser.astype(BF16), normed_ref[b]).astype(BF16)

    bias = bias_ref[0:1, :]
    tile = min(256, group)
    loads[1].wait()

    for b in range(branches):
        made = {}

        def make(kind, t):
            features = slice(t * tile, (t + 1) * tile)
            if kind == "query":
                array = project_query(
                    next_q_ref[b], w_ref[0, features, :], gain_ref[features, 0:1], head_size
                )
            elif kind == "key":
                array = project_keys(
                    normed_ref[b], w_ref[1, features, :], gain_ref[features, 1:2], head_size
                )
                keys_ref[b, features, :] = array
            else:
                array = project_values(normed_ref[b], w_ref[2, features, :])
                values_ref[b, :, features] = array
            made[kind, t] = array

        def get(kind, t):
            if (kind, t) not in made:
                make(kind, t)
            return made[kind, t]

        for kind in ("query", "key", "value"):
            make(kind, 0)
        waiting = [(kind, t) for t in range(1, group // tile) for kind in ("query", "key", "value")]

        def before_head(i):
            if i < len(waiting):
                get(*waiting[i])

        attend_heads(
            functools.partial(get, "query"),
            functools.partial(get, "key"),
            functools.partial(get, "value"),
            before_head,
            att_ref,
            bias,
            tile,
            head_size,
        )
        if b == 0:
            loads[2].wait()
        term = dot(att_ref[...], w_out_ref[...]) * (scales[b] * modulation_ref[b, 2:3, :])
        if b == 0:
            sum_ref[...] = term
        else:
            sum_ref[...] += term
    sent_ref[...] = sum_ref[...] * SENT_SCALE


def query_kernel(
    head_size,
    distance,
    last,
    guidance_ref,
    modulation_ref,
    gain_rows_ref,
    normed_q_ref,
    keys_ref,
    values_ref,
    bias_ref,
    w_ref,
    w_out_ref,
    start_ref,
    sum_ref,
    gain_ref,
    att_ref,
):
    branches, _, slots = keys_ref.shape
    group = att_ref.shape[1]
    scales = branch_scales(guidance_ref)
    tile = min(256, group)
    gain_ref[...] = gain_columns(gain_rows_ref)
    bias = bias_ref[0:1, :]

    for b in range(branches):
        made = {}

        def query(t):
            if t not in made:
                features = slice(t * tile, (t + 1) * tile)
                made[t] = project_query(
                    normed_q_ref[distance - 1, b],
                    w_ref[0, features, :],
                    gain_ref[features, 0:1], head_size
                )
            return made[t]

        attend_heads(
            query,
            lambda t: keys_ref[b, t * tile : (t + 1) * tile, :],
            lambda t: values_ref[b, :, t * tile : (t + 1) * tile],
            lambda i: query(min(i, group // tile - 1)),
            att_ref,
            bias,
            tile,
            head_size,
        )
        term = dot(att_ref[...], w_out_ref[...]) * (scales[b] * modulation_ref[b, 2:3, :])
        if b == 0:
            sum_ref[...] = start_ref[...] + term if last else term
        else:
            sum_ref[...] += term
    if not last:
        sum_ref[...] = sum_ref[...] * SENT_SCALE


def return_kernel(placed_ref, rows_ref, out_ref):
    voxels = placed_ref.shape[1]
    column = jnp.broadcast_to(placed_ref[...], (128, voxels)).T
    column = column.astype(jnp.int32)
    lane = iota((voxels, 128), 1)
    placing = jnp.concatenate(
        [(column == lane + start).astype(F32).astype(BF16) for start in range(0, SLOTS, 128)], axis=1
    )
    out_ref[...] = dot(placing, rows_ref[...]).astype(BF16)


def on_device(x_latent, windows, coords, modulation, w_qkv, w_out, qk_gain, guidance):
    voxels, width = x_latent.shape
    group = w_qkv.shape[2]
    head_size = width // HEADS
    branches = modulation.shape[0]
    senders = lax.axis_size(("cfg", "vox"))
    heads = lax.axis_size("head")
    capacity = SLOTS // senders
    queries = SLOTS // heads
    share = capacity // heads

    vmem, dma = pltpu.VMEM, pltpu.SemaphoreType.DMA
    outgoing, placed = pl.pallas_call(
        functools.partial(place_kernel, senders, capacity),
        out_shape=(
            jax.ShapeDtypeStruct((SLOTS, width + EXTRA), BF16),
            jax.ShapeDtypeStruct((1, voxels), F32),
        ),
        in_specs=[HBM] * 3,
        out_specs=(VMEM, VMEM),
        scratch_shapes=[
            vmem((voxels, width), BF16),
            vmem(windows.shape, jnp.int32),
            vmem(coords.shape, jnp.int32),
            dma((3,)),
        ],
        compiler_params=params(64),
        name="place",
    )(windows, coords, x_latent)
    arrived = lax.all_to_all(
        outgoing.reshape(senders, capacity, width + EXTRA),
        ("cfg", "vox"),
        split_axis=0,
        concat_axis=0,
        tiled=True,
    ).reshape(SLOTS, width + EXTRA)

    table = position_parts(width)
    flat = jnp.transpose(w_qkv, (1, 2, 0))
    shapes = dict(
        normed_q=((heads - 1, branches, queries, width), BF16),
        keys=((branches, group, SLOTS), BF16),
        values=((branches, SLOTS, group), BF16),
        residual=((queries, width), F32),
        bias=((8, SLOTS), F32),
        sent=((queries, width), F32),
    )
    made = pl.pallas_call(
        functools.partial(first_kernel, senders, head_size),
        out_shape=tuple(jax.ShapeDtypeStruct(*shape) for shape in shapes.values()),
        in_specs=[SMEM, VMEM, VMEM, VMEM] + [HBM] * 3,
        out_specs=(VMEM,) * 6,
        scratch_shapes=[
            vmem(table.shape, BF16),
            vmem((3, group, width), BF16),
            vmem((group, 8), F32),
            vmem((group, width), BF16),
            vmem((branches, SLOTS, width), BF16),
            vmem((branches, queries, width), BF16),
            vmem((SLOTS, width), F32),
            vmem((queries, group), BF16),
            vmem((queries, width), F32),
            dma((3,)),
        ],
        compiler_params=params(43),
        name="first_queries",
    )(guidance, modulation, qk_gain, arrived, table, flat, w_out)
    normed_q, keys, values, residual, bias, partial = made

    def attend(distance, last):
        return pl.pallas_call(
            functools.partial(query_kernel, head_size, distance, last),
            out_shape=jax.ShapeDtypeStruct((queries, width), F32),
            in_specs=[SMEM] + [VMEM] * 9,
            out_specs=VMEM,
            scratch_shapes=[vmem((group, 8), F32), vmem((queries, group), BF16)],
            compiler_params=params(28),
            name="more_queries",
        )(guidance, modulation, qk_gain, normed_q, keys, values, bias, flat, w_out, residual)

    terms = []
    for distance in range(1, heads):
        turn = [(h, (h + distance) % heads) for h in range(heads)]
        terms.append(lax.ppermute(partial.astype(jnp.float16), "head", turn))
        partial = attend(distance, distance == heads - 1)
    for term in terms:
        partial = partial + term.astype(F32) * (1.0 / SENT_SCALE)
    columns = width // heads
    rows = jnp.concatenate(
        [
            partial[:, h * columns : (h + 1) * columns].reshape(senders, 1, share, columns)
            for h in range(heads)
        ],
        axis=1,
    ).astype(BF16)
    back = lax.all_to_all(
        rows.reshape(senders * heads, share, width // heads),
        ("cfg", "vox", "head"),
        split_axis=0,
        concat_axis=0,
        tiled=True,
    )
    return pl.pallas_call(
        return_kernel,
        out_shape=jax.ShapeDtypeStruct((voxels, width // heads), BF16),
        in_specs=[VMEM, VMEM],
        out_specs=VMEM,
        compiler_params=params(16),
        name="return_rows",
    )(placed, back.reshape(SLOTS, width // heads))


def solution(mesh):
    placed = (
        P(("cfg", "vox"), None),
        P(("cfg", "vox")),
        P(None, ("cfg", "vox")),
        P(),
        P(None, None, "head"),
        P("head", None),
        P(None, "head"),
        P(),
    )
    return jax.shard_map(
        on_device, mesh=mesh, in_specs=placed, out_specs=P(("cfg", "vox"), "head"), check_vma=False
    )
```

```python
import functools

import jax
import jax.numpy as jnp
from jax import lax
from jax.experimental import pallas as pl
from jax.experimental.pallas import tpu as pltpu
from jax.sharding import PartitionSpec as P

HEADS = 16
SLOTS = 512
GRID = 64
EXTRA = 128
BF16 = jnp.bfloat16
F32 = jnp.float32
VMEM = pl.BlockSpec(memory_space=pltpu.VMEM)
SMEM = pl.BlockSpec(memory_space=pltpu.SMEM)
HBM = pl.BlockSpec(memory_space=pltpu.HBM)
SENT_SCALE = 2.0**-7
NT = (((1,), (1,)), ((), ()))


def params(megabytes):
    return pltpu.CompilerParams(vmem_limit_bytes=megabytes * 1024 * 1024)


def iota(shape, dim):
    return lax.broadcasted_iota(jnp.int32, shape, dim)


def dot(a, b):
    return jnp.dot(a, b, preferred_element_type=F32)


def position_parts(model_width):
    freq_count = model_width // 3 // 2
    frequency = 1.0 / 10000.0 ** (jnp.arange(freq_count, dtype=F32) / freq_count)
    angles = jnp.arange(GRID, dtype=F32)[:, None] * frequency[None, :]
    block = jnp.concatenate([jnp.sin(angles), jnp.cos(angles)], axis=1)
    width = 2 * freq_count
    rows = [
        jnp.pad(block, ((0, 0), (c * width, model_width - (c + 1) * width))) for c in range(3)
    ]
    table = jnp.concatenate(rows, axis=0)
    top = lax.reduce_precision(table, 8, 7)
    rest = table - top
    middle = lax.reduce_precision(rest, 8, 7)
    low = rest - middle
    return jnp.concatenate([top, middle, low], axis=0).astype(BF16)


def place_kernel(
    senders,
    capacity,
    windows_hbm,
    coords_hbm,
    x_hbm,
    out_ref,
    placed_ref,
    x_ref,
    windows_ref,
    coords_ref,
    sems,
):
    loads = [
        pltpu.make_async_copy(source, target, sems.at[n])
        for n, (source, target) in enumerate(
            ((windows_hbm, windows_ref), (coords_hbm, coords_ref), (x_hbm, x_ref))
        )
    ]
    for load in loads:
        load.start()
    voxels, width = x_hbm.shape
    loads[0].wait()
    windows = windows_ref[...].reshape(1, voxels)
    member = windows == iota((senders, voxels), 0)
    earlier = (iota((voxels, voxels), 0) < iota((voxels, voxels), 1)).astype(F32).astype(BF16)
    member_f = member.astype(F32)
    before = dot(member_f.astype(BF16), earlier)
    rank = jnp.sum(before * member_f, axis=0, keepdims=True).astype(jnp.int32)
    placed = windows * capacity + rank
    placed_ref[...] = placed.astype(F32)
    placing = (placed == iota((SLOTS, voxels), 0)).astype(F32).astype(BF16)
    loads[1].wait()
    row = iota((EXTRA, voxels), 0)
    extra = jnp.where(row == 3, 1.0, 0.0).astype(F32)
    for c in range(3):
        extra = jnp.where(row == c, coords_ref[c : c + 1, :].astype(F32), extra)
    out_ref[:, width:] = lax.dot_general(
        placing, extra.astype(BF16), NT, preferred_element_type=F32
    ).astype(BF16)
    loads[2].wait()
    out_ref[:, :width] = dot(placing, x_ref[...]).astype(BF16)


def column_norm(rows, gain, head_size):
    blocks = []
    for start in range(0, rows.shape[0], head_size):
        block = rows[start : start + head_size]
        mean = jnp.sum(block * block, axis=0, keepdims=True) * (1.0 / head_size)
        blocks.append(block * lax.rsqrt(mean + 1e-06) * gain[start : start + head_size])
    return jnp.concatenate(blocks, axis=0).astype(BF16)


def project_keys(normed, w_key, gain, head_size):
    key = lax.dot_general(w_key, normed, NT, preferred_element_type=F32)
    return column_norm(key, gain, head_size)


def project_values(normed, w_value):
    return lax.dot_general(normed, w_value, NT, preferred_element_type=F32).astype(BF16)


def attend_heads(query, key, value, before_head, att_ref, bias, tile, head_size):
    queries, group = att_ref.shape
    lane_head = iota((queries, tile), 1) // head_size
    per_tile = tile // head_size
    heads = group // head_size

    def score(i):
        one = jnp.where(lane_head == i % per_tile, query(i // per_tile), 0.0).astype(BF16)
        return dot(one, key(i // per_tile))

    scores = score(0)
    mixed = jnp.zeros((queries, tile), F32)
    step = min(32, queries)
    for i in range(heads):
        before_head(i)
        following = score(i + 1) if i + 1 < heads else None
        pieces = []
        for r in range(0, queries, step):
            piece = scores[r : r + step] + bias
            weights = jnp.exp(piece - jnp.max(piece, axis=1, keepdims=True))
            total = jnp.sum(weights, axis=1, keepdims=True)
            pieces.append((weights * (1.0 / total)).astype(BF16))
        attend = jnp.concatenate(pieces, axis=0)
        mixed = jnp.where(lane_head == i % per_tile, dot(attend, value(i // per_tile)), mixed)
        if (i + 1) % per_tile == 0:
            start = i // per_tile * tile
            att_ref[:, start : start + tile] = mixed.astype(BF16)
        scores = following


def project_query(normed_q, w_query, gain, head_size):
    query = lax.dot_general(w_query, normed_q, NT, preferred_element_type=F32)
    query = column_norm(query, gain, head_size)
    return (query.astype(F32) * (1.0 / head_size**0.5)).T


def branch_scales(guidance_ref):
    g0, g1 = guidance_ref[0], guidance_ref[1]
    return 1.0 - g0, g0 - g1, g1


def pick_scale(b, scales):
    return jnp.where(b == 0, scales[0], jnp.where(b == 1, scales[1], scales[2]))


def copies(pairs, sems):
    return [
        pltpu.make_async_copy(source, target, sems.at[n])
        for n, (source, target) in enumerate(pairs)
    ]


def gain_columns(gain_rows_ref):
    rows = gain_rows_ref[...]
    return jnp.concatenate([rows, rows, rows, rows], axis=0).T


def first_kernel(
    senders,
    head_size,
    guidance_ref,
    modulation_ref,
    gain_rows_ref,
    rows_ref,
    table_hbm,
    w_hbm,
    w_out_hbm,
    half_q_ref,
    later_q_ref,
    keys_ref,
    values_ref,
    residual_ref,
    bias_ref,
    sent_ref,
    table_ref,
    w_ref,
    gain_ref,
    w_out_ref,
    normed_ref,
    next_q_ref,
    hidden_ref,
    att_ref,
    sum_ref,
    in_sems,
):
    loads = copies(
        (
            (table_hbm, table_ref),
            (w_hbm, w_ref),
            (w_out_hbm, w_out_ref),
        ),
        in_sems,
    )
    for load in loads:
        load.start()
    branches, slots, width = normed_ref.shape
    queries, heads = later_q_ref.shape[2], later_q_ref.shape[0] + 1
    half = queries // 2
    group = att_ref.shape[1]
    capacity = slots // senders
    share = queries // senders
    me = lax.axis_index("head")
    scales = branch_scales(guidance_ref)
    total = (scales[0] + scales[1]) + scales[2]

    gain_ref[...] = gain_columns(gain_rows_ref)
    extra = rows_ref[:, width:]
    pick = ((iota((8, EXTRA), 1) == 3)).astype(F32).astype(BF16)
    live = lax.dot_general(pick, extra, NT, preferred_element_type=F32)
    bias_ref[...] = jnp.where(live > 0.5, 0.0, -1e30)

    spots = extra.astype(F32)
    lane = iota((slots, 3 * GRID), 1)
    wanted = jnp.where(
        lane < GRID,
        spots[:, 0:1],
        jnp.where(lane < 2 * GRID, spots[:, 1:2], spots[:, 2:3]),
    )
    chosen = (wanted == (lane % GRID).astype(F32)).astype(F32).astype(BF16)
    chosen = jnp.concatenate([chosen, chosen, chosen], axis=1)
    loads[0].wait()
    chunk = min(128, slots)
    shifts = [modulation_ref[b, 0:1, :] for b in range(branches)]
    stretches = [1.0 + modulation_ref[b, 1:2, :] for b in range(branches)]
    for start in range(0, slots, chunk):
        rows = slice(start, start + chunk)
        hidden = dot(chosen[rows], table_ref[...]) + rows_ref[rows, :width].astype(F32)
        hidden_ref[rows, :] = hidden
        centred = hidden - jnp.mean(hidden, axis=1, keepdims=True)
        spread = jnp.mean(centred * centred, axis=1, keepdims=True)
        normal = centred * lax.rsqrt(spread + 1e-06)
        for b in range(branches):
            normed_ref[b, rows, :] = (normal * stretches[b] + shifts[b]).astype(BF16)

    for d in range(heads):
        def put(b, start, rows):
            if d > 0:
                later_q_ref[d - 1, b, start : start + rows.shape[0], :] = rows
            elif start < half:
                next_q_ref[b, start : start + rows.shape[0], :] = rows
            else:
                half_q_ref[0, b, start - half : start - half + rows.shape[0], :] = rows

        first = lax.rem(me + d + 1, heads) * share
        if share % 16 == 0:
            for s in range(senders):
                source = pl.ds(pl.multiple_of(s * capacity + first, 16), share)
                target = slice(s * share, (s + 1) * share)
                if d == heads - 1:
                    residual_ref[target, :] = hidden_ref[source, :] * total
                for b in range(branches):
                    put(b, s * share, normed_ref[b, source, :])
        else:
            row = iota((queries, slots), 0)
            wanted_slot = (row // share) * capacity + first + row % share
            chooser = (wanted_slot == iota((queries, slots), 1)).astype(F32)
            if d == heads - 1:
                picked = jnp.dot(
                    chooser,
                    hidden_ref[...],
                    preferred_element_type=F32,
                    precision=lax.Precision.HIGHEST,
                )
                residual_ref[...] = picked * total
            for b in range(branches):
                rows = dot(chooser.astype(BF16), normed_ref[b]).astype(BF16)
                put(b, 0, rows[:half])
                put(b, half, rows[half:])

    bias = bias_ref[0:1, :]
    tile = min(256, group)
    loads[1].wait()

    for b in range(branches):
        made = {}

        def make(kind, t):
            features = slice(t * tile, (t + 1) * tile)
            if kind == "query":
                array = project_query(
                    next_q_ref[b], w_ref[0, features, :], gain_ref[features, 0:1], head_size
                )
            elif kind == "key":
                array = project_keys(
                    normed_ref[b], w_ref[1, features, :], gain_ref[features, 1:2], head_size
                )
                keys_ref[b, features, :] = array
            else:
                array = project_values(normed_ref[b], w_ref[2, features, :])
                values_ref[b, :, features] = array
            made[kind, t] = array

        def get(kind, t):
            if (kind, t) not in made:
                make(kind, t)
            return made[kind, t]

        for kind in ("query", "key", "value"):
            make(kind, 0)
        waiting = [(kind, t) for t in range(1, group // tile) for kind in ("query", "key", "value")]

        def before_head(i):
            if i < len(waiting):
                get(*waiting[i])

        attend_heads(
            functools.partial(get, "query"),
            functools.partial(get, "key"),
            functools.partial(get, "value"),
            before_head,
            att_ref,
            bias,
            tile,
            head_size,
        )
        if b == 0:
            loads[2].wait()
        term = dot(att_ref[...], w_out_ref[...]) * (scales[b] * modulation_ref[b, 2:3, :])
        if b == 0:
            sum_ref[...] = term
        else:
            sum_ref[...] += term
    sent_ref[...] = sum_ref[...] * SENT_SCALE


def query_kernel(
    head_size,
    distance,
    last,
    guidance_ref,
    modulation_ref,
    gain_rows_ref,
    normed_q_ref,
    keys_ref,
    values_ref,
    bias_ref,
    w_ref,
    w_out_ref,
    start_ref,
    sum_ref,
    gain_ref,
    att_ref,
):
    branches, _, slots = keys_ref.shape
    group = att_ref.shape[1]
    scales = branch_scales(guidance_ref)
    tile = min(256, group)
    gain_ref[...] = gain_columns(gain_rows_ref)
    bias = bias_ref[0:1, :]

    for b in range(branches):
        made = {}

        def query(t):
            if t not in made:
                features = slice(t * tile, (t + 1) * tile)
                made[t] = project_query(
                    normed_q_ref[distance - 1, b],
                    w_ref[0, features, :],
                    gain_ref[features, 0:1], head_size
                )
            return made[t]

        attend_heads(
            query,
            lambda t: keys_ref[b, t * tile : (t + 1) * tile, :],
            lambda t: values_ref[b, :, t * tile : (t + 1) * tile],
            lambda i: query(min(i, group // tile - 1)),
            att_ref,
            bias,
            tile,
            head_size,
        )
        term = dot(att_ref[...], w_out_ref[...]) * (scales[b] * modulation_ref[b, 2:3, :])
        if b == 0:
            sum_ref[...] = start_ref[...] + term if last else term
        else:
            sum_ref[...] += term
    if not last:
        sum_ref[...] = sum_ref[...] * SENT_SCALE


def return_kernel(placed_ref, rows_ref, out_ref):
    voxels = placed_ref.shape[1]
    column = jnp.broadcast_to(placed_ref[...], (128, voxels)).T
    column = column.astype(jnp.int32)
    lane = iota((voxels, 128), 1)
    placing = jnp.concatenate(
        [(column == lane + start).astype(F32).astype(BF16) for start in range(0, SLOTS, 128)], axis=1
    )
    out_ref[...] = dot(placing, rows_ref[...]).astype(BF16)


def on_device(x_latent, windows, coords, modulation, w_qkv, w_out, qk_gain, guidance):
    voxels, width = x_latent.shape
    group = w_qkv.shape[2]
    head_size = width // HEADS
    branches = modulation.shape[0]
    senders = lax.axis_size(("cfg", "vox"))
    heads = lax.axis_size("head")
    capacity = SLOTS // senders
    queries = SLOTS // heads
    share = capacity // heads

    vmem, dma = pltpu.VMEM, pltpu.SemaphoreType.DMA
    outgoing, placed = pl.pallas_call(
        functools.partial(place_kernel, senders, capacity),
        out_shape=(
            jax.ShapeDtypeStruct((SLOTS, width + EXTRA), BF16),
            jax.ShapeDtypeStruct((1, voxels), F32),
        ),
        in_specs=[HBM] * 3,
        out_specs=(VMEM, VMEM),
        scratch_shapes=[
            vmem((voxels, width), BF16),
            vmem(windows.shape, jnp.int32),
            vmem(coords.shape, jnp.int32),
            dma((3,)),
        ],
        compiler_params=params(64),
        name="place",
    )(windows, coords, x_latent)
    arrived = lax.all_to_all(
        outgoing.reshape(senders, capacity, width + EXTRA),
        ("cfg", "vox"),
        split_axis=0,
        concat_axis=0,
        tiled=True,
    ).reshape(SLOTS, width + EXTRA)

    table = position_parts(width)
    flat = jnp.transpose(w_qkv, (1, 2, 0))
    shapes = dict(
        half_q=((1, branches, queries // 2, width), BF16),
        normed_q=((heads - 1, branches, queries, width), BF16),
        keys=((branches, group, SLOTS), BF16),
        values=((branches, SLOTS, group), BF16),
        residual=((queries, width), F32),
        bias=((8, SLOTS), F32),
        sent=((queries // 2, width), F32),
    )
    made = pl.pallas_call(
        functools.partial(first_kernel, senders, head_size),
        out_shape=tuple(jax.ShapeDtypeStruct(*shape) for shape in shapes.values()),
        in_specs=[SMEM, VMEM, VMEM, VMEM] + [HBM] * 3,
        out_specs=(VMEM,) * 7,
        scratch_shapes=[
            vmem(table.shape, BF16),
            vmem((3, group, width), BF16),
            vmem((group, 8), F32),
            vmem((group, width), BF16),
            vmem((branches, SLOTS, width), BF16),
            vmem((branches, queries // 2, width), BF16),
            vmem((SLOTS, width), F32),
            vmem((queries // 2, group), BF16),
            vmem((queries // 2, width), F32),
            dma((3,)),
        ],
        compiler_params=params(42),
        name="first_queries",
    )(guidance, modulation, qk_gain, arrived, table, flat, w_out)
    half_q, normed_q, keys, values, residual, bias, partial = made

    def attend(normed_q, distance, last):
        queries = normed_q.shape[2]
        return pl.pallas_call(
            functools.partial(query_kernel, head_size, distance, last),
            out_shape=jax.ShapeDtypeStruct((queries, width), F32),
            in_specs=[SMEM] + [VMEM] * 9,
            out_specs=VMEM,
            scratch_shapes=[vmem((group, 8), F32), vmem((queries, group), BF16)],
            compiler_params=params(28),
            name="more_queries",
        )(guidance, modulation, qk_gain, normed_q, keys, values, bias, flat, w_out, residual)

    terms = []
    for distance in range(1, heads):
        turn = [(h, (h + distance) % heads) for h in range(heads)]
        term = lax.ppermute(partial.astype(jnp.float16), "head", turn)
        if distance == 1:
            partial = attend(half_q, 1, False)
            other = lax.ppermute(partial.astype(jnp.float16), "head", turn)
            term = jnp.concatenate([term, other], axis=0)
        terms.append(term)
        partial = attend(normed_q, distance, distance == heads - 1)
    for term in terms:
        partial = partial + term.astype(F32) * (1.0 / SENT_SCALE)
    columns = width // heads
    rows = jnp.concatenate(
        [
            partial[:, h * columns : (h + 1) * columns].reshape(senders, 1, share, columns)
            for h in range(heads)
        ],
        axis=1,
    ).astype(BF16)
    back = lax.all_to_all(
        rows.reshape(senders * heads, share, width // heads),
        ("cfg", "vox", "head"),
        split_axis=0,
        concat_axis=0,
        tiled=True,
    )
    return pl.pallas_call(
        return_kernel,
        out_shape=jax.ShapeDtypeStruct((voxels, width // heads), BF16),
        in_specs=[VMEM, VMEM],
        out_specs=VMEM,
        compiler_params=params(16),
        name="return_rows",
    )(placed, back.reshape(SLOTS, width // heads))


def solution(mesh):
    placed = (
        P(("cfg", "vox"), None),
        P(("cfg", "vox")),
        P(None, ("cfg", "vox")),
        P(),
        P(None, None, "head"),
        P("head", None),
        P(None, "head"),
        P(),
    )
    return jax.shard_map(
        on_device, mesh=mesh, in_specs=placed, out_specs=P(("cfg", "vox"), "head"), check_vma=False
    )
```

```python
import functools

import jax
import jax.numpy as jnp
from jax import lax
from jax.experimental import pallas as pl
from jax.experimental.pallas import tpu as pltpu
from jax.sharding import PartitionSpec as P

HEADS = 16
SLOTS = 512
GRID = 64
EXTRA = 128
BF16 = jnp.bfloat16
F32 = jnp.float32
VMEM = pl.BlockSpec(memory_space=pltpu.VMEM)
SMEM = pl.BlockSpec(memory_space=pltpu.SMEM)
HBM = pl.BlockSpec(memory_space=pltpu.HBM)
SENT_SCALE = 2.0**-7
NT = (((1,), (1,)), ((), ()))


def params(megabytes):
    return pltpu.CompilerParams(vmem_limit_bytes=megabytes * 1024 * 1024)


def iota(shape, dim):
    return lax.broadcasted_iota(jnp.int32, shape, dim)


def dot(a, b):
    return jnp.dot(a, b, preferred_element_type=F32)


def position_parts(model_width):
    freq_count = model_width // 3 // 2
    frequency = 1.0 / 10000.0 ** (jnp.arange(freq_count, dtype=F32) / freq_count)
    angles = jnp.arange(GRID, dtype=F32)[:, None] * frequency[None, :]
    block = jnp.concatenate([jnp.sin(angles), jnp.cos(angles)], axis=1)
    width = 2 * freq_count
    rows = [
        jnp.pad(block, ((0, 0), (c * width, model_width - (c + 1) * width))) for c in range(3)
    ]
    table = jnp.concatenate(rows, axis=0)
    top = lax.reduce_precision(table, 8, 7)
    rest = table - top
    middle = lax.reduce_precision(rest, 8, 7)
    low = rest - middle
    return jnp.concatenate([top, middle, low], axis=0).astype(BF16)


def place_kernel(
    senders,
    capacity,
    windows_hbm,
    coords_hbm,
    x_hbm,
    out_ref,
    placed_ref,
    x_ref,
    windows_ref,
    coords_ref,
    sems,
):
    loads = [
        pltpu.make_async_copy(source, target, sems.at[n])
        for n, (source, target) in enumerate(
            ((windows_hbm, windows_ref), (coords_hbm, coords_ref), (x_hbm, x_ref))
        )
    ]
    for load in loads:
        load.start()
    voxels, width = x_hbm.shape
    loads[0].wait()
    windows = windows_ref[...].reshape(1, voxels)
    member = windows == iota((senders, voxels), 0)
    earlier = (iota((voxels, voxels), 0) < iota((voxels, voxels), 1)).astype(F32).astype(BF16)
    member_f = member.astype(F32)
    before = dot(member_f.astype(BF16), earlier)
    rank = jnp.sum(before * member_f, axis=0, keepdims=True).astype(jnp.int32)
    placed = windows * capacity + rank
    placed_ref[...] = placed.astype(F32)
    placing = (placed == iota((SLOTS, voxels), 0)).astype(F32).astype(BF16)
    loads[1].wait()
    row = iota((EXTRA, voxels), 0)
    extra = jnp.where(row == 3, 1.0, 0.0).astype(F32)
    for c in range(3):
        extra = jnp.where(row == c, coords_ref[c : c + 1, :].astype(F32), extra)
    out_ref[:, width:] = lax.dot_general(
        placing, extra.astype(BF16), NT, preferred_element_type=F32
    ).astype(BF16)
    loads[2].wait()
    out_ref[:, :width] = dot(placing, x_ref[...]).astype(BF16)


def column_norm(rows, gain, head_size):
    blocks = []
    for start in range(0, rows.shape[0], head_size):
        block = rows[start : start + head_size]
        mean = jnp.sum(block * block, axis=0, keepdims=True) * (1.0 / head_size)
        blocks.append(block * lax.rsqrt(mean + 1e-06) * gain[start : start + head_size])
    return jnp.concatenate(blocks, axis=0).astype(BF16)


def project_keys(normed, w_key, gain, head_size):
    key = lax.dot_general(w_key, normed, NT, preferred_element_type=F32)
    return column_norm(key, gain, head_size)


def project_values(normed, w_value):
    return lax.dot_general(normed, w_value, NT, preferred_element_type=F32).astype(BF16)


def attend_heads(query, key, value, before_head, att_ref, bias, tile, head_size):
    queries, group = att_ref.shape
    lane_head = iota((queries, tile), 1) // head_size
    per_tile = tile // head_size
    heads = group // head_size

    def score(i):
        one = jnp.where(lane_head == i % per_tile, query(i // per_tile), 0.0).astype(BF16)
        return dot(one, key(i // per_tile))

    scores = score(0)
    mixed = jnp.zeros((queries, tile), F32)
    step = min(32, queries)
    for i in range(heads):
        before_head(i)
        following = score(i + 1) if i + 1 < heads else None
        pieces = []
        for r in range(0, queries, step):
            piece = scores[r : r + step] + bias
            weights = jnp.exp(piece - jnp.max(piece, axis=1, keepdims=True))
            total = jnp.sum(weights, axis=1, keepdims=True)
            pieces.append((weights * (1.0 / total)).astype(BF16))
        attend = jnp.concatenate(pieces, axis=0)
        mixed = jnp.where(lane_head == i % per_tile, dot(attend, value(i // per_tile)), mixed)
        if (i + 1) % per_tile == 0:
            start = i // per_tile * tile
            att_ref[:, start : start + tile] = mixed.astype(BF16)
        scores = following


def project_query(normed_q, w_query, gain, head_size):
    query = lax.dot_general(w_query, normed_q, NT, preferred_element_type=F32)
    query = column_norm(query, gain, head_size)
    return (query.astype(F32) * (1.0 / head_size**0.5)).T


def branch_scales(guidance_ref):
    g0, g1 = guidance_ref[0], guidance_ref[1]
    return 1.0 - g0, g0 - g1, g1


def pick_scale(b, scales):
    return jnp.where(b == 0, scales[0], jnp.where(b == 1, scales[1], scales[2]))


def copies(pairs, sems):
    return [
        pltpu.make_async_copy(source, target, sems.at[n])
        for n, (source, target) in enumerate(pairs)
    ]


def gain_columns(gain_rows_ref):
    rows = gain_rows_ref[...]
    return jnp.concatenate([rows, rows, rows, rows], axis=0).T


def first_kernel(
    senders,
    head_size,
    guidance_ref,
    modulation_ref,
    gain_rows_ref,
    rows_ref,
    table_hbm,
    w_hbm,
    w_out_hbm,
    later_q_ref,
    keys_ref,
    values_ref,
    residual_ref,
    bias_ref,
    sent_ref,
    table_ref,
    w_ref,
    gain_ref,
    w_out_ref,
    normed_ref,
    next_q_ref,
    hidden_ref,
    att_ref,
    sum_ref,
    in_sems,
):
    loads = copies(
        (
            (table_hbm, table_ref),
            (w_hbm, w_ref),
            (w_out_hbm, w_out_ref),
        ),
        in_sems,
    )
    for load in loads:
        load.start()
    branches, slots, width = normed_ref.shape
    queries, heads = next_q_ref.shape[1], later_q_ref.shape[0] + 1
    group = att_ref.shape[1]
    capacity = slots // senders
    share = queries // senders
    me = lax.axis_index("head")
    scales = branch_scales(guidance_ref)
    total = (scales[0] + scales[1]) + scales[2]

    gain_ref[...] = gain_columns(gain_rows_ref)
    extra = rows_ref[:, width:]
    pick = ((iota((8, EXTRA), 1) == 3)).astype(F32).astype(BF16)
    live = lax.dot_general(pick, extra, NT, preferred_element_type=F32)
    bias_ref[...] = jnp.where(live > 0.5, 0.0, -1e30)

    spots = extra.astype(F32)
    lane = iota((slots, 3 * GRID), 1)
    wanted = jnp.where(
        lane < GRID,
        spots[:, 0:1],
        jnp.where(lane < 2 * GRID, spots[:, 1:2], spots[:, 2:3]),
    )
    chosen = (wanted == (lane % GRID).astype(F32)).astype(F32).astype(BF16)
    chosen = jnp.concatenate([chosen, chosen, chosen], axis=1)
    loads[0].wait()
    chunk = min(128, slots)
    shifts = [modulation_ref[b, 0:1, :] for b in range(branches)]
    stretches = [1.0 + modulation_ref[b, 1:2, :] for b in range(branches)]
    for start in range(0, slots, chunk):
        rows = slice(start, start + chunk)
        hidden = dot(chosen[rows], table_ref[...]) + rows_ref[rows, :width].astype(F32)
        hidden_ref[rows, :] = hidden
        centred = hidden - jnp.mean(hidden, axis=1, keepdims=True)
        spread = jnp.mean(centred * centred, axis=1, keepdims=True)
        normal = centred * lax.rsqrt(spread + 1e-06)
        for b in range(branches):
            normed_ref[b, rows, :] = (normal * stretches[b] + shifts[b]).astype(BF16)

    for d in range(heads):
        normed_q_ref = next_q_ref if d == 0 else later_q_ref.at[d - 1]
        first = lax.rem(me + d + 1, heads) * share
        if share % 16 == 0:
            for s in range(senders):
                source = pl.ds(pl.multiple_of(s * capacity + first, 16), share)
                target = slice(s * share, (s + 1) * share)
                if d == heads - 1:
                    residual_ref[target, :] = hidden_ref[source, :] * total
                for b in range(branches):
                    normed_q_ref[b, target, :] = normed_ref[b, source, :]
        else:
            row = iota((queries, slots), 0)
            wanted_slot = (row // share) * capacity + first + row % share
            chooser = (wanted_slot == iota((queries, slots), 1)).astype(F32)
            if d == heads - 1:
                picked = jnp.dot(
                    chooser,
                    hidden_ref[...],
                    preferred_element_type=F32,
                    precision=lax.Precision.HIGHEST,
                )
                residual_ref[...] = picked * total
            for b in range(branches):
                normed_q_ref[b] = dot(chooser.astype(BF16), normed_ref[b]).astype(BF16)

    bias = bias_ref[0:1, :]
    tile = min(256, group)
    loads[1].wait()

    for b in range(branches):
        made = {}

        def make(kind, t):
            features = slice(t * tile, (t + 1) * tile)
            if kind == "query":
                array = project_query(
                    next_q_ref[b], w_ref[0, features, :], gain_ref[features, 0:1], head_size
                )
            elif kind == "key":
                array = project_keys(
                    normed_ref[b], w_ref[1, features, :], gain_ref[features, 1:2], head_size
                )
                keys_ref[b, features, :] = array
            else:
                array = project_values(normed_ref[b], w_ref[2, features, :])
                values_ref[b, :, features] = array
            made[kind, t] = array

        def get(kind, t):
            if (kind, t) not in made:
                make(kind, t)
            return made[kind, t]

        for kind in ("query", "key", "value"):
            make(kind, 0)
        waiting = [(kind, t) for t in range(1, group // tile) for kind in ("query", "key", "value")]

        def before_head(i):
            if i < len(waiting):
                get(*waiting[i])

        attend_heads(
            functools.partial(get, "query"),
            functools.partial(get, "key"),
            functools.partial(get, "value"),
            before_head,
            att_ref,
            bias,
            tile,
            head_size,
        )
        if b == 0:
            loads[2].wait()
        term = dot(att_ref[...], w_out_ref[...]) * (scales[b] * modulation_ref[b, 2:3, :])
        if b == 0:
            sum_ref[...] = term
        elif b < branches - 1:
            sum_ref[...] += term
        else:
            sent_ref[...] = (sum_ref[...] + term) * SENT_SCALE


def query_kernel(
    head_size,
    distance,
    last,
    guidance_ref,
    modulation_ref,
    gain_rows_ref,
    normed_q_ref,
    keys_ref,
    values_ref,
    bias_ref,
    w_ref,
    w_out_ref,
    start_ref,
    sum_ref,
    gain_ref,
    att_ref,
):
    branches, _, slots = keys_ref.shape
    group = att_ref.shape[1]
    scales = branch_scales(guidance_ref)
    tile = min(256, group)
    gain_ref[...] = gain_columns(gain_rows_ref)
    bias = bias_ref[0:1, :]

    for b in range(branches):
        made = {}

        def query(t):
            if t not in made:
                features = slice(t * tile, (t + 1) * tile)
                made[t] = project_query(
                    normed_q_ref[distance - 1, b],
                    w_ref[0, features, :],
                    gain_ref[features, 0:1], head_size
                )
            return made[t]

        attend_heads(
            query,
            lambda t: keys_ref[b, t * tile : (t + 1) * tile, :],
            lambda t: values_ref[b, :, t * tile : (t + 1) * tile],
            lambda i: query(min(i, group // tile - 1)),
            att_ref,
            bias,
            tile,
            head_size,
        )
        term = dot(att_ref[...], w_out_ref[...]) * (scales[b] * modulation_ref[b, 2:3, :])
        if b == 0:
            sum_ref[...] = start_ref[...] + term if last else term
        else:
            sum_ref[...] += term
    if not last:
        sum_ref[...] = sum_ref[...] * SENT_SCALE


def return_kernel(placed_ref, rows_ref, out_ref):
    voxels = placed_ref.shape[1]
    column = jnp.broadcast_to(placed_ref[...], (128, voxels)).T
    column = column.astype(jnp.int32)
    lane = iota((voxels, 128), 1)
    placing = jnp.concatenate(
        [(column == lane + start).astype(F32).astype(BF16) for start in range(0, SLOTS, 128)], axis=1
    )
    out_ref[...] = dot(placing, rows_ref[...]).astype(BF16)


def on_device(x_latent, windows, coords, modulation, w_qkv, w_out, qk_gain, guidance):
    voxels, width = x_latent.shape
    group = w_qkv.shape[2]
    head_size = width // HEADS
    branches = modulation.shape[0]
    senders = lax.axis_size(("cfg", "vox"))
    heads = lax.axis_size("head")
    capacity = SLOTS // senders
    queries = SLOTS // heads
    share = capacity // heads

    vmem, dma = pltpu.VMEM, pltpu.SemaphoreType.DMA
    outgoing, placed = pl.pallas_call(
        functools.partial(place_kernel, senders, capacity),
        out_shape=(
            jax.ShapeDtypeStruct((SLOTS, width + EXTRA), BF16),
            jax.ShapeDtypeStruct((1, voxels), F32),
        ),
        in_specs=[HBM] * 3,
        out_specs=(VMEM, VMEM),
        scratch_shapes=[
            vmem((voxels, width), BF16),
            vmem(windows.shape, jnp.int32),
            vmem(coords.shape, jnp.int32),
            dma((3,)),
        ],
        compiler_params=params(64),
        name="place",
    )(windows, coords, x_latent)
    arrived = lax.all_to_all(
        outgoing.reshape(senders, capacity, width + EXTRA),
        ("cfg", "vox"),
        split_axis=0,
        concat_axis=0,
        tiled=True,
    ).reshape(SLOTS, width + EXTRA)

    table = position_parts(width)
    flat = jnp.transpose(w_qkv, (1, 2, 0))
    shapes = dict(
        normed_q=((heads - 1, branches, queries, width), BF16),
        keys=((branches, group, SLOTS), BF16),
        values=((branches, SLOTS, group), BF16),
        residual=((queries, width), F32),
        bias=((8, SLOTS), F32),
        sent=((queries, width), F32),
    )
    made = pl.pallas_call(
        functools.partial(first_kernel, senders, head_size),
        out_shape=tuple(jax.ShapeDtypeStruct(*shape) for shape in shapes.values()),
        in_specs=[SMEM, VMEM, VMEM, VMEM] + [HBM] * 3,
        out_specs=(VMEM,) * 6,
        scratch_shapes=[
            vmem(table.shape, BF16),
            vmem((3, group, width), BF16),
            vmem((group, 8), F32),
            vmem((group, width), BF16),
            vmem((branches, SLOTS, width), BF16),
            vmem((branches, queries, width), BF16),
            vmem((SLOTS, width), F32),
            vmem((queries, group), BF16),
            vmem((queries, width), F32),
            dma((3,)),
        ],
        compiler_params=params(43),
        name="first_queries",
    )(guidance, modulation, qk_gain, arrived, table, flat, w_out)
    normed_q, keys, values, residual, bias, partial = made

    def attend(distance, last):
        return pl.pallas_call(
            functools.partial(query_kernel, head_size, distance, last),
            out_shape=jax.ShapeDtypeStruct((queries, width), F32),
            in_specs=[SMEM] + [VMEM] * 9,
            out_specs=VMEM,
            scratch_shapes=[vmem((group, 8), F32), vmem((queries, group), BF16)],
            compiler_params=params(28),
            name="more_queries",
        )(guidance, modulation, qk_gain, normed_q, keys, values, bias, flat, w_out, residual)

    terms = []
    for distance in range(1, heads):
        turn = [(h, (h + distance) % heads) for h in range(heads)]
        terms.append(lax.ppermute(partial.astype(jnp.float16), "head", turn))
        partial = attend(distance, distance == heads - 1)
    for term in terms:
        partial = partial + term.astype(F32) * (1.0 / SENT_SCALE)
    columns = width // heads
    rows = jnp.concatenate(
        [
            partial[:, h * columns : (h + 1) * columns].reshape(senders, 1, share, columns)
            for h in range(heads)
        ],
        axis=1,
    ).astype(BF16)
    back = lax.all_to_all(
        rows.reshape(senders * heads, share, width // heads),
        ("cfg", "vox", "head"),
        split_axis=0,
        concat_axis=0,
        tiled=True,
    )
    return pl.pallas_call(
        return_kernel,
        out_shape=jax.ShapeDtypeStruct((voxels, width // heads), BF16),
        in_specs=[VMEM, VMEM],
        out_specs=VMEM,
        compiler_params=params(16),
        name="return_rows",
    )(placed, back.reshape(SLOTS, width // heads))


def solution(mesh):
    placed = (
        P(("cfg", "vox"), None),
        P(("cfg", "vox")),
        P(None, ("cfg", "vox")),
        P(),
        P(None, None, "head"),
        P("head", None),
        P(None, "head"),
        P(),
    )
    return jax.shard_map(
        on_device, mesh=mesh, in_specs=placed, out_specs=P(("cfg", "vox"), "head"), check_vma=False
    )
```
